32 devices in a mesh: dp: 8 (over z, x), tensor: 4 (over y, core).
Axes of the slice: x: 2, y: 2, z: 4, core: 2. Of those that a mesh axis runs over, the one named last changes fastest.
Arguments:
- block_input: bfloat16 [8192, 2048], P('dp'), may hold values from -6 to 6
- out_grad: bfloat16 [8192, 2048], P('dp'), may hold values from -6 to 6
- segments: int32 [8192], P('dp'), may hold values from 0 to 3, as said below
- positions: int32 [8192], P('dp'), may hold values from 0 to 1535, as said below
- w_query: float32 [2048, 2048], P('dp', 'tensor'), may hold values from -0.1875 to 0.1875
- key_weight_master: float32 [2048, 1024], P('dp', 'tensor'), may hold values from -0.1875 to 0.1875
- value_weight_master: float32 [2048, 1024], P('dp', 'tensor'), may hold values from -0.125 to 0.125
- w_output: float32 [2048, 2048], P('tensor', 'dp'), may hold values from -0.375 to 0.375
- w_gate: float32 [2048, 8192], P('dp', 'tensor'), may hold values from -0.125 to 0.125
- w_up: float32 [2048, 8192], P('dp', 'tensor'), may hold values from -0.125 to 0.125
- w_down: float32 [8192, 2048], P('tensor', 'dp'), may hold values from -0.0625 to 0.0625
- gains: float32 [2, 2048], P(None, 'dp'), may hold values from 0.5 to 1.5
- m_query: float32 [2048, 2048], P('dp', 'tensor'), may hold values from -1024 to 1024
- first_moment_key: float32 [2048, 1024], P('dp', 'tensor'), may hold values from -1024 to 1024
- first_moment_value: float32 [2048, 1024], P('dp', 'tensor'), may hold values from -1024 to 1024
- m_output: float32 [2048, 2048], P('tensor', 'dp'), may hold values from -256 to 256
- m_gate: float32 [2048, 8192], P('dp', 'tensor'), may hold values from -160 to 160
- m_up: float32 [2048, 8192], P('dp', 'tensor'), may hold values from -160 to 160
- m_down: float32 [8192, 2048], P('tensor', 'dp'), may hold values from -320 to 320
- m_gains: float32 [2, 2048], P(None, 'dp'), may hold values from -1024 to 1024
- v_query: float32 [2048, 2048], P('dp', 'tensor'), may hold values from 32768 to 131072
- second_moment_key: float32 [2048, 1024], P('dp', 'tensor'), may hold values from 32768 to 131072
- second_moment_value: float32 [2048, 1024], P('dp', 'tensor'), may hold values from 32768 to 131072
- v_output: float32 [2048, 2048], P('tensor', 'dp'), may hold values from 2048 to 8192
- v_gate: float32 [2048, 8192], P('dp', 'tensor'), may hold values from 744 to 2730
- v_up: float32 [2048, 8192], P('dp', 'tensor'), may hold values from 744 to 2730
- v_down: float32 [8192, 2048], P('tensor', 'dp'), may hold values from 2730 to 10922
- v_gains: float32 [2, 2048], P(None, 'dp'), may hold values from 32768 to 131072
Outputs:
- block_output: bfloat16 [8192, 2048], P('dp')
- input_gradient: float32 [8192, 2048], P('dp')
- new_query: float32 [2048, 2048], P('dp', 'tensor')
- new_key: float32 [2048, 1024], P('dp', 'tensor')
- new_value: float32 [2048, 1024], P('dp', 'tensor')
- new_output: float32 [2048, 2048], P('tensor', 'dp')
- new_gate: float32 [2048, 8192], P('dp', 'tensor')
- new_up: float32 [2048, 8192], P('dp', 'tensor')
- new_down: float32 [8192, 2048], P('tensor', 'dp')
- new_gains: float32 [2, 2048], P(None, 'dp')
- new_m_query: float32 [2048, 2048], P('dp', 'tensor')
- new_m_key: float32 [2048, 1024], P('dp', 'tensor')
- new_m_value: float32 [2048, 1024], P('dp', 'tensor')
- new_m_output: float32 [2048, 2048], P('tensor', 'dp')
- new_m_gate: float32 [2048, 8192], P('dp', 'tensor')
- new_m_up: float32 [2048, 8192], P('dp', 'tensor')
- new_m_down: float32 [8192, 2048], P('tensor', 'dp')
- new_m_gains: float32 [2, 2048], P(None, 'dp')
- new_v_query: float32 [2048, 2048], P('dp', 'tensor')
- new_v_key: float32 [2048, 1024], P('dp', 'tensor')
- new_v_value: float32 [2048, 1024], P('dp', 'tensor')
- new_v_output: float32 [2048, 2048], P('tensor', 'dp')
- new_v_gate: float32 [2048, 8192], P('dp', 'tensor')
- new_v_up: float32 [2048, 8192], P('dp', 'tensor')
- new_v_down: float32 [8192, 2048], P('tensor', 'dp')
- new_v_gains: float32 [2, 2048], P(None, 'dp')
The draws below stay inside these ranges and needn't reach their ends.
Inputs may be any that keep to these rules, and one draw needn't show every extreme that they name: `segments`: tokens 2048 * s to 2048 * s + 2047 form sequence s; within each, segment numbers start at 0, never fall, and rise by one at each document bound; each sequence holds exactly 4 documents, one of which (drawn from the seed) has exactly 1536 tokens and the others 2048 // 4 tokens together. `positions`: 0 at each document's first token and rising by one along the document.
All inputs are finite; a program needn't handle non-finite values.
Results may differ from the reference program's by a relative error of at most 0.015.
The reference program's roundings to bfloat16 on the way count: a program that leaves them out, or rounds other values in their place, can miss the bound.
Values may be sent and summed in bfloat16 or wider, within the bound.
A program may use at most 256 MiB of HBM per device.

```python
import math
from functools import partial
import jax
import jax.numpy as jnp
from jax import lax

MODEL_WIDTH = 2048
QUERY_HEADS = 16
KEY_VALUE_HEADS = 8
HEAD_SIZE = 128
FF = 8192
SEQ = 2048
WINDOW = 1024
DOCS = 4
STEP = 5
TOKENS_PER_SHARD = 1024
TOKENS = 8192
N_DP = 8


def one_layout(key):
    longest = 3 * SEQ // 4
    rest = SEQ - longest
    pick_key, cut_key = jax.random.split(key)
    chosen = jax.random.randint(pick_key, (), 0, DOCS).astype(jnp.int32)
    cuts = jnp.sort(jax.random.permutation(cut_key, rest - 1)[:DOCS - 2].astype(jnp.int32) + 1)
    edges = jnp.concatenate([jnp.zeros((1,), jnp.int32), cuts, jnp.full((1,), rest, jnp.int32)])
    small = edges[1:] - edges[:-1]
    index = jnp.arange(DOCS, dtype=jnp.int32)
    before = small[jnp.clip(index, 0, DOCS - 2)]
    after = small[jnp.clip(index - 1, 0, DOCS - 2)]
    lengths = jnp.where(index < chosen, before, jnp.where(index == chosen, longest, after)).astype(jnp.int32)
    starts = (jnp.cumsum(lengths) - lengths).astype(jnp.int32)
    places = jnp.arange(SEQ, dtype=jnp.int32)
    reached = starts[None, 1:] <= places[:, None]
    segment_ids = jnp.sum(reached.astype(jnp.int32), -1).astype(jnp.int32)
    begin = jnp.sum(jnp.where(index[None, :] == segment_ids[:, None], starts[None, :], 0), -1).astype(jnp.int32)
    return (segment_ids, places - begin)


def document_layout(key):
    count = TOKENS // SEQ
    key_matrix = jax.random.split(key, count)
    segment_ids, position_ids = jax.vmap(one_layout)(key_matrix)
    return (segment_ids.reshape(TOKENS), position_ids.reshape(TOKENS))


def draw_segments(key, part):
    layout = document_layout(key)
    return layout[0]


def draw_positions(key, part):
    layout = document_layout(key)
    return layout[1]


def steps_of(stream_key, dims, shards, smallest, top_value):
    factor_of = 1.0
    for axis_at, shards_of in shards:
        steps = jax.random.uniform(jax.random.fold_in(jax.random.fold_in(stream_key, 6), axis_at), (shards_of,), jnp.float32, smallest / len(shards), top_value / len(shards))
        factor_of = factor_of * jnp.repeat(jnp.exp(steps), dims[axis_at] // shards_of).reshape((-1,) + (1,) * (len(dims) - 1 - axis_at))
    return factor_of


def centred(key, dims, deviation, limit, cuts=(), held_as=jnp.bfloat16):
    array = deviation * jax.random.normal(key, dims, jnp.float32)
    if cuts:
        array = array * steps_of(key, dims, cuts, -0.22, 0.18)
    return jnp.clip(array, -limit, limit).astype(held_as)


def setup_inputs(seed: int = 0) -> dict:
    arg_keys = jax.random.split(jax.random.key(seed), 29)
    return {
        "block_input": centred(arg_keys[0], (TOKENS, MODEL_WIDTH), 1.0, 6.0, ((0, 8),)),
        "out_grad": centred(arg_keys[1], (TOKENS, MODEL_WIDTH), 1.0, 6.0, ((0, 8),)),
        "segments": draw_segments(jax.random.fold_in(arg_keys[28], 71), 0),
        "positions": draw_positions(jax.random.fold_in(arg_keys[28], 71), 0),
        "w_query": centred(arg_keys[4], (MODEL_WIDTH, QUERY_HEADS * HEAD_SIZE), (MODEL_WIDTH // 2) ** -0.5, 0.1875, ((0, 8), (1, 4)), jnp.float32),
        "key_weight_master": centred(arg_keys[5], (MODEL_WIDTH, KEY_VALUE_HEADS * HEAD_SIZE), (MODEL_WIDTH // 2) ** -0.5, 0.1875, ((0, 8), (1, 4)), jnp.float32),
        "value_weight_master": centred(arg_keys[6], (MODEL_WIDTH, KEY_VALUE_HEADS * HEAD_SIZE), MODEL_WIDTH ** -0.5, 0.125, ((0, 8), (1, 4)), jnp.float32),
        "w_output": centred(arg_keys[7], (QUERY_HEADS * HEAD_SIZE, MODEL_WIDTH), (QUERY_HEADS * HEAD_SIZE // 8) ** -0.5, 0.375, ((0, 4), (1, 8)), jnp.float32),
        "w_gate": centred(arg_keys[8], (MODEL_WIDTH, FF), MODEL_WIDTH ** -0.5, 0.125, ((0, 8), (1, 4)), jnp.float32),
        "w_up": centred(arg_keys[9], (MODEL_WIDTH, FF), MODEL_WIDTH ** -0.5, 0.125, ((0, 8), (1, 4)), jnp.float32),
        "w_down": centred(arg_keys[10], (FF, MODEL_WIDTH), FF ** -0.5, 0.0625, ((0, 4), (1, 8)), jnp.float32),
        "gains": jnp.clip(1.0 + 0.1 * jax.random.normal(arg_keys[11], (2, MODEL_WIDTH), jnp.float32), 0.5, 1.5),
        "m_query": centred(arg_keys[12], (MODEL_WIDTH, QUERY_HEADS * HEAD_SIZE), (2 * (TOKENS_PER_SHARD * N_DP) ** 0.5), 1024.0, ((0, 8), (1, 4)), jnp.float32),
        "first_moment_key": centred(arg_keys[13], (MODEL_WIDTH, KEY_VALUE_HEADS * HEAD_SIZE), (2 * (TOKENS_PER_SHARD * N_DP) ** 0.5), 1024.0, ((0, 8), (1, 4)), jnp.float32),
        "first_moment_value": centred(arg_keys[14], (MODEL_WIDTH, KEY_VALUE_HEADS * HEAD_SIZE), (2 * (TOKENS_PER_SHARD * N_DP) ** 0.5), 1024.0, ((0, 8), (1, 4)), jnp.float32),
        "m_output": centred(arg_keys[15], (QUERY_HEADS * HEAD_SIZE, MODEL_WIDTH), (0.5 * (TOKENS_PER_SHARD * N_DP) ** 0.5), 256.0, ((0, 4), (1, 8)), jnp.float32),
        "m_gate": centred(arg_keys[16], (MODEL_WIDTH, FF), (0.3 * (TOKENS_PER_SHARD * N_DP) ** 0.5), 160.0, ((0, 8), (1, 4)), jnp.float32),
        "m_up": centred(arg_keys[17], (MODEL_WIDTH, FF), (0.3 * (TOKENS_PER_SHARD * N_DP) ** 0.5), 160.0, ((0, 8), (1, 4)), jnp.float32),
        "m_down": centred(arg_keys[18], (FF, MODEL_WIDTH), (0.6 * (TOKENS_PER_SHARD * N_DP) ** 0.5), 320.0, ((0, 4), (1, 8)), jnp.float32),
        "m_gains": centred(arg_keys[19], (2, MODEL_WIDTH), (2 * (TOKENS_PER_SHARD * N_DP) ** 0.5), 1024.0, ((1, 8),), jnp.float32),
        "v_query": jnp.clip(jnp.exp(math.log(131072.0) - 1.3862944 * jax.random.uniform(arg_keys[20], (MODEL_WIDTH, QUERY_HEADS * HEAD_SIZE), jnp.float32) ** steps_of(arg_keys[20], (MODEL_WIDTH, QUERY_HEADS * HEAD_SIZE), ((0, 8), (1, 4)), -0.2, 0.2)), 32768.0, 131072.0),
        "second_moment_key": jnp.clip(jnp.exp(math.log(131072.0) - 1.3862944 * jax.random.uniform(arg_keys[21], (MODEL_WIDTH, KEY_VALUE_HEADS * HEAD_SIZE), jnp.float32) ** steps_of(arg_keys[21], (MODEL_WIDTH, KEY_VALUE_HEADS * HEAD_SIZE), ((0, 8), (1, 4)), -0.2, 0.2)), 32768.0, 131072.0),
        "second_moment_value": jnp.clip(jnp.exp(math.log(131072.0) - 1.3862944 * jax.random.uniform(arg_keys[22], (MODEL_WIDTH, KEY_VALUE_HEADS * HEAD_SIZE), jnp.float32) ** steps_of(arg_keys[22], (MODEL_WIDTH, KEY_VALUE_HEADS * HEAD_SIZE), ((0, 8), (1, 4)), -0.2, 0.2)), 32768.0, 131072.0),
        "v_output": jnp.clip(jnp.exp(math.log(8192.0) - 1.3862944 * jax.random.uniform(arg_keys[23], (QUERY_HEADS * HEAD_SIZE, MODEL_WIDTH), jnp.float32) ** steps_of(arg_keys[23], (QUERY_HEADS * HEAD_SIZE, MODEL_WIDTH), ((0, 4), (1, 8)), -0.2, 0.2)), 2048.0, 8192.0),
        "v_gate": jnp.clip(jnp.exp(math.log(2730.0) - 1.30001585 * jax.random.uniform(arg_keys[24], (MODEL_WIDTH, FF), jnp.float32) ** steps_of(arg_keys[24], (MODEL_WIDTH, FF), ((0, 8), (1, 4)), -0.2, 0.2)), 744.0, 2730.0),
        "v_up": jnp.clip(jnp.exp(math.log(2730.0) - 1.30001585 * jax.random.uniform(arg_keys[25], (MODEL_WIDTH, FF), jnp.float32) ** steps_of(arg_keys[25], (MODEL_WIDTH, FF), ((0, 8), (1, 4)), -0.2, 0.2)), 744.0, 2730.0),
        "v_down": jnp.clip(jnp.exp(math.log(10922.0) - 1.3864775 * jax.random.uniform(arg_keys[26], (FF, MODEL_WIDTH), jnp.float32) ** steps_of(arg_keys[26], (FF, MODEL_WIDTH), ((0, 4), (1, 8)), -0.2, 0.2)), 2730.0, 10922.0),
        "v_gains": jnp.clip(jnp.exp(math.log(131072.0) - 1.3862944 * jax.random.uniform(arg_keys[27], (2, MODEL_WIDTH), jnp.float32) ** steps_of(arg_keys[27], (2, MODEL_WIDTH), ((1, 8),), -0.2, 0.2)), 32768.0, 131072.0),
    }


EPS = 1e-06
THETA = 1000000.0
BETA_ONE = 0.5
BETA_TWO = 0.5
RATE_MATRIX = 0.02
RATE_GAIN = 0.3
DECAY = 0.1
ADAM_EPS = 1e-08
NEGATIVE = -1e+30

@jax.custom_vjp
def lower_precision(v):
    return lax.optimization_barrier(v.astype(jnp.bfloat16)).astype(jnp.float32)

@jax.custom_vjp
def lower_precision_backward(v):
    return v

def low_keep(v):
    return (lower_precision(v), None)

def low_pass(kept, grad):
    return (grad,)

def back_keep(v):
    return (v, None)

def back_low(kept, grad):
    return (lower_precision(grad),)
lower_precision.defvjp(low_keep, low_pass)
lower_precision_backward.defvjp(back_keep, back_low)

def matrix_product(left, right):
    return jnp.dot(left, right, precision=lax.Precision.HIGHEST, preferred_element_type=jnp.float32)

def norm_rows(value_matrix):
    factor = lax.rsqrt(lax.optimization_barrier(jnp.mean(value_matrix * value_matrix, -1, keepdims=True)) + EPS)
    return value_matrix * factor

def rotary_tables(positions):
    half = HEAD_SIZE // 2
    frequency = THETA ** (-2.0 * jnp.arange(half, dtype=jnp.float32) / HEAD_SIZE)
    angles = positions.astype(jnp.float32)[:, None] * frequency[None, :]
    cosine_table = jnp.cos(angles)
    sine_table = jnp.sin(angles)
    return (jnp.concatenate([cosine_table, cosine_table], -1), jnp.concatenate([sine_table, sine_table], -1))

def apply_rotation(heads, cosine_table, sine_table):
    half = heads.shape[-1] // 2
    turned = jnp.concatenate([-heads[..., half:], heads[..., :half]], -1)
    return heads * cosine_table[:, None, :] + turned * sine_table[:, None, :]

def attend_rows(query_matrix, key_matrix, value_matrix, segment_rows, position_rows, start, block):
    rows = lax.dynamic_slice_in_dim(query_matrix, start, block, 0)
    row_segments = lax.dynamic_slice_in_dim(segment_rows, start, block, 0)
    row_positions = lax.dynamic_slice_in_dim(position_rows, start, block, 0)
    scores = jnp.einsum('qhgd,khd->hgqk', rows, key_matrix, precision=lax.Precision.HIGHEST) / math.sqrt(HEAD_SIZE)
    scores = lower_precision_backward(scores)
    distance = row_positions[:, None] - position_rows[None, :]
    allowed = (row_segments[:, None] == segment_rows[None, :]) & (distance >= 0) & (distance < WINDOW)
    scores = jnp.where(allowed[None, None], scores, NEGATIVE)
    top = lax.optimization_barrier(jnp.max(scores, -1, keepdims=True))
    expo = jnp.exp(scores - top)
    probs = expo / lax.optimization_barrier(jnp.sum(expo, -1, keepdims=True))
    return jnp.einsum('hgqk,khd->qhgd', lower_precision(probs), value_matrix, precision=lax.Precision.HIGHEST)

def layer(inputs, weights, segment_rows, position_rows):
    w_query, key_weight_master, value_weight_master, w_output, w_gate, w_up, w_down, gains = weights
    document_length = inputs.shape[0]
    head_group = QUERY_HEADS // KEY_VALUE_HEADS
    low_gains = lower_precision(gains)
    normed_input = lower_precision(norm_rows(inputs) * low_gains[0])
    query_unrotated = lower_precision_backward(matrix_product(normed_input, lower_precision(w_query)))
    key_unrotated = lower_precision_backward(matrix_product(normed_input, lower_precision(key_weight_master)))
    value_matrix = lower_precision(lower_precision_backward(matrix_product(normed_input, lower_precision(value_weight_master)))).reshape(document_length, KEY_VALUE_HEADS, HEAD_SIZE)
    cosine_table, sine_table = rotary_tables(position_rows)
    query_matrix = lower_precision(apply_rotation(query_unrotated.reshape(document_length, QUERY_HEADS, HEAD_SIZE), cosine_table, sine_table)).reshape(document_length, KEY_VALUE_HEADS, head_group, HEAD_SIZE)
    key_matrix = lower_precision(apply_rotation(key_unrotated.reshape(document_length, KEY_VALUE_HEADS, HEAD_SIZE), cosine_table, sine_table))
    block = min(512, document_length)
    blockwise = jax.checkpoint(partial(attend_rows, block=block))

    def one_block(start):
        return blockwise(query_matrix, key_matrix, value_matrix, segment_rows, position_rows, start)
    starts = jnp.arange(document_length // block, dtype=jnp.int32) * block
    attended = lax.map(one_block, starts).reshape(document_length, QUERY_HEADS * HEAD_SIZE)
    attended = lower_precision(lower_precision_backward(attended))
    mixed = lower_precision_backward(matrix_product(attended, lower_precision(w_output)))
    residual = inputs + mixed
    second_in = lower_precision(norm_rows(residual) * low_gains[1])
    gate = lower_precision_backward(matrix_product(second_in, lower_precision(w_gate)))
    up = lower_precision_backward(matrix_product(second_in, lower_precision(w_up)))
    hidden = lower_precision(gate * jax.nn.sigmoid(gate) * up)
    return residual + matrix_product(hidden, lower_precision(w_down))

def adamw(weight, gradient, first, second, rate, decay):
    first_new = BETA_ONE * first + (1.0 - BETA_ONE) * gradient
    second_new = BETA_TWO * second + (1.0 - BETA_TWO) * gradient * gradient
    bias_first = 1.0 - BETA_ONE ** STEP
    bias_second = 1.0 - BETA_TWO ** STEP
    moved = first_new / bias_first / (jnp.sqrt(second_new / bias_second) + ADAM_EPS)
    return (weight - rate * (moved + decay * weight), first_new, second_new)

def reference(block_input, out_grad, segments, positions, w_query, key_weight_master, value_weight_master, w_output, w_gate, w_up, w_down, gains, m_query, first_moment_key, first_moment_value, m_output, m_gate, m_up, m_down, m_gains, v_query, second_moment_key, second_moment_value, v_output, v_gate, v_up, v_down, v_gains):
    count = block_input.shape[0] // SEQ
    weights = (w_query, key_weight_master, value_weight_master, w_output, w_gate, w_up, w_down, gains)

    def one_sequence(totals, item):
        rows, cotangent, segment_rows, position_rows = item

        def forward(inputs, params):
            return layer(inputs, params, segment_rows, position_rows)
        result, pullback = jax.vjp(forward, rows.astype(jnp.float32), weights)
        input_part, weight_parts = pullback(cotangent.astype(jnp.float32))
        totals = tuple((total + part for total, part in zip(totals, weight_parts)))
        return (totals, (result.astype(jnp.bfloat16), input_part))
    zeros = tuple((jnp.zeros(weight.shape, jnp.float32) for weight in weights))
    items = (block_input.reshape(count, SEQ, MODEL_WIDTH), out_grad.reshape(count, SEQ, MODEL_WIDTH), segments.reshape(count, SEQ), positions.reshape(count, SEQ))
    totals, (outputs, input_parts) = lax.scan(one_sequence, zeros, items)
    block_output = outputs.reshape(block_input.shape)
    input_gradient = input_parts.reshape(block_input.shape)
    firsts = (m_query, first_moment_key, first_moment_value, m_output, m_gate, m_up, m_down, m_gains)
    seconds = (v_query, second_moment_key, second_moment_value, v_output, v_gate, v_up, v_down, v_gains)
    rates = (RATE_MATRIX,) * 7 + (RATE_GAIN,)
    decays = (DECAY,) * 7 + (0.0,)
    fresh = [adamw(weight, gradient, first, second, rate, decay) for weight, gradient, first, second, rate, decay in zip(weights, totals, firsts, seconds, rates, decays)]
    return (block_output, input_gradient, fresh[0][0], fresh[1][0], fresh[2][0], fresh[3][0], fresh[4][0], fresh[5][0], fresh[6][0], fresh[7][0], fresh[0][1], fresh[1][1], fresh[2][1], fresh[3][1], fresh[4][1], fresh[5][1], fresh[6][1], fresh[7][1], fresh[0][2], fresh[1][2], fresh[2][2], fresh[3][2], fresh[4][2], fresh[5][2], fresh[6][2], fresh[7][2])
```

```python
import functools
import math

import jax
import jax.numpy as jnp
from jax import lax
from jax.experimental import pallas as pl
from jax.experimental.pallas import tpu as pltpu
from jax.sharding import PartitionSpec as P

HEAD_SIZE = 128
WINDOW = 1024
STEP = 5
EPS = 1e-06
THETA = 1000000.0
BETA_ONE = 0.5
BETA_TWO = 0.5
RATE_MATRIX = 0.02
RATE_GAIN = 0.3
DECAY = 0.1
ADAM_EPS = 1e-08
NEGATIVE = -1e30
SLICES = 4
BF = jnp.bfloat16
F32 = jnp.float32
VMEM_LIMIT = 63 * 1024 * 1024
MESH = pl.DeviceIdType.MESH


class Place:
    def __init__(self, sequences):
        self.count = sequences
        self.locate()

    def locate(self):
        self.dp, self.tensor = lax.axis_index("dp"), lax.axis_index("tensor")
        self.sequence, self.half = self.dp // 2, self.dp % 2
        self.y, self.core = self.tensor // 2, self.tensor % 2
        across = 1 - 2 * self.half
        beside = 2 - 4 * self.y
        self.partner = {
            "core": (self.dp, self.tensor + 1 - 2 * self.core),
            "x": (self.dp + across, self.tensor),
            "y": (self.dp, self.tensor + beside),
            "first": (self.dp + (1 - self.core) * across, self.tensor + self.core * beside),
            "second": (self.dp + self.core * across, self.tensor + (1 - self.core) * beside),
            "right": (self.dp + 2, self.tensor),
            "left": (self.dp - 2, self.tensor),
        }

    def of_group(self, g):
        dh = (g // 4 + self.half) % 2
        dy = ((g // 2) % 2 + self.y) % 2
        dc = (g % 2 + self.core) % 2
        from_core = (self.core + dc) % 2
        straight = dh * 2 + dy
        return dc * 4 + straight + from_core * (dy * 2 + dh - straight)

    def greet(self):
        barrier = pltpu.get_barrier_semaphore()
        for name in ("core", "x", "y"):
            pl.semaphore_signal(barrier, inc=1, device_id=self.partner[name], device_id_type=MESH)

        @pl.when(self.sequence >= 1)
        def _():
            pl.semaphore_signal(barrier, inc=1, device_id=self.partner["left"], device_id_type=MESH)

        @pl.when(self.sequence <= self.count - 2)
        def _():
            pl.semaphore_signal(barrier, inc=1, device_id=self.partner["right"], device_id_type=MESH)

        ends = (self.sequence + self.count - 1) // self.count + (2 * self.count - 2 - self.sequence) // self.count
        pl.semaphore_wait(barrier, 3 + ends)

    def copy(self, source, target, send, recv, name):
        return pltpu.make_async_remote_copy(
            src_ref=source, dst_ref=target, send_sem=send, recv_sem=recv,
            device_id=self.partner[name], device_id_type=MESH,
        )


class Gather:
    moves = [("second", 0, 1), ("first", 0, 2), ("first", 1, 3)] + [("core", p, p + 4) for p in range(4)]

    def __init__(self, place, buffer, group, send, recv, own=None):
        self.place, self.buffer, self.group = place, buffer, group
        self.send, self.recv, self.own = send, recv, own

    def at(self, index):
        return self.buffer.at[pl.ds(index * self.group, self.group)]

    def copy(self, index):
        name, source, target = self.moves[index]
        source = self.own if self.own is not None and source == 0 else self.at(source)
        return self.place.copy(source, self.at(target), self.send.at[index], self.recv.at[index], name)

    def start(self):
        for index in (0, 1, 3):
            self.copy(index).start()

    def step(self, index):
        if index == 1:
            self.copy(0).wait_recv()
            self.copy(2).start()
            self.copy(4).start()
        else:
            self.copy(index - 1).wait_recv()
            self.copy(index + 3).start()

    def arrived(self, index):
        self.copy(3 + index).wait_recv()

    def sent(self):
        for index in range(7):
            self.copy(index).wait_send()


class Line:
    def __init__(self, place, slot, send, recv):
        self.place, self.slot = place, slot
        self.sends, self.recvs = send, recv

    def move(self, way, stage):
        place = self.place
        shard = place.sequence - stage if way == 0 else place.sequence + stage
        target = self.slot(shard)
        name = "right" if way == 0 else "left"
        return place.copy(target, target, self.sends.at[way, stage], self.recvs.at[way, stage], name)

    def conditions(self, stage):
        place = self.place
        last = place.count - 1
        sends = (
            (place.sequence >= stage) & (place.sequence <= last - 1),
            (place.sequence <= last - stage) & (place.sequence >= 1),
        )
        recvs = (place.sequence >= stage + 1, place.sequence <= last - 1 - stage)
        return sends, recvs

    def start(self, stage):
        for way, condition in enumerate(self.conditions(stage)[0]):
            @pl.when(condition)
            def _(way=way):
                self.move(way, stage).start()

    def arrived(self, stage):
        for way, condition in enumerate(self.conditions(stage)[1]):
            @pl.when(condition)
            def _(way=way):
                place = self.place
                shard = place.sequence - 1 - stage if way == 0 else place.sequence + 1 + stage
                target = self.slot(shard)
                place.copy(
                    target, target, self.sends.at[way, stage], self.recvs.at[way, stage],
                    "right" if way == 0 else "left",
                ).wait_recv()

    def sent(self, stage):
        for way, condition in enumerate(self.conditions(stage)[0]):
            @pl.when(condition)
            def _(way=way):
                self.move(way, stage).wait_send()


def turn(head, cosine, sine):
    return head * cosine + pltpu.roll(head, HEAD_SIZE // 2, 1) * sine


def key_range(block_at, block):
    low = max(0, block_at * block - WINDOW + 1) // block * block
    return low, (block_at + 1) * block


def allowed_pairs(segment_rows, segment_columns, block_at, block):
    low, high = key_range(block_at, block)
    shape = (block, high - low)
    distance = (
        lax.broadcasted_iota(jnp.int32, shape, 0)
        - lax.broadcasted_iota(jnp.int32, shape, 1)
        + (block_at * block - low)
    )
    same = segment_rows[block_at * block : high, 0:1] == segment_columns[0:1, low:high]
    return same & (distance >= 0) & (distance < WINDOW)


NT = (((1,), (1,)), ((), ()))
TN = (((0,), (0,)), ((), ()))


def rows_at(index, size):
    return pl.ds(pl.multiple_of(index * size, size), size)


def group_at(place, p):
    dc = p // 4
    from_core = (place.core + dc) % 2
    one, two = (p // 2) % 2, p % 2
    dh = one + from_core * (two - one)
    dy = two + from_core * (one - two)
    return ((dh + place.half) % 2) * 4 + ((dy + place.y) % 2) * 2 + (dc + place.core) % 2


def attend_blocks(place, heads, q_cols, k_cols, aux, columns_ref, between):
    block = heads.shape[0] // 8
    qkv_cols = q_cols + 2 * k_cols
    scale = 1.0 / math.sqrt(HEAD_SIZE)
    for at in range(8):
        low, high = key_range(at, block)
        allowed = allowed_pairs(aux, columns_ref, at, block)
        keys, values = heads[low:high, q_cols : q_cols + k_cols], heads[low:high, q_cols + k_cols : qkv_cols]
        to = rows_at(place.of_group(at), block)
        for head in range(q_cols // HEAD_SIZE):
            columns = slice(head * HEAD_SIZE, (head + 1) * HEAD_SIZE)
            rows = heads[at * block : high, columns]
            scores = lax.dot_general(rows, keys, NT, preferred_element_type=F32) * scale
            scores = jnp.where(allowed, scores, NEGATIVE)
            top = jnp.max(scores, -1, keepdims=True)
            weights = jnp.exp(scores - top)
            total = jnp.sum(weights, -1, keepdims=True)
            probs = (weights * (1.0 / total)).astype(BF)
            heads[to, qkv_cols + columns.start : qkv_cols + columns.stop] = jnp.dot(
                probs, values, preferred_element_type=F32
            ).astype(BF)
            aux[at * block : high, 1 + head : 2 + head] = top + jnp.log(total)
        between(at)


class LineSum:
    def __init__(self, place, item, rows, index, own, recv, loads, ring, send_sem, recv_sem, load_sem, before):
        self.place, self.item, self.index, self.own, self.recv = place, item, index, own, recv
        self.rows = pl.ds(*rows)
        self.loads, self.ring = loads.at[:, self.rows], ring.at[:, self.rows]
        self.send_sem, self.recv_sem, self.load_sem = send_sem, recv_sem, load_sem
        self.before = before
        self.width = recv.shape[-1]

    def own_part(self, d):
        return self.own.at[self.item, self.rows, pl.ds(pl.multiple_of(d * self.width, self.width), self.width)]

    def dest(self, way, j):
        return self.place.count - 1 - j if way == 0 else j

    def move(self, way, j, source):
        return self.place.copy(
            source, self.recv.at[self.item, way, j, self.rows],
            self.send_sem.at[self.index, way, j], self.recv_sem.at[self.index, way, j],
            "right" if way == 0 else "left",
        )

    def start(self):
        last = self.place.count - 1
        for way, end in ((0, 0), (1, last)):
            @pl.when(self.place.sequence == end)
            def _(way=way):
                for j in range(last):
                    self.move(way, j, self.own_part(self.dest(way, j))).start()

    def turn_of(self, way, stage):
        depth = self.place.sequence if way == 0 else self.place.count - 1 - self.place.sequence
        return (depth >= 1) & (depth <= stage - 1), stage - 1 - depth, depth

    def slot(self, way, j):
        return j if way == 0 else self.place.count - 1 - self.place.sequence + j

    def own_load(self, way, d):
        return pltpu.make_async_copy(self.own_part(d), self.loads.at[2 * way], self.load_sem.at[2 * way])

    def came_load(self, way, j):
        return pltpu.make_async_copy(
            self.recv.at[self.item, way, j, self.rows], self.loads.at[2 * way + 1], self.load_sem.at[2 * way + 1]
        )

    def prepare(self, stage):
        for way in (0, 1):
            condition, j, _ = self.turn_of(way, stage)

            @pl.when(condition)
            def _(way=way, j=j):
                self.own_load(way, self.dest(way, j)).start()
                self.move(way, j, self.ring.at[self.slot(way, j)]).wait_recv()
                self.came_load(way, j).start()

    def service(self, stage):
        for way in (0, 1):
            condition, j, _ = self.turn_of(way, stage)

            @pl.when(condition)
            def _(way=way, j=j):
                slot = self.slot(way, j)
                if self.before is not None:
                    self.before.move(way, j, self.before.ring.at[slot]).wait_send()
                self.own_load(way, self.dest(way, j)).wait()
                self.came_load(way, j).wait()
                self.ring[slot] = (self.loads[2 * way].astype(F32) + self.loads[2 * way + 1].astype(F32)).astype(BF)
                self.move(way, j, self.ring.at[slot]).start()

    def last(self, way):
        place = self.place
        if way == 0:
            return place.sequence >= 1, place.count - 1 - place.sequence
        return place.sequence <= place.count - 2, place.sequence

    def prepare_total(self):
        self.own_load(0, self.place.sequence).start()
        for way in (0, 1):
            condition, j = self.last(way)

            @pl.when(condition)
            def _(way=way, j=j):
                self.move(way, j, self.loads.at[2 * way + 1]).wait_recv()
                self.came_load(way, j).start()

            @pl.when(jnp.logical_not(condition))
            def _(way=way):
                self.loads[2 * way + 1] = jnp.zeros(self.loads.shape[1:], BF)

    def total(self, out):
        self.own_load(0, self.place.sequence).wait()
        for way in (0, 1):
            condition, j = self.last(way)

            @pl.when(condition)
            def _(way=way, j=j):
                self.came_load(way, j).wait()

        out[...] = (
            self.loads[0].astype(F32) + self.loads[1].astype(F32) + self.loads[3].astype(F32)
        ).astype(BF)

    def sent(self, last_item):
        last = self.place.count - 1
        for way, end in ((0, 0), (1, last)):
            @pl.when(self.place.sequence == end)
            def _(way=way):
                for j in range(last):
                    self.move(way, j, self.own_part(self.dest(way, j))).wait_send()

        if last_item:
            for stage in range(2, last + 1):
                for way in (0, 1):
                    condition, j, _ = self.turn_of(way, stage)

                    @pl.when(condition)
                    def _(way=way, j=j):
                        self.move(way, j, self.ring.at[self.slot(way, j)]).wait_send()


class PlaneSum:
    def __init__(self, place, part, own, got, send_sem, recv_sem, chunk):
        self.place, self.part, self.own, self.got = place, part, own, got
        self.send_sem, self.recv_sem, self.chunk = send_sem, recv_sem, chunk
        self.group = own.shape[0]

    def columns(self, c):
        return pl.ds(c * self.chunk, self.chunk)

    def move(self, step, c):
        group, columns = self.group, self.columns(c)
        rows = ((4, 4), (2, 2), (1, 1))[step]
        name = ("core", "first", "second")[step]
        return self.place.copy(
            self.part.at[pl.ds(rows[0] * group, rows[1] * group), columns], self.got[step].at[:, columns],
            self.send_sem.at[step, c], self.recv_sem.at[step, c], name,
        )

    def push(self, c):
        self.move(0, c).start()

    def middle(self, c):
        self.move(0, c).wait_recv()
        rows, columns = pl.ds(2 * self.group, 2 * self.group), self.columns(c)
        self.part[rows, columns] = (
            self.part[rows, columns].astype(F32) + self.got[0][rows, columns].astype(F32)
        ).astype(BF)
        self.move(1, c).start()

    def late(self, c):
        self.move(1, c).wait_recv()
        rows, columns = pl.ds(self.group, self.group), self.columns(c)
        self.part[rows, columns] = (
            self.part[rows, columns].astype(F32)
            + self.got[0][rows, columns].astype(F32)
            + self.got[1][rows, columns].astype(F32)
        ).astype(BF)
        self.move(2, c).start()

    def total(self, c):
        self.move(2, c).wait_recv()
        rows, columns = pl.ds(0, self.group), self.columns(c)
        self.own[:, columns] = (
            self.own[:, columns]
            + self.got[0][rows, columns].astype(F32)
            + self.got[1][rows, columns].astype(F32)
            + self.got[2][:, columns].astype(F32)
        )

    def sent(self, c):
        for step in range(3):
            self.move(step, c).wait_send()


class HalfGather:
    def __init__(self, place, own, buffer, send, recv, local):
        self.place = place
        group = own.shape[0]
        tensor, across = place.tensor, place.tensor + 2 - 4 * place.y

        def at(index):
            return buffer.at[rows_at(index, group)]

        self.keep = pltpu.make_async_copy(own, at(tensor), local)
        self.y = place.copy(own, at(tensor), send.at[0], recv.at[0], "y")
        self.core = place.copy(own, at(tensor), send.at[1], recv.at[1], "core")
        self.far = place.copy(at(across), at(across), send.at[2], recv.at[2], "core")

    def start(self):
        self.keep.start()
        self.y.start()
        self.core.start()

    def step(self):
        self.y.wait_recv()
        self.far.start()

    def end(self):
        self.keep.wait()
        self.y.wait_send()
        self.core.wait()
        self.far.wait()


def layer_kernel(
    count, gains_here,
    block_input, out_grad, gains, table_half, marks_half,
    w_query, w_key, w_value, w_output, w_gate, w_up, w_down,
    block_output, input_gradient, shares, gain_out,
    own_grads, line_got, w_attention, w_forward, normed_out, heads_out, table_out, aux_out,
    second, grad, both, wide, got_core, got_first, got_second, loads, ring, ready, turned,
    one, two, own_rows, small_own, small_got, small_all, gain_ref, marks_ref,
    load_sem, wide_sem, ready_sem, swap_send, swap_recv, line_send, line_recv, sum_send, sum_recv,
    gather_send, gather_recv, half_send, half_recv, small_send, small_recv, gain_send, gain_recv, free_sem,
    line_load_sem, early_send, early_recv, slice_send, slice_recv, shard_send, shard_recv, master_sem, keep_sem, out_sem,
):
    place = Place(count)
    group, width = own_rows.shape
    tokens = 8 * group
    packed = wide.shape[1]
    slice_cols = packed // 3
    pair = 2 * slice_cols
    shard = w_query.shape[0]
    q_cols, k_cols = w_query.shape[1] // 2, w_key.shape[1] // 2
    qkv_cols = q_cols + 2 * k_cols
    shard2 = line_got.shape[-1]
    part_width = shares.shape[-1]
    chunk = width // 8
    big = width // 4
    block = 2 * group
    got = (got_core, got_first, got_second)

    def load_wide(source, index):
        return pltpu.make_async_copy(source, wide, wide_sem.at[index])

    def shard_rows():
        return pl.ds(pl.multiple_of(place.dp * shard, shard), shard)

    def sequence_rows(k):
        return pl.ds(pl.multiple_of(k * 2 * shard, 2 * shard), 2 * shard)

    local = pltpu.make_async_copy

    masters = [
        local(w_query, one.at[pl.ds(0, shard), pl.ds(0, 2 * q_cols)], master_sem.at[0]),
        local(w_key, one.at[pl.ds(0, shard), pl.ds(2 * q_cols, 2 * k_cols)], master_sem.at[1]),
        local(w_value, one.at[pl.ds(0, shard), pl.ds(2 * q_cols + 2 * k_cols, 2 * k_cols)], master_sem.at[2]),
    ]
    own_loads = [
        local(block_input.at[rows_at(place.tensor, group)], both.at[pl.ds(0, group)], load_sem.at[2]),
        local(out_grad.at[rows_at(place.tensor, group)], grad.at[pl.ds(0, group)], load_sem.at[3]),
    ]
    table_keep = local(table_half, table_out.at[rows_at(place.half, 4 * group)], load_sem.at[4])
    for copy in masters + own_loads + [table_keep]:
        copy.start()
    marks_ref[:, rows_at(place.half, 4 * group)] = marks_half[...]

    def early(index):
        columns = rows_at(place.half, 4 * group)
        source, target = (
            (own_rows.at[pl.ds(0, shard), pl.ds(0, packed)], wide.at[shard_rows()]),
            (marks_half, marks_ref.at[:, columns]),
            (table_half, table_out.at[columns]),
            (gains, gain_ref.at[:, shard_rows()] if gains_here else None),
        )[index]
        return place.copy(source, target, early_send.at[index], early_recv.at[index], "x")

    def unit(s, theirs, part):
        k = 2 * s + theirs
        if part == 0:
            return pl.ds((k // 4) * slice_cols, shard), pl.ds((k % 4) * pair, pair)
        return pl.ds(pair, shard), pl.ds(k * slice_cols, slice_cols)

    def slice_target(s, part):
        return w_forward.at[s, shard_rows(), pl.ds(0, pair) if part == 0 else pl.ds(pair, slice_cols)]

    def slice_swap(s, part):
        return place.copy(
            turned.at[unit(s, 1, part)], slice_target(s, part), slice_send.at[s, part], slice_recv.at[s, part], "x"
        )

    def slice_keep(s, part):
        return local(turned.at[unit(s, 0, part)], slice_target(s, part), keep_sem.at[s, part])

    lines = [
        Line(
            place, lambda k: wide.at[sequence_rows(k), pl.ds(0, qkv_cols)], shard_send.at[0], shard_recv.at[0]
        )
    ] + [
        Line(
            place, lambda k, s=s: w_forward.at[s, sequence_rows(k)], shard_send.at[1 + s], shard_recv.at[1 + s]
        )
        for s in range(SLICES)
    ]
    output_line = Line(
        place, lambda k: wide.at[sequence_rows(k), pl.ds(qkv_cols, q_cols)],
        shard_send.at[2 + SLICES], shard_recv.at[2 + SLICES],
    )

    def output_steps(first, last):
        for stage in range(min(first, count - 1), min(last, count - 1)):
            output_line.arrived(stage)
            if stage < count - 2:
                output_line.start(stage + 1)

    gain_shards = Line(
        place, lambda k: gain_ref.at[:, sequence_rows(k)], shard_send.at[1 + SLICES], shard_recv.at[1 + SLICES]
    )

    begin = (0, 1, 2 * count - 3, 3 * count - 4)
    sends = sorted(
        ((s, stage) for s in range(SLICES) for stage in range(count - 1)),
        key=lambda item: (begin[item[0]] + 2 * item[1], item[0]),
    )

    def advance(number):
        for _ in range(min(number, len(sends))):
            s, stage = sends.pop(0)
            if stage == 0:
                for part in range(2):
                    slice_swap(s, part).wait_recv()
            else:
                lines[1 + s].arrived(stage - 1)
            lines[1 + s].start(stage)

    def advance_through(s):
        while any(item[0] == s for item in sends):
            advance(1)

    place.greet()

    def attention_shard(output, target, rows, side):
        target[rows, :q_cols] = one[:shard, rows_at(side, q_cols)].astype(BF)
        for index in range(2):
            base = 2 * q_cols + 2 * k_cols * index
            target[rows, q_cols + k_cols * index : q_cols + k_cols * (index + 1)] = one[
                :shard, pl.ds(pl.multiple_of(base + side * k_cols, k_cols), k_cols)
            ].astype(BF)
        target[rows, qkv_cols:packed] = output[rows_at(side, q_cols), :].T.astype(BF)

    def fill_attention(output):
        place.locate()
        output_load = local(w_output, output, master_sem.at[3])
        output_load.start()
        for copy in masters + [output_load]:
            copy.wait()
        attention_shard(output, own_rows, slice(0, shard), 1 - place.half)
        early(0).start()
        attention_shard(output, wide, shard_rows(), place.half)

    pl.run_scoped(fill_attention, pltpu.VMEM(w_output.shape, F32))
    place.locate()
    masters = [
        local(w_gate, one.at[pl.ds(0, shard)], master_sem.at[0]),
        local(w_up, two.at[pl.ds(0, shard)], master_sem.at[1]),
    ]
    for copy in masters:
        copy.start()
    early(1).start()
    if gains_here:
        gain_ref[:, shard_rows()] = gains[...]
        early(3).start()
    else:
        gain_ref[...] = gains[...]
    inputs = Gather(place, both, group, gather_send.at[0], gather_recv.at[0])
    own_loads[0].wait()
    inputs.start()
    early(0).wait_recv()
    lines[0].start(0)
    if gains_here:
        early(3).wait_recv()
        gain_shards.start(0)

    def fill_slices(down):
        place.locate()
        down_load = local(w_down, down, master_sem.at[2])
        down_load.start()
        for copy in masters + [down_load]:
            copy.wait()
        for s in range(SLICES):
            for theirs in (1, 0):
                side = place.half + theirs - 2 * theirs * place.half
                columns = rows_at(side * SLICES + s, slice_cols)
                (rows, at), (down_rows, down_at) = unit(s, theirs, 0), unit(s, theirs, 1)
                turned[rows, pl.ds(at.start, slice_cols)] = one[:shard, columns].astype(BF)
                turned[rows, pl.ds(at.start + slice_cols, slice_cols)] = two[:shard, columns].astype(BF)
                turned[down_rows, down_at] = down[columns, :].T.astype(BF)
            for part in range(2):
                slice_keep(s, part).start()
            if s == 0:
                inputs.step(1)

    pl.run_scoped(fill_slices, pltpu.VMEM(w_down.shape, F32))
    place.locate()
    if gains_here:
        for stage in range(count - 1):
            gain_shards.arrived(stage)
            if stage < count - 2:
                gain_shards.start(stage + 1)
    lines[0].arrived(0)
    if count > 2:
        lines[0].start(1)

    def start_swap(s):
        for part in range(2):
            slice_swap(s, part).start()

    inputs.step(2)
    inputs.step(3)
    start_swap(0)
    start_swap(1)
    early(2).start()

    def norm_block(p, _):
        rows = rows_at(p, group)
        x = both[rows, :].astype(F32)
        factor = lax.rsqrt(jnp.mean(x * x, -1, keepdims=True) + EPS)
        second[rows, :] = (x * factor * gain_ref[0:1, :]).astype(BF)
        return 0

    lax.fori_loop(0, 4, norm_block, 0)
    for stage in range(1, count - 1):
        lines[0].arrived(stage)
        if stage < count - 2:
            lines[0].start(stage + 1)
    for p in range(4):
        inputs.arrived(p)
    lax.fori_loop(4, 8, norm_block, 0)
    for s in range(SLICES):
        for part in range(2):
            slice_keep(s, part).wait()
    output_line.start(0)
    grads = Gather(place, grad, group, gather_send.at[2], gather_recv.at[2])
    own_loads[1].wait()
    grads.start()
    start_swap(2)
    normed_copy = local(second, normed_out, out_sem.at[0])
    wide_copy = local(wide, w_attention, out_sem.at[1])
    normed_copy.start()
    mixed = PlaneSum(place, both, two, got, sum_send.at[0], sum_recv.at[0], chunk)

    def attention_forward(heads, table, aux):
        place.locate()
        table_keep.wait()
        early(2).wait_recv()
        table_load = local(table_out, table, load_sem.at[4])
        table_load.start()
        aux[...] = jnp.zeros_like(aux)
        early(1).wait_recv()
        tile = (HEAD_SIZE, HEAD_SIZE)
        diagonal = lax.broadcasted_iota(jnp.int32, tile, 0) == lax.broadcasted_iota(jnp.int32, tile, 1)
        for at in range(0, tokens, HEAD_SIZE):
            aux[at : at + HEAD_SIZE, 0:1] = jnp.sum(
                jnp.where(diagonal, marks_ref[0:1, at : at + HEAD_SIZE], 0.0), -1, keepdims=True
            )
        table_load.wait()

        def project_block(p, _):
            out = jnp.dot(second[rows_at(p, group), :], wide[:, :qkv_cols], preferred_element_type=F32)
            to = rows_at(group_at(place, p), group)
            cosine, sine = rotation(table[to, :])
            for at in range(0, q_cols + k_cols, HEAD_SIZE):
                heads[to, at : at + HEAD_SIZE] = turn(out[:, at : at + HEAD_SIZE], cosine, sine).astype(BF)
            heads[to, q_cols + k_cols : qkv_cols] = out[:, q_cols + k_cols :].astype(BF)
            return 0

        lax.fori_loop(0, 8, project_block, 0)
        output_steps(0, 1)
        advance(1)
        grads.step(1)

        def between(at):
            if at == 2:
                output_steps(1, 2)
            if at == 3:
                advance(1)
            if at == 5:
                output_steps(2, count)
            if at == 6:
                advance(1)

        attend_blocks(place, heads, q_cols, k_cols, aux, marks_ref, between)
        wide_copy.start()
        heads_copy = local(heads, heads_out, out_sem.at[2])
        aux_copy = local(aux, aux_out, out_sem.at[3])
        heads_copy.start()
        aux_copy.start()
        inputs.sent()
        normed_copy.wait()

        for c in range(8):
            columns = pl.ds(c * chunk, chunk)

            def mixed_part(rows, c=c):
                return lax.dot_general(
                    heads[rows, qkv_cols:], wide[c * chunk : (c + 1) * chunk, qkv_cols:], NT,
                    preferred_element_type=F32,
                )

            def mixed_rows(b, _, columns=columns, mixed_part=mixed_part):
                rows = rows_at(b, block)
                both[rows, columns] = mixed_part(rows).astype(BF)
                return 0

            first = mixed_part(pl.ds(0, block))
            two[:, columns] = first[:group]
            both[pl.ds(group, group), columns] = first[group:].astype(BF)
            lax.fori_loop(1, 4, mixed_rows, 0)
            mixed.push(c)
            if c >= 1:
                mixed.middle(c - 1)
            if c >= 3:
                mixed.late(c - 3)
            if c >= 5:
                mixed.total(c - 5)
            if c == 2:
                advance(1)
            if c == 3:
                grads.step(2)
            if c == 4:
                grads.step(3)
            if c == 6:
                advance(1)
        heads_copy.wait()
        aux_copy.wait()

    pl.run_scoped(
        attention_forward,
        pltpu.VMEM((tokens, packed), BF), pltpu.VMEM((tokens, HEAD_SIZE), F32), pltpu.VMEM((tokens, HEAD_SIZE), F32),
    )
    place.locate()
    mixed.middle(7)
    for c in (5, 6, 7):
        mixed.late(c)
        mixed.total(c - 2)
    mixed.total(6)
    mixed.total(7)
    early(0).wait_send()

    def by_rows(step):
        def some(b, _):
            step(rows_at(b, group // 4))
            return 0

        lax.fori_loop(0, 4, some, 0)

    def residual_step(rows):
        residual = two[rows, :] + both[rows, :].astype(F32)
        two[rows, :] = residual
        factor = lax.rsqrt(jnp.mean(residual * residual, -1, keepdims=True) + EPS)
        normal = (residual * factor * gain_ref[1:2, :]).astype(BF)
        own_rows[rows, :] = normal
        second[rows, :] = normal

    by_rows(residual_step)
    seconds = Gather(place, second, group, gather_send.at[1], gather_recv.at[1], own_rows)
    seconds.start()
    start_swap(3)
    advance(1)
    seconds.step(1)
    advance(1)
    wide_copy.wait()
    for stage in range(count - 1):
        lines[0].sent(stage)
        output_line.sent(stage)
    for c in range(8):
        mixed.sent(c)
    for s in range(SLICES):
        for part in range(2):
            if s < SLICES - 1:
                slice_swap(s, part).wait_send()
    seconds.step(2)
    seconds.step(3)
    for part in range(2):
        slice_swap(SLICES - 1, part).wait_send()
    for p in range(4):
        grads.arrived(p)
    advance(1)
    for p in range(4):
        seconds.arrived(p)
    seconds.sent()
    grads.sent()

    sums = []
    sum_items = [(s, 0, packed) for s in range(SLICES)]
    sum_items += [(SLICES, qkv_cols, q_cols), (SLICES, 0, qkv_cols)]
    for index, (item, low, size) in enumerate(sum_items):
        sums.append(
            LineSum(
                place, item, (low, size), index, own_grads, line_got, loads, ring, line_send, line_recv, line_load_sem,
                sums[-1] if sums else None,
            )
        )

    pending = {0: [], 1: []}
    turn_at = [0]

    def next_ready():
        slot = turn_at[0] % 2
        turn_at[0] += 1
        for wait in pending[slot]:
            wait()
        pending[slot] = []
        return slot

    def flush():
        for slot in (0, 1):
            for wait in pending[slot]:
                wait()
            pending[slot] = []

    swaps = []

    def finish(index):
        item, low, size = sum_items[index]
        slot = next_ready()
        rows = pl.ds(low, size)
        sums[index].total(ready.at[slot, rows, pl.ds(0, shard2)])

        def parts():
            if part_width == shard2:
                mine = theirs = ready.at[slot, rows, pl.ds(0, shard2)]
            else:
                mine, theirs = [
                    ready.at[slot, rows, pl.ds(pl.multiple_of(side * part_width, part_width), part_width)]
                    for side in (place.half, 1 - place.half)
                ]
            target = shares.at[place.half, item, rows]
            keep = pltpu.make_async_copy(mine, target, ready_sem.at[slot])
            swap = place.copy(theirs, target, swap_send.at[index], swap_recv.at[index], "x")
            return keep, swap

        for copy in parts():
            copy.start()
        pending[slot] += [lambda: parts()[0].wait(), lambda: parts()[1].wait_send()]
        swaps.append(lambda: parts()[1].wait_recv())

    def stages_of(kind):
        return list(range(2, min(3, count)) if kind == "first" else range(3, count))

    def prepare(item, kind):
        if kind == "total":
            sums[item].prepare_total()
        elif stages_of(kind):
            sums[item].prepare(stages_of(kind)[0])

    def complete(item, kind):
        if kind == "total":
            finish(item)
            return
        for index, stage in enumerate(stages_of(kind)):
            if index:
                sums[item].prepare(stage)
            sums[item].service(stage)

    def weight_grads(item, low, high, right, tasks=()):
        for c in range(4):
            for at, do, task in tasks:
                if at == c:
                    do(*task)
            slot = next_ready()
            columns = pl.ds(c * big, big)
            for first, last, matrix in zip(low, high, right):
                ready[slot, first:last, :] = jnp.dot(
                    turned[first:last, :], matrix[:, columns], preferred_element_type=F32
                ).astype(BF)
            rows = pl.ds(low[0], high[-1] - low[0])
            copy = pltpu.make_async_copy(ready.at[slot, rows], own_grads.at[item, rows, columns], ready_sem.at[slot])
            copy.start()
            pending[slot].append(copy.wait)

    plane = PlaneSum(place, grad, one, got, sum_send.at[1], sum_recv.at[1], chunk)

    def give_credit(index):
        for name in ("core", "first", "second"):
            pl.semaphore_signal(free_sem.at[index], inc=1, device_id=place.partner[name], device_id_type=MESH)

    def second_step(rows):
        residual, grad_second = two[rows, :], one[rows, :]
        factor = lax.rsqrt(jnp.mean(residual * residual, -1, keepdims=True) + EPS)
        normal = residual * factor
        small_own[1:2, :] += jnp.sum(grad_second * normal, 0, keepdims=True)
        scaled = grad_second * gain_ref[1:2, :]
        residual_grad = grad[rows, :].astype(F32) + factor * (
            scaled - normal * jnp.mean(scaled * normal, -1, keepdims=True)
        )
        one[rows, :] = residual_grad
        own_rows[rows, :] = residual_grad.astype(BF)
        both[rows, :] = residual_grad.astype(BF)

    branch = Gather(place, both, group, gather_send.at[3], gather_recv.at[3], own_rows)

    def feed_forward(hidden):
        place.locate()
        for s in range(SLICES):
            advance_through(s)
            lines[1 + s].arrived(count - 2)
            load_wide(w_forward.at[s], s).start()
            load_wide(w_forward.at[s], s).wait()

            def rows_step(b, _, s=s):
                rows = rows_at(b, block)
                gate_up = jnp.dot(second[rows, :], wide[:, :pair], preferred_element_type=F32)
                grad_hidden = jnp.dot(grad[rows, :], wide[:, pair:], preferred_element_type=F32)
                gate, up = gate_up[:, :slice_cols], gate_up[:, slice_cols:]
                sigmoid = 1.0 / (1.0 + jnp.exp(-gate))
                activated = gate * sigmoid
                hidden_rows = (activated * up).astype(BF)
                gate_rows = (grad_hidden * up * (sigmoid + activated * (1.0 - sigmoid))).astype(BF)
                up_rows = (grad_hidden * activated).astype(BF)
                hidden[rows, s * slice_cols : (s + 1) * slice_cols] = hidden_rows
                both[rows, s * pair : s * pair + slice_cols] = gate_rows
                both[rows, s * pair + slice_cols : (s + 1) * pair] = up_rows
                turned[:slice_cols, rows] = gate_rows.T
                turned[slice_cols:pair, rows] = up_rows.T
                turned[pair:, rows] = hidden_rows.T
                return 0

            lax.fori_loop(0, 4, rows_step, 0)
            advance(1)
            weight_grads(
                s, (0, pair), (pair, packed), (second, grad),
                (
                    (),
                    ((2, prepare, (0, "first")), (3, complete, (0, "first"))),
                    ((2, prepare, (0, "later")), (3, complete, (0, "later"))),
                    (
                        (0, prepare, (0, "total")), (1, complete, (0, "total")),
                        (2, prepare, (1, "first")), (3, complete, (1, "first")),
                    ),
                )[s],
            )
            flush()
            sums[s].start()
            advance(1)

        def chunk_loads(c, low):
            base = (c % 2) * SLICES
            return [
                pltpu.make_async_copy(
                    w_forward.at[s, pl.ds(c * chunk, chunk), pl.ds(low, packed - low)],
                    wide.at[pl.ds((base + s) * chunk, chunk), pl.ds(low, packed - low)],
                    wide_sem.at[SLICES + base + s],
                )
                for s in range(SLICES)
            ]

        def summed(source, rows, step, low, high, base):
            return sum(
                lax.dot_general(
                    source[rows, s * step : (s + 1) * step],
                    wide[(base + s) * chunk : (base + s + 1) * chunk, low:high], NT,
                    preferred_element_type=F32,
                )
                for s in range(SLICES)
            )

        for copy in chunk_loads(0, 0):
            copy.start()
        for c in range(8):
            if c < 7:
                for copy in chunk_loads(c + 1, 0):
                    copy.start()
            for copy in chunk_loads(c, 0):
                copy.wait()
            base = (c % 2) * SLICES
            columns = pl.ds(c * chunk, chunk)

            def grad_rows(b, _, columns=columns, base=base):
                rows = rows_at(b, block)
                grad[rows, columns] = summed(both, rows, pair, 0, pair, base).astype(BF)
                return 0

            first = summed(both, pl.ds(0, block), pair, 0, pair, base)
            one[:, columns] = first[:group]
            grad[pl.ds(group, group), columns] = first[group:].astype(BF)
            lax.fori_loop(1, 4, grad_rows, 0)
            plane.push(c)
            if c >= 1:
                plane.middle(c - 1)
            if c >= 2:
                plane.late(c - 2)
            if c >= 3:
                plane.total(c - 3)
            if c == 3:
                prepare(1, "later")
            if c == 4:
                complete(1, "later")
        for copy in chunk_loads(0, pair):
            copy.start()
        plane.middle(7)
        plane.late(6)
        plane.late(7)
        prepare(1, "total")
        for c in (5, 6, 7):
            plane.total(c)
        give_credit(0)
        complete(1, "total")
        small_own[...] = jnp.zeros_like(small_own)
        by_rows(second_step)
        branch.start()
        prepare(2, "first")
        for c in range(8):
            if c < 7:
                for copy in chunk_loads(c + 1, pair):
                    copy.start()
            for copy in chunk_loads(c, pair):
                copy.wait()

            def branch_rows(b, _, c=c):
                rows = rows_at(b, block)
                second[rows, pl.ds(c * chunk, chunk)] = summed(
                    hidden, rows, slice_cols, pair, packed, (c % 2) * SLICES
                ).astype(BF)
                return 0

            lax.fori_loop(0, 4, branch_rows, 0)
            if c == 0:
                complete(2, "first")
            if c == 5:
                branch.step(1)

    pl.run_scoped(feed_forward, pltpu.VMEM((tokens, SLICES * slice_cols), BF))
    place.locate()
    w_load = load_wide(w_attention, 0)
    w_load.start()

    outer = PlaneSum(place, second, two, got, sum_send.at[2], sum_recv.at[2], width)

    def rows_add(target, first_row, rows, sources):
        def step(b, _):
            at = rows_at(b, group)
            to = pl.ds(pl.multiple_of(first_row + b * group, group), group)
            value = target[to, :].astype(F32)
            for source in sources:
                value = value + source[to, :].astype(F32)
            target[to, :] = value.astype(BF)
            return 0

        lax.fori_loop(0, rows // group, step, 0)

    pl.semaphore_wait(free_sem.at[0], 3)
    outer.push(0)
    for c in range(8):
        plane.sent(c)
    marks = [0, q_cols, q_cols + k_cols, qkv_cols, qkv_cols + q_cols, qkv_cols + 2 * q_cols]
    arrays = [local(heads_out, grad.at[:, pl.ds(0, packed)], load_sem.at[5])]
    for copy in arrays:
        copy.start()
    q_ref, k_ref = grad.at[:, pl.ds(0, q_cols)], grad.at[:, pl.ds(marks[1], k_cols)]
    v_ref, attended = grad.at[:, pl.ds(marks[2], k_cols)], grad.at[:, pl.ds(marks[3], q_cols)]
    attended_grad, qkv_grad = grad.at[:, pl.ds(marks[4], q_cols)], grad.at[:, pl.ds(marks[5], qkv_cols)]
    prepare(2, "later")
    w_load.wait()

    def attended_step(p, _):
        rows = rows_at(p, group)
        attended_grad[rows, :] = jnp.dot(
            both[rows, :], wide[:, qkv_cols:], preferred_element_type=F32
        ).astype(BF)
        return 0

    for copy in arrays:
        copy.wait()
    lax.fori_loop(0, 2, attended_step, 0)
    branch.step(2)
    branch.step(3)
    outer.move(0, 0).wait_recv()
    rows_add(second, 2 * group, 2 * group, (got_core,))
    outer.move(1, 0).start()
    lax.fori_loop(2, 4, attended_step, 0)
    complete(2, "later")
    for p in range(4):
        branch.arrived(p)
    lax.fori_loop(4, 8, attended_step, 0)

    def outer_late():
        outer.move(1, 0).wait_recv()
        rows_add(second, group, group, (got_core, got_first))
        outer.move(2, 0).start()
        prepare(2, "total")

    def attention(table, aux, key_sum, value_sum):
        place.locate()
        table_load = pltpu.make_async_copy(table_out, table, load_sem.at[9])
        aux_load = pltpu.make_async_copy(aux_out, aux, load_sem.at[10])
        table_load.start()
        aux_load.start()
        table_load.wait()
        aux_load.wait()
        attend_back_blocks(
            place, q_ref, k_ref, v_ref, aux, marks_ref, attended_grad, table, qkv_grad, key_sum, value_sum,
            outer_late,
        )

    pl.run_scoped(
        attention,
        pltpu.VMEM((tokens, HEAD_SIZE), F32), pltpu.VMEM((tokens, HEAD_SIZE), F32),
        pltpu.VMEM((tokens, k_cols), F32), pltpu.VMEM((tokens, k_cols), F32),
    )
    place.locate()
    branch.sent()
    outer.move(2, 0).wait_recv()

    def output_step(rows):
        own_rows[rows, :] = (
            two[rows, :]
            + second[rows, :].astype(F32)
            + got_core[rows, :].astype(F32)
            + got_first[rows, :].astype(F32)
            + got_second[rows, :].astype(F32)
        ).astype(BF)

    by_rows(output_step)
    give_credit(1)
    blocks = HalfGather(place, own_rows, block_output, half_send.at[0], half_recv.at[0], load_sem.at[3])
    blocks.start()
    complete(2, "total")
    prepare(3, "first")

    def turn_rows(source, first, last):
        def step(b, _):
            rows = rows_at(b, group)
            turned[first:last, rows] = source[rows, :].T
            return 0

        lax.fori_loop(0, 8, step, 0)

    turn_rows(attended, qkv_cols, packed)
    weight_grads(SLICES, (qkv_cols,), (packed,), (both,))
    flush()
    sums[SLICES].start()
    normed_load = pltpu.make_async_copy(normed_out, both, load_sem.at[2])
    normed_load.start()
    complete(3, "first")
    turn_rows(qkv_grad, 0, qkv_cols)
    normed_load.wait()
    weight_grads(SLICES, (0,), (qkv_cols,), (both,))
    flush()
    sums[SLICES + 1].start()
    prepare(3, "later")

    outer.sent(0)
    pl.semaphore_wait(free_sem.at[1], 3)
    inner = PlaneSum(place, second, two, got, sum_send.at[3], sum_recv.at[3], chunk)
    for c in range(8):
        columns = pl.ds(c * chunk, chunk)

        def first_part(rows, c=c):
            return lax.dot_general(
                qkv_grad[rows, :], wide[c * chunk : (c + 1) * chunk, :qkv_cols], NT, preferred_element_type=F32
            )

        def first_rows(b, _, columns=columns, first_part=first_part):
            rows = rows_at(b, block)
            second[rows, columns] = first_part(rows).astype(BF)
            return 0

        first = first_part(pl.ds(0, block))
        two[:, columns] = first[:group]
        second[pl.ds(group, group), columns] = first[group:].astype(BF)
        lax.fori_loop(1, 4, first_rows, 0)
        inner.push(c)
        if c == 0:
            complete(3, "later")
        if c == 1:
            prepare(SLICES, "first")
        if c == 2:
            complete(SLICES, "first")
        if c == 4:
            prepare(SLICES + 1, "first")
        if c == 5:
            complete(SLICES + 1, "first")
        if c == 6:
            prepare(3, "total")
        if c == 7:
            complete(3, "total")
        if c >= 1:
            inner.middle(c - 1)
        if c >= 3:
            inner.late(c - 3)
        if c >= 5:
            inner.total(c - 5)
    inner.middle(7)
    prepare(SLICES, "later")
    blocks.step()
    for c in (5, 6, 7):
        inner.late(c)
        inner.total(c - 2)
    complete(SLICES, "later")
    inner.total(6)
    prepare(SLICES + 1, "later")
    inner.total(7)
    input_load = pltpu.make_async_copy(
        block_input.at[rows_at(place.tensor, group)], second.at[pl.ds(0, group)], load_sem.at[4]
    )
    input_load.start()
    input_load.wait()

    def first_step(rows):
        value, grad_first = second[rows, :].astype(F32), two[rows, :]
        factor = lax.rsqrt(jnp.mean(value * value, -1, keepdims=True) + EPS)
        normal = value * factor
        small_own[0:1, :] += jnp.sum(grad_first * normal, 0, keepdims=True)
        scaled = grad_first * gain_ref[0:1, :]
        input_grad = one[rows, :] + factor * (scaled - normal * jnp.mean(scaled * normal, -1, keepdims=True))
        second[rows, :] = input_grad.astype(BF)

    by_rows(first_step)
    gradients = HalfGather(
        place, second.at[pl.ds(0, group)], input_gradient, half_send.at[1], half_recv.at[1], load_sem.at[4]
    )
    gradients.start()
    complete(SLICES + 1, "later")

    for index, name in enumerate(("core", "y", "x")):
        move = place.copy(
            small_own.at[pl.ds(8 * index, 8)], small_got.at[index], small_send.at[index], small_recv.at[index], name
        )
        move.start()
        move.wait_recv()
        value = small_own[8 * index : 8 * index + 8, :] + small_got[index]
        if index < 2:
            small_own[8 * index + 8 : 8 * index + 16, :] = value
        else:
            small_all[place.sequence] = value
    gain_line = Line(place, lambda k: small_all.at[k], gain_send, gain_recv)
    gain_line.start(0)
    prepare(SLICES, "total")
    gradients.step()
    complete(SLICES, "total")
    for stage in range(count - 1):
        gain_line.arrived(stage)
        if stage < count - 2:
            gain_line.start(stage + 1)
    own_columns = pl.ds(pl.multiple_of(place.sequence * shard2, shard2), shard2)
    gain_out[...] = sum(small_all[k, :, own_columns] for k in range(count))
    prepare(SLICES + 1, "total")
    complete(SLICES + 1, "total")

    flush()
    for line in lines[1:]:
        for stage in range(count - 1):
            line.sent(stage)
    if gains_here:
        for stage in range(count - 1):
            gain_shards.sent(stage)
    for index in (1, 2, 3) if gains_here else (1, 2):
        early(index).wait_send()
    for item, item_sum in enumerate(sums):
        item_sum.sent(item == SLICES + 1)
    for arrived in swaps:
        arrived()
    for c in range(8):
        inner.sent(c)
    for index, name in enumerate(("core", "y", "x")):
        place.copy(
            small_own.at[pl.ds(8 * index, 8)], small_got.at[index], small_send.at[index], small_recv.at[index], name
        ).wait_send()
    for stage in range(count - 1):
        gain_line.sent(stage)
    blocks.end()
    gradients.end()


def rotation(table):
    other = pltpu.roll(table, HEAD_SIZE // 2, 1)
    low = lax.broadcasted_iota(jnp.int32, table.shape, 1) < HEAD_SIZE // 2
    return jnp.where(low, table, other), jnp.where(low, -other, table)


def attend_back_blocks(
    place, q_ref, k_ref, v_ref, aux, columns_ref, grad_ref, table, out_ref, key_sum, value_sum, late
):
    block = q_ref.shape[0] // 8
    scale = 1.0 / math.sqrt(HEAD_SIZE)
    q_cols, k_cols = q_ref.shape[1], k_ref.shape[1]
    key_sum[...] = jnp.zeros_like(key_sum)
    value_sum[...] = jnp.zeros_like(value_sum)
    for at in range(8):
        low, high = key_range(at, block)
        here = slice(at * block, high)
        span = slice(low, high)
        allowed = allowed_pairs(aux, columns_ref, at, block)
        keys, values = k_ref[span, :], v_ref[span, :]
        cosine, sine = rotation(table[here, :])
        to = rows_at(place.of_group(at), block)
        for head in range(q_cols // HEAD_SIZE):
            columns = slice(head * HEAD_SIZE, (head + 1) * HEAD_SIZE)
            rows = q_ref[here, columns]
            grad_rows = grad_ref[to, columns]
            scores = lax.dot_general(rows, keys, NT, preferred_element_type=F32) * scale
            scores = jnp.where(allowed, scores, NEGATIVE)
            probs = jnp.exp(scores - aux[here, 1 + head : 2 + head])
            value_sum[span, :] += lax.dot_general(
                probs.astype(BF), grad_rows, TN, preferred_element_type=F32
            )
            prob_grad = lax.dot_general(grad_rows, values, NT, preferred_element_type=F32)
            inner = jnp.sum(probs * prob_grad, -1, keepdims=True)
            score_grad = (probs * (prob_grad - inner)).astype(BF)
            query_grad = jnp.dot(score_grad, keys, preferred_element_type=F32) * scale
            key_sum[span, :] += lax.dot_general(score_grad, rows, TN, preferred_element_type=F32)
            out_ref[to, columns] = turn(query_grad, cosine, -sine).astype(BF)
        if at == 5:
            late()
    for at in range(8):
        here = slice(at * block, (at + 1) * block)
        cosine, sine = rotation(table[here, :])
        to = rows_at(place.of_group(at), block)
        out_ref[to, q_cols : q_cols + k_cols] = turn(key_sum[here, :] * scale, cosine, -sine).astype(BF)
        out_ref[to, q_cols + k_cols :] = value_sum[here, :].astype(BF)


def layer(block_input, out_grad, gains, table, marks, masters, count):
    half_tokens, width = block_input.shape
    group, tokens = half_tokens // 4, 2 * half_tokens
    shard = masters[0].shape[0]
    q_cols, k_cols = masters[0].shape[1] // 2, masters[1].shape[1] // 2
    slice_cols = masters[4].shape[1] // 2 // SLICES
    packed = 3 * slice_cols
    assert packed == 2 * q_cols + 2 * k_cols and q_cols == group >= shard
    gains_here = shard % 128 == 0
    if not gains_here:
        gains = lax.all_gather(gains, "dp", axis=1, tiled=True)
    part = shard if gains_here else 2 * shard
    vmem, hbm = pl.BlockSpec(memory_space=pltpu.VMEM), pl.BlockSpec(memory_space=pl.ANY)
    struct = jax.ShapeDtypeStruct
    dma = pltpu.SemaphoreType.DMA
    items = 1 + SLICES
    return pl.pallas_call(
        functools.partial(layer_kernel, count, gains_here),
        in_specs=[hbm, hbm, vmem, hbm, vmem] + [hbm] * 7,
        out_specs=[hbm] * 3 + [vmem] + [hbm] * 8,
        out_shape=[
            struct((half_tokens, width), BF),
            struct((half_tokens, width), BF),
            struct((2, items, packed, part), BF),
            struct((8, 2 * shard), F32),
            struct((items, packed, width), BF),
            struct((items, 2, count - 1, packed, 2 * shard), BF),
            struct((width, packed), BF),
            struct((SLICES, width, packed), BF),
            struct((tokens, width), BF),
            struct((tokens, packed), BF),
            struct((tokens, HEAD_SIZE), F32),
            struct((tokens, HEAD_SIZE), F32),
        ],
        scratch_shapes=[
            pltpu.VMEM((tokens, width), BF),
            pltpu.VMEM((tokens, width), BF),
            pltpu.VMEM((tokens, width), BF),
            pltpu.VMEM((width, packed), BF),
            pltpu.VMEM((4 * group, width), BF),
            pltpu.VMEM((2 * group, width), BF),
            pltpu.VMEM((group, width), BF),
            pltpu.VMEM((4, packed, 2 * shard), BF),
            pltpu.VMEM((count - 1, packed, 2 * shard), BF),
            pltpu.VMEM((2, packed, width // 4), BF),
            pltpu.VMEM((packed, tokens), BF),
            pltpu.VMEM((group, width), F32),
            pltpu.VMEM((group, width), F32),
            pltpu.VMEM((group, width), BF),
            pltpu.VMEM((24, width), F32),
            pltpu.VMEM((3, 8, width), F32),
            pltpu.VMEM((count, 8, width), F32),
            pltpu.VMEM((8, width), F32),
            pltpu.VMEM((8, tokens), F32),
            dma((12,)),
            dma((3 * SLICES,)),
            dma((2,)),
            dma((1 + items,)),
            dma((1 + items,)),
            dma((1 + items, 2, count - 1)),
            dma((1 + items, 2, count - 1)),
            dma((4, 3, 8)),
            dma((4, 3, 8)),
            dma((4, 7)),
            dma((4, 7)),
            dma((2, 3)),
            dma((2, 3)),
            dma((3,)),
            dma((3,)),
            dma((2, count - 1)),
            dma((2, count - 1)),
            pltpu.SemaphoreType.REGULAR((2,)),
            dma((4,)),
            dma((4,)),
            dma((4,)),
            dma((SLICES, 2)),
            dma((SLICES, 2)),
            dma((2 + items, 2, count - 1)),
            dma((2 + items, 2, count - 1)),
            dma((5,)),
            dma((SLICES, 2)),
            dma((4,)),
        ],
        compiler_params=pltpu.CompilerParams(
            vmem_limit_bytes=VMEM_LIMIT, collective_id=0, has_side_effects=True
        ),
        name="layer",
    )(block_input, out_grad, gains, table, marks, *masters)


def adamw(weight, gradient, first, second, rate, decay):
    first_new = BETA_ONE * first + (1.0 - BETA_ONE) * gradient
    second_new = BETA_TWO * second + (1.0 - BETA_TWO) * gradient * gradient
    bias_first = 1.0 - BETA_ONE**STEP
    bias_second = 1.0 - BETA_TWO**STEP
    moved = first_new * (1.0 / bias_first) / (jnp.sqrt(second_new * (1.0 / bias_second)) + ADAM_EPS)
    return (weight - rate * (moved + decay * weight), first_new, second_new)


def update_kernel(attention_cuts, forward_cuts, *refs):
    a, f = 12, 9
    attention_share, forward_share, block_in, gradient_in = refs[:4]
    states, outs = refs[4 : 4 + a + f], refs[4 + a + f :]
    outs[0][...] = block_in[...]
    outs[1][...] = gradient_in[...].astype(F32)

    def one(gradient, arrays, results, at):
        fresh = adamw(arrays[0][at], gradient, arrays[1][at], arrays[2][at], RATE_MATRIX, DECAY)
        for result, value in zip(results, fresh):
            result[at] = value

    everything = (slice(None), slice(None))
    for i in range(3):
        gradient = forward_share[forward_cuts[i] : forward_cuts[i + 1], :].astype(F32)
        one(gradient if i == 2 else gradient.T, states[a + i :: 3][:3], outs[2 + a + i :: 3][:3], everything)

    @pl.when(pl.program_id(0) == 0)
    def _():
        for i in range(4):
            for side in range(2):
                low, high = attention_cuts[i], attention_cuts[i + 1]
                gradient = attention_share[side, low:high, :].astype(F32)
                span = slice(side * (high - low), (side + 1) * (high - low))
                if i == 3:
                    one(gradient, states[i:a:4], outs[2 + i : 2 + a : 4], (span, slice(None)))
                else:
                    one(gradient.T, states[i:a:4], outs[2 + i : 2 + a : 4], (slice(None), span))


def update(shares, block_output, input_gradient, attention_cuts, attention, forward_cuts, feed):
    packed, part = shares.shape[2:]
    steps = 2 * SLICES

    def rows_block(array):
        return pl.BlockSpec((array.shape[0] // steps, array.shape[1]), lambda g: (g, 0))

    def columns_block(array):
        return pl.BlockSpec((array.shape[0], array.shape[1] // steps), lambda g: (0, g))

    state_specs = [pl.BlockSpec(array.shape, lambda g: (0, 0)) for array in attention]
    state_specs += [rows_block(array) if i % 3 == 2 else columns_block(array) for i, array in enumerate(feed)]
    plain = [rows_block(block_output), rows_block(input_gradient)]
    return pl.pallas_call(
        functools.partial(update_kernel, attention_cuts, forward_cuts),
        grid=(steps,),
        in_specs=[
            pl.BlockSpec((2, None, packed, part), lambda g: (0, SLICES, 0, 0)),
            pl.BlockSpec((None, None, packed, part), lambda g: (g // SLICES, g % SLICES, 0, 0)),
        ]
        + plain
        + state_specs,
        out_specs=plain + state_specs,
        out_shape=[
            jax.ShapeDtypeStruct(block_output.shape, BF),
            jax.ShapeDtypeStruct(input_gradient.shape, F32),
        ]
        + [jax.ShapeDtypeStruct(array.shape, F32) for array in (*attention, *feed)],
        compiler_params=pltpu.CompilerParams(vmem_limit_bytes=VMEM_LIMIT),
        name="update",
    )(shares, shares, block_output, input_gradient, *attention, *feed)


def rotary_tables(positions):
    half = HEAD_SIZE // 2
    frequency = THETA ** (-2.0 * jnp.arange(half, dtype=F32) / HEAD_SIZE)
    angles = positions.astype(F32)[:, None] * frequency[None, :]
    cosine, sine = jnp.cos(angles), jnp.sin(angles)
    return jnp.concatenate([cosine, sine], -1)


def local(
    block_input, out_grad, segments, positions,
    w_query, w_key, w_value, w_output, w_gate, w_up, w_down, gains,
    m_query, m_key, m_value, m_output, m_gate, m_up, m_down, m_gains,
    v_query, v_key, v_value, v_output, v_gate, v_up, v_down, v_gains,
):
    half_tokens = block_input.shape[0]
    rows = w_query.shape[0]
    sequences = lax.axis_size("dp") // 2
    half = lax.axis_index("dp") % 2
    table = rotary_tables(positions)
    marks = jnp.broadcast_to(segments.astype(F32)[None, :], (8, half_tokens))
    gain_rows = jnp.pad(gains.astype(BF).astype(F32), ((0, 6), (0, 0)))
    masters = (w_query, w_key, w_value, w_output, w_gate, w_up, w_down)
    block_output, input_gradient, shares, gain_grads = layer(
        block_input, out_grad, gain_rows, table, marks, masters, sequences
    )[:4]
    if shares.shape[-1] != rows:
        shares = lax.dynamic_slice_in_dim(shares, half * rows, rows, 3)
    q_cols, k_cols, o_cols = w_query.shape[1] // 2, w_key.shape[1] // 2, w_output.shape[0] // 2
    slice_cols = w_gate.shape[1] // 2 // SLICES

    def cuts(*sizes):
        return [sum(sizes[:i]) for i in range(len(sizes) + 1)]

    block_output, input_gradient, *fresh = update(
        shares, block_output, input_gradient,
        cuts(q_cols, k_cols, k_cols, o_cols),
        (w_query, w_key, w_value, w_output, m_query, m_key, m_value, m_output, v_query, v_key, v_value, v_output),
        cuts(slice_cols, slice_cols, slice_cols),
        (w_gate, w_up, w_down, m_gate, m_up, m_down, v_gate, v_up, v_down),
    )
    attention_new, forward_new = fresh[:12], fresh[12:]
    gain_grads = lax.dynamic_slice_in_dim(gain_grads[:2], half * rows, rows, 1)
    gains_new = adamw(gains, gain_grads, m_gains, v_gains, RATE_GAIN, 0.0)
    new = [
        list(attention_new[4 * part : 4 * part + 4]) + list(forward_new[3 * part : 3 * part + 3]) + [gains_new[part]]
        for part in range(3)
    ]
    return tuple([block_output, input_gradient] + new[0] + new[1] + new[2])


def solution(mesh):
    matrices = [P("dp", "tensor")] * 3 + [P("tensor", "dp")] + [P("dp", "tensor")] * 2 + [P("tensor", "dp")]
    state = tuple(matrices + [P(None, "dp")])
    rows = (P("dp", None), P("dp", None))
    return jax.shard_map(
        local,
        mesh=mesh,
        in_specs=rows + (P("dp"), P("dp")) + state * 3,
        out_specs=rows + state * 3,
        check_vma=False,
    )
```

```python
import functools
import math

import jax
import jax.numpy as jnp
from jax import lax
from jax.experimental import pallas as pl
from jax.experimental.pallas import tpu as pltpu
from jax.sharding import PartitionSpec as P

HEAD_SIZE = 128
WINDOW = 1024
STEP = 5
EPS = 1e-06
THETA = 1000000.0
BETA_ONE = 0.5
BETA_TWO = 0.5
RATE_MATRIX = 0.02
RATE_GAIN = 0.3
DECAY = 0.1
ADAM_EPS = 1e-08
NEGATIVE = -1e30
SLICES = 4
BF = jnp.bfloat16
F32 = jnp.float32
VMEM_LIMIT = 63 * 1024 * 1024
MESH = pl.DeviceIdType.MESH


class Place:
    def __init__(self, sequences):
        self.count = sequences
        self.locate()

    def locate(self):
        self.dp, self.tensor = lax.axis_index("dp"), lax.axis_index("tensor")
        self.sequence, self.half = self.dp // 2, self.dp % 2
        self.y, self.core = self.tensor // 2, self.tensor % 2
        across = 1 - 2 * self.half
        beside = 2 - 4 * self.y
        self.partner = {
            "core": (self.dp, self.tensor + 1 - 2 * self.core),
            "x": (self.dp + across, self.tensor),
            "y": (self.dp, self.tensor + beside),
            "first": (self.dp + (1 - self.core) * across, self.tensor + self.core * beside),
            "second": (self.dp + self.core * across, self.tensor + (1 - self.core) * beside),
            "right": (self.dp + 2, self.tensor),
            "left": (self.dp - 2, self.tensor),
        }

    def of_group(self, g):
        dh = (g // 4 + self.half) % 2
        dy = ((g // 2) % 2 + self.y) % 2
        dc = (g % 2 + self.core) % 2
        from_core = (self.core + dc) % 2
        straight = dh * 2 + dy
        return dc * 4 + straight + from_core * (dy * 2 + dh - straight)

    def greet(self):
        barrier = pltpu.get_barrier_semaphore()
        for name in ("core", "x", "y"):
            pl.semaphore_signal(barrier, inc=1, device_id=self.partner[name], device_id_type=MESH)

        @pl.when(self.sequence >= 1)
        def _():
            pl.semaphore_signal(barrier, inc=1, device_id=self.partner["left"], device_id_type=MESH)

        @pl.when(self.sequence <= self.count - 2)
        def _():
            pl.semaphore_signal(barrier, inc=1, device_id=self.partner["right"], device_id_type=MESH)

        ends = (self.sequence + self.count - 1) // self.count + (2 * self.count - 2 - self.sequence) // self.count
        pl.semaphore_wait(barrier, 3 + ends)

    def copy(self, source, target, send, recv, name):
        return pltpu.make_async_remote_copy(
            src_ref=source, dst_ref=target, send_sem=send, recv_sem=recv,
            device_id=self.partner[name], device_id_type=MESH,
        )


class Gather:
    moves = [("second", 0, 1), ("first", 0, 2), ("first", 1, 3)] + [("core", p, p + 4) for p in range(4)]

    def __init__(self, place, buffer, group, send, recv, own=None):
        self.place, self.buffer, self.group = place, buffer, group
        self.send, self.recv, self.own = send, recv, own

    def at(self, index):
        return self.buffer.at[pl.ds(index * self.group, self.group)]

    def copy(self, index):
        name, source, target = self.moves[index]
        source = self.own if self.own is not None and source == 0 else self.at(source)
        return self.place.copy(source, self.at(target), self.send.at[index], self.recv.at[index], name)

    def start(self):
        for index in (0, 1, 3):
            self.copy(index).start()

    def step(self, index):
        if index == 1:
            self.copy(0).wait_recv()
            self.copy(2).start()
            self.copy(4).start()
        else:
            self.copy(index - 1).wait_recv()
            self.copy(index + 3).start()

    def arrived(self, index):
        self.copy(3 + index).wait_recv()

    def sent(self):
        for index in range(7):
            self.copy(index).wait_send()


class Line:
    def __init__(self, place, slot, send, recv):
        self.place, self.slot = place, slot
        self.sends, self.recvs = send, recv

    def move(self, way, stage):
        place = self.place
        shard = place.sequence - stage if way == 0 else place.sequence + stage
        target = self.slot(shard)
        name = "right" if way == 0 else "left"
        return place.copy(target, target, self.sends.at[way, stage], self.recvs.at[way, stage], name)

    def conditions(self, stage):
        place = self.place
        last = place.count - 1
        sends = (
            (place.sequence >= stage) & (place.sequence <= last - 1),
            (place.sequence <= last - stage) & (place.sequence >= 1),
        )
        recvs = (place.sequence >= stage + 1, place.sequence <= last - 1 - stage)
        return sends, recvs

    def start(self, stage):
        for way, condition in enumerate(self.conditions(stage)[0]):
            @pl.when(condition)
            def _(way=way):
                self.move(way, stage).start()

    def arrived(self, stage):
        for way, condition in enumerate(self.conditions(stage)[1]):
            @pl.when(condition)
            def _(way=way):
                place = self.place
                shard = place.sequence - 1 - stage if way == 0 else place.sequence + 1 + stage
                target = self.slot(shard)
                place.copy(
                    target, target, self.sends.at[way, stage], self.recvs.at[way, stage],
                    "right" if way == 0 else "left",
                ).wait_recv()

    def sent(self, stage):
        for way, condition in enumerate(self.conditions(stage)[0]):
            @pl.when(condition)
            def _(way=way):
                self.move(way, stage).wait_send()


def turn(head, cosine, sine):
    return head * cosine + pltpu.roll(head, HEAD_SIZE // 2, 1) * sine


def key_range(block_at, block):
    low = max(0, block_at * block - WINDOW + 1) // block * block
    return low, (block_at + 1) * block


def allowed_pairs(segment_rows, segment_columns, block_at, block):
    low, high = key_range(block_at, block)
    shape = (block, high - low)
    distance = (
        lax.broadcasted_iota(jnp.int32, shape, 0)
        - lax.broadcasted_iota(jnp.int32, shape, 1)
        + (block_at * block - low)
    )
    same = segment_rows[block_at * block : high, 0:1] == segment_columns[0:1, low:high]
    return same & (distance >= 0) & (distance < WINDOW)


NT = (((1,), (1,)), ((), ()))
TN = (((0,), (0,)), ((), ()))


def rows_at(index, size):
    return pl.ds(pl.multiple_of(index * size, size), size)


def group_at(place, p):
    dc = p // 4
    from_core = (place.core + dc) % 2
    one, two = (p // 2) % 2, p % 2
    dh = one + from_core * (two - one)
    dy = two + from_core * (one - two)
    return ((dh + place.half) % 2) * 4 + ((dy + place.y) % 2) * 2 + (dc + place.core) % 2


def attend_blocks(place, heads, q_cols, k_cols, aux, columns_ref, between):
    block = heads.shape[0] // 8
    qkv_cols = q_cols + 2 * k_cols
    scale = 1.0 / math.sqrt(HEAD_SIZE)
    for at in range(8):
        low, high = key_range(at, block)
        allowed = allowed_pairs(aux, columns_ref, at, block)
        keys, values = heads[low:high, q_cols : q_cols + k_cols], heads[low:high, q_cols + k_cols : qkv_cols]
        to = rows_at(place.of_group(at), block)
        for head in range(q_cols // HEAD_SIZE):
            columns = slice(head * HEAD_SIZE, (head + 1) * HEAD_SIZE)
            rows = heads[at * block : high, columns]
            scores = lax.dot_general(rows, keys, NT, preferred_element_type=F32) * scale
            scores = jnp.where(allowed, scores, NEGATIVE)
            top = jnp.max(scores, -1, keepdims=True)
            weights = jnp.exp(scores - top)
            total = jnp.sum(weights, -1, keepdims=True)
            probs = (weights * (1.0 / total)).astype(BF)
            heads[to, qkv_cols + columns.start : qkv_cols + columns.stop] = jnp.dot(
                probs, values, preferred_element_type=F32
            ).astype(BF)
            aux[at * block : high, 1 + head : 2 + head] = top + jnp.log(total)
        between(at)


class LineSum:
    def __init__(self, place, item, rows, index, own, recv, loads, ring, send_sem, recv_sem, load_sem, before):
        self.place, self.item, self.index, self.own, self.recv = place, item, index, own, recv
        self.rows = pl.ds(*rows)
        self.loads, self.ring = loads.at[:, self.rows], ring.at[:, self.rows]
        self.send_sem, self.recv_sem, self.load_sem = send_sem, recv_sem, load_sem
        self.before = before
        self.width = recv.shape[-1]

    def own_part(self, d):
        return self.own.at[self.item, self.rows, pl.ds(pl.multiple_of(d * self.width, self.width), self.width)]

    def dest(self, way, j):
        return self.place.count - 1 - j if way == 0 else j

    def move(self, way, j, source):
        return self.place.copy(
            source, self.recv.at[self.item, way, j, self.rows],
            self.send_sem.at[self.index, way, j], self.recv_sem.at[self.index, way, j],
            "right" if way == 0 else "left",
        )

    def start(self):
        last = self.place.count - 1
        for way, end in ((0, 0), (1, last)):
            @pl.when(self.place.sequence == end)
            def _(way=way):
                for j in range(last):
                    self.move(way, j, self.own_part(self.dest(way, j))).start()

    def turn_of(self, way, stage):
        depth = self.place.sequence if way == 0 else self.place.count - 1 - self.place.sequence
        return (depth >= 1) & (depth <= stage - 1), stage - 1 - depth, depth

    def slot(self, way, j):
        return j if way == 0 else self.place.count - 1 - self.place.sequence + j

    def own_load(self, way, d):
        return pltpu.make_async_copy(self.own_part(d), self.loads.at[2 * way], self.load_sem.at[2 * way])

    def came_load(self, way, j):
        return pltpu.make_async_copy(
            self.recv.at[self.item, way, j, self.rows], self.loads.at[2 * way + 1], self.load_sem.at[2 * way + 1]
        )

    def prepare(self, stage):
        for way in (0, 1):
            condition, j, _ = self.turn_of(way, stage)

            @pl.when(condition)
            def _(way=way, j=j):
                self.own_load(way, self.dest(way, j)).start()
                self.move(way, j, self.ring.at[self.slot(way, j)]).wait_recv()
                self.came_load(way, j).start()

    def service(self, stage):
        for way in (0, 1):
            condition, j, _ = self.turn_of(way, stage)

            @pl.when(condition)
            def _(way=way, j=j):
                slot = self.slot(way, j)
                if self.before is not None:
                    self.before.move(way, j, self.before.ring.at[slot]).wait_send()
                self.own_load(way, self.dest(way, j)).wait()
                self.came_load(way, j).wait()
                self.ring[slot] = (self.loads[2 * way].astype(F32) + self.loads[2 * way + 1].astype(F32)).astype(BF)
                self.move(way, j, self.ring.at[slot]).start()

    def last(self, way):
        place = self.place
        if way == 0:
            return place.sequence >= 1, place.count - 1 - place.sequence
        return place.sequence <= place.count - 2, place.sequence

    def prepare_total(self):
        self.own_load(0, self.place.sequence).start()
        for way in (0, 1):
            condition, j = self.last(way)

            @pl.when(condition)
            def _(way=way, j=j):
                self.move(way, j, self.loads.at[2 * way + 1]).wait_recv()
                self.came_load(way, j).start()

            @pl.when(jnp.logical_not(condition))
            def _(way=way):
                self.loads[2 * way + 1] = jnp.zeros(self.loads.shape[1:], BF)

    def total(self, out):
        self.own_load(0, self.place.sequence).wait()
        for way in (0, 1):
            condition, j = self.last(way)

            @pl.when(condition)
            def _(way=way, j=j):
                self.came_load(way, j).wait()

        out[...] = (
            self.loads[0].astype(F32) + self.loads[1].astype(F32) + self.loads[3].astype(F32)
        ).astype(BF)

    def sent(self, last_item):
        last = self.place.count - 1
        for way, end in ((0, 0), (1, last)):
            @pl.when(self.place.sequence == end)
            def _(way=way):
                for j in range(last):
                    self.move(way, j, self.own_part(self.dest(way, j))).wait_send()

        if last_item:
            for stage in range(2, last + 1):
                for way in (0, 1):
                    condition, j, _ = self.turn_of(way, stage)

                    @pl.when(condition)
                    def _(way=way, j=j):
                        self.move(way, j, self.ring.at[self.slot(way, j)]).wait_send()


class PlaneSum:
    def __init__(self, place, part, own, got, send_sem, recv_sem, chunk):
        self.place, self.part, self.own, self.got = place, part, own, got
        self.send_sem, self.recv_sem, self.chunk = send_sem, recv_sem, chunk
        self.group = own.shape[0]

    def columns(self, c):
        return pl.ds(c * self.chunk, self.chunk)

    def move(self, step, c):
        group, columns = self.group, self.columns(c)
        rows = ((4, 4), (2, 2), (1, 1))[step]
        name = ("core", "first", "second")[step]
        return self.place.copy(
            self.part.at[pl.ds(rows[0] * group, rows[1] * group), columns], self.got[step].at[:, columns],
            self.send_sem.at[step, c], self.recv_sem.at[step, c], name,
        )

    def push(self, c):
        self.move(0, c).start()

    def middle(self, c):
        self.move(0, c).wait_recv()
        rows, columns = pl.ds(2 * self.group, 2 * self.group), self.columns(c)
        self.part[rows, columns] = (
            self.part[rows, columns].astype(F32) + self.got[0][rows, columns].astype(F32)
        ).astype(BF)
        self.move(1, c).start()

    def late(self, c):
        self.move(1, c).wait_recv()
        rows, columns = pl.ds(self.group, self.group), self.columns(c)
        self.part[rows, columns] = (
            self.part[rows, columns].astype(F32)
            + self.got[0][rows, columns].astype(F32)
            + self.got[1][rows, columns].astype(F32)
        ).astype(BF)
        self.move(2, c).start()

    def total(self, c):
        self.move(2, c).wait_recv()
        rows, columns = pl.ds(0, self.group), self.columns(c)
        self.own[:, columns] = (
            self.own[:, columns]
            + self.got[0][rows, columns].astype(F32)
            + self.got[1][rows, columns].astype(F32)
            + self.got[2][:, columns].astype(F32)
        )

    def sent(self, c):
        for step in range(3):
            self.move(step, c).wait_send()


class HalfGather:
    def __init__(self, place, own, buffer, send, recv, local):
        self.place = place
        group = own.shape[0]
        tensor, across = place.tensor, place.tensor + 2 - 4 * place.y

        def at(index):
            return buffer.at[rows_at(index, group)]

        self.keep = pltpu.make_async_copy(own, at(tensor), local)
        self.y = place.copy(own, at(tensor), send.at[0], recv.at[0], "y")
        self.core = place.copy(own, at(tensor), send.at[1], recv.at[1], "core")
        self.far = place.copy(at(across), at(across), send.at[2], recv.at[2], "core")

    def start(self):
        self.keep.start()
        self.y.start()
        self.core.start()

    def step(self):
        self.y.wait_recv()
        self.far.start()

    def end(self):
        self.keep.wait()
        self.y.wait_send()
        self.core.wait()
        self.far.wait()


def layer_kernel(
    count, gains_here,
    block_input, out_grad, gains, table_half, marks_half,
    w_query, w_key, w_value, w_output, w_gate, w_up, w_down,
    block_output, input_gradient, shares, gain_out,
    own_grads, line_got, totals, w_attention, w_forward, normed_out, heads_out, table_out, aux_out,
    second, grad, both, wide, got_core, got_first, got_second, loads, ring, ready, turned,
    one, two, own_rows, small_own, small_got, small_all, gain_ref, marks_ref,
    load_sem, wide_sem, ready_sem, swap_send, swap_recv, line_send, line_recv, sum_send, sum_recv,
    gather_send, gather_recv, half_send, half_recv, small_send, small_recv, gain_send, gain_recv, free_sem,
    line_load_sem, owner_sem, early_send, early_recv, slice_send, slice_recv, shard_send, shard_recv, master_sem, keep_sem, out_sem,
):
    place = Place(count)
    group, width = own_rows.shape
    tokens = 8 * group
    packed = wide.shape[1]
    slice_cols = packed // 3
    pair = 2 * slice_cols
    shard = w_query.shape[0]
    q_cols, k_cols = w_query.shape[1] // 2, w_key.shape[1] // 2
    qkv_cols = q_cols + 2 * k_cols
    shard2 = line_got.shape[-1]
    part_width = shares.shape[-1]
    chunk = width // 8
    big = width // 4
    block = 2 * group
    got = (got_core, got_first, got_second)

    def load_wide(source, index):
        return pltpu.make_async_copy(source, wide, wide_sem.at[index])

    def shard_rows():
        return pl.ds(pl.multiple_of(place.dp * shard, shard), shard)

    def sequence_rows(k):
        return pl.ds(pl.multiple_of(k * 2 * shard, 2 * shard), 2 * shard)

    local = pltpu.make_async_copy

    masters = [
        local(w_query, one.at[pl.ds(0, shard), pl.ds(0, 2 * q_cols)], master_sem.at[0]),
        local(w_key, one.at[pl.ds(0, shard), pl.ds(2 * q_cols, 2 * k_cols)], master_sem.at[1]),
        local(w_value, one.at[pl.ds(0, shard), pl.ds(2 * q_cols + 2 * k_cols, 2 * k_cols)], master_sem.at[2]),
    ]
    own_loads = [
        local(block_input.at[rows_at(place.tensor, group)], both.at[pl.ds(0, group)], load_sem.at[2]),
        local(out_grad.at[rows_at(place.tensor, group)], grad.at[pl.ds(0, group)], load_sem.at[3]),
    ]
    table_keep = local(table_half, table_out.at[rows_at(place.half, 4 * group)], load_sem.at[4])
    for copy in masters + own_loads + [table_keep]:
        copy.start()
    marks_ref[:, rows_at(place.half, 4 * group)] = marks_half[...]

    def early(index):
        columns = rows_at(place.half, 4 * group)
        source, target = (
            (own_rows.at[pl.ds(0, shard), pl.ds(0, packed)], wide.at[shard_rows()]),
            (marks_half, marks_ref.at[:, columns]),
            (table_half, table_out.at[columns]),
            (gains, gain_ref.at[:, shard_rows()] if gains_here else None),
        )[index]
        return place.copy(source, target, early_send.at[index], early_recv.at[index], "x")

    def unit(s, theirs, part):
        k = 2 * s + theirs
        if part == 0:
            return pl.ds((k // 4) * slice_cols, shard), pl.ds((k % 4) * pair, pair)
        return pl.ds(pair, shard), pl.ds(k * slice_cols, slice_cols)

    def slice_target(s, part):
        return w_forward.at[s, shard_rows(), pl.ds(0, pair) if part == 0 else pl.ds(pair, slice_cols)]

    def slice_swap(s, part):
        return place.copy(
            turned.at[unit(s, 1, part)], slice_target(s, part), slice_send.at[s, part], slice_recv.at[s, part], "x"
        )

    def slice_keep(s, part):
        return local(turned.at[unit(s, 0, part)], slice_target(s, part), keep_sem.at[s, part])

    lines = [
        Line(
            place, lambda k: wide.at[sequence_rows(k), pl.ds(0, qkv_cols)], shard_send.at[0], shard_recv.at[0]
        )
    ] + [
        Line(
            place, lambda k, s=s: w_forward.at[s, sequence_rows(k)], shard_send.at[1 + s], shard_recv.at[1 + s]
        )
        for s in range(SLICES)
    ]
    output_line = Line(
        place, lambda k: wide.at[sequence_rows(k), pl.ds(qkv_cols, q_cols)],
        shard_send.at[2 + SLICES], shard_recv.at[2 + SLICES],
    )

    def output_steps(first, last):
        for stage in range(min(first, count - 1), min(last, count - 1)):
            output_line.arrived(stage)
            if stage < count - 2:
                output_line.start(stage + 1)

    gain_shards = Line(
        place, lambda k: gain_ref.at[:, sequence_rows(k)], shard_send.at[1 + SLICES], shard_recv.at[1 + SLICES]
    )

    begin = (0, 1, 2 * count - 4, 3 * count - 6.5)
    sends = sorted(
        ((s, stage) for s in range(SLICES) for stage in range(count - 1)),
        key=lambda item: (begin[item[0]] + 2 * item[1] + (item[1] > 0) * (item[0] >= 2) * 2, item[0]),
    )

    def advance(number):
        for _ in range(min(number, len(sends))):
            s, stage = sends.pop(0)
            if stage == 0:
                for part in range(2):
                    slice_swap(s, part).wait_recv()
            else:
                lines[1 + s].arrived(stage - 1)
            lines[1 + s].start(stage)

    def advance_through(s):
        while any(item[0] == s for item in sends):
            advance(1)

    place.greet()

    def attention_shard(output, target, rows, side):
        target[rows, :q_cols] = one[:shard, rows_at(side, q_cols)].astype(BF)
        for index in range(2):
            base = 2 * q_cols + 2 * k_cols * index
            target[rows, q_cols + k_cols * index : q_cols + k_cols * (index + 1)] = one[
                :shard, pl.ds(pl.multiple_of(base + side * k_cols, k_cols), k_cols)
            ].astype(BF)
        target[rows, qkv_cols:packed] = output[rows_at(side, q_cols), :].T.astype(BF)

    def fill_attention(output):
        place.locate()
        output_load = local(w_output, output, master_sem.at[3])
        output_load.start()
        for copy in masters + [output_load]:
            copy.wait()
        attention_shard(output, own_rows, slice(0, shard), 1 - place.half)
        early(0).start()
        attention_shard(output, wide, shard_rows(), place.half)

    pl.run_scoped(fill_attention, pltpu.VMEM(w_output.shape, F32))
    place.locate()
    masters = [
        local(w_gate, one.at[pl.ds(0, shard)], master_sem.at[0]),
        local(w_up, two.at[pl.ds(0, shard)], master_sem.at[1]),
    ]
    for copy in masters:
        copy.start()
    early(1).start()
    if gains_here:
        gain_ref[:, shard_rows()] = gains[...]
        early(3).start()
    else:
        gain_ref[...] = gains[...]
    inputs = Gather(place, both, group, gather_send.at[0], gather_recv.at[0])
    own_loads[0].wait()
    inputs.start()
    early(0).wait_recv()
    lines[0].start(0)
    if gains_here:
        early(3).wait_recv()
        gain_shards.start(0)

    def fill_slices(down):
        place.locate()
        down_load = local(w_down, down, master_sem.at[2])
        down_load.start()
        for copy in masters + [down_load]:
            copy.wait()
        for s in range(SLICES):
            for theirs in (1, 0):
                side = place.half + theirs - 2 * theirs * place.half
                columns = rows_at(side * SLICES + s, slice_cols)
                (rows, at), (down_rows, down_at) = unit(s, theirs, 0), unit(s, theirs, 1)
                turned[rows, pl.ds(at.start, slice_cols)] = one[:shard, columns].astype(BF)
                turned[rows, pl.ds(at.start + slice_cols, slice_cols)] = two[:shard, columns].astype(BF)
                turned[down_rows, down_at] = down[columns, :].T.astype(BF)
            for part in range(2):
                slice_keep(s, part).start()
            if s == 0:
                inputs.step(1)

    pl.run_scoped(fill_slices, pltpu.VMEM(w_down.shape, F32))
    place.locate()
    if gains_here:
        for stage in range(count - 1):
            gain_shards.arrived(stage)
            if stage < count - 2:
                gain_shards.start(stage + 1)
    lines[0].arrived(0)
    if count > 2:
        lines[0].start(1)

    def start_swap(s):
        for part in range(2):
            slice_swap(s, part).start()

    inputs.step(2)
    inputs.step(3)
    start_swap(0)
    start_swap(1)
    early(2).start()

    def norm_block(p, _):
        rows = rows_at(p, group)
        x = both[rows, :].astype(F32)
        factor = lax.rsqrt(jnp.mean(x * x, -1, keepdims=True) + EPS)
        second[rows, :] = (x * factor * gain_ref[0:1, :]).astype(BF)
        return 0

    lax.fori_loop(0, 4, norm_block, 0)
    for stage in range(1, count - 1):
        lines[0].arrived(stage)
        if stage < count - 2:
            lines[0].start(stage + 1)
    for p in range(4):
        inputs.arrived(p)
    lax.fori_loop(4, 8, norm_block, 0)
    for s in range(SLICES):
        for part in range(2):
            slice_keep(s, part).wait()
    output_line.start(0)
    grads = Gather(place, grad, group, gather_send.at[2], gather_recv.at[2])
    own_loads[1].wait()
    grads.start()
    start_swap(2)
    normed_copy = local(second, normed_out, out_sem.at[0])
    wide_copy = local(wide, w_attention, out_sem.at[1])
    normed_copy.start()
    mixed = PlaneSum(place, both, two, got, sum_send.at[0], sum_recv.at[0], chunk)

    def attention_forward(heads, table, aux):
        place.locate()
        table_keep.wait()
        early(2).wait_recv()
        table_load = local(table_out, table, load_sem.at[4])
        table_load.start()
        aux[...] = jnp.zeros_like(aux)
        early(1).wait_recv()
        tile = (HEAD_SIZE, HEAD_SIZE)
        diagonal = lax.broadcasted_iota(jnp.int32, tile, 0) == lax.broadcasted_iota(jnp.int32, tile, 1)
        for at in range(0, tokens, HEAD_SIZE):
            aux[at : at + HEAD_SIZE, 0:1] = jnp.sum(
                jnp.where(diagonal, marks_ref[0:1, at : at + HEAD_SIZE], 0.0), -1, keepdims=True
            )
        table_load.wait()

        def project_block(p, _):
            out = jnp.dot(second[rows_at(p, group), :], wide[:, :qkv_cols], preferred_element_type=F32)
            to = rows_at(group_at(place, p), group)
            cosine, sine = rotation(table[to, :])
            for at in range(0, q_cols + k_cols, HEAD_SIZE):
                heads[to, at : at + HEAD_SIZE] = turn(out[:, at : at + HEAD_SIZE], cosine, sine).astype(BF)
            heads[to, q_cols + k_cols : qkv_cols] = out[:, q_cols + k_cols :].astype(BF)
            return 0

        lax.fori_loop(0, 8, project_block, 0)
        output_steps(0, 1)
        advance(1)
        grads.step(1)

        def between(at):
            if at == 2:
                output_steps(1, 2)
            if at == 3:
                advance(1)
            if at == 5:
                output_steps(2, count)
            if at == 6:
                advance(1)

        attend_blocks(place, heads, q_cols, k_cols, aux, marks_ref, between)
        wide_copy.start()
        heads_copy = local(heads, heads_out, out_sem.at[2])
        aux_copy = local(aux, aux_out, out_sem.at[3])
        heads_copy.start()
        aux_copy.start()
        inputs.sent()
        normed_copy.wait()

        for c in range(8):
            columns = pl.ds(c * chunk, chunk)

            def mixed_part(rows, c=c):
                return lax.dot_general(
                    heads[rows, qkv_cols:], wide[c * chunk : (c + 1) * chunk, qkv_cols:], NT,
                    preferred_element_type=F32,
                )

            def mixed_rows(b, _, columns=columns, mixed_part=mixed_part):
                rows = rows_at(b, block)
                both[rows, columns] = mixed_part(rows).astype(BF)
                return 0

            first = mixed_part(pl.ds(0, block))
            two[:, columns] = first[:group]
            both[pl.ds(group, group), columns] = first[group:].astype(BF)
            lax.fori_loop(1, 4, mixed_rows, 0)
            mixed.push(c)
            if c >= 1:
                mixed.middle(c - 1)
            if c >= 3:
                mixed.late(c - 3)
            if c >= 5:
                mixed.total(c - 5)
            if c == 2:
                advance(1)
            if c == 3:
                grads.step(2)
            if c == 4:
                grads.step(3)
            if c == 5:
                advance(1)
        heads_copy.wait()
        aux_copy.wait()

    pl.run_scoped(
        attention_forward,
        pltpu.VMEM((tokens, packed), BF), pltpu.VMEM((tokens, HEAD_SIZE), F32), pltpu.VMEM((tokens, HEAD_SIZE), F32),
    )
    place.locate()
    mixed.middle(7)
    mixed.late(5)
    advance(1)
    mixed.total(3)
    for c in (6, 7):
        mixed.late(c)
        mixed.total(c - 2)
    mixed.total(6)
    mixed.total(7)
    early(0).wait_send()

    def by_rows(step):
        def some(b, _):
            step(rows_at(b, group // 4))
            return 0

        lax.fori_loop(0, 4, some, 0)

    def residual_step(rows):
        residual = two[rows, :] + both[rows, :].astype(F32)
        two[rows, :] = residual
        factor = lax.rsqrt(jnp.mean(residual * residual, -1, keepdims=True) + EPS)
        normal = (residual * factor * gain_ref[1:2, :]).astype(BF)
        own_rows[rows, :] = normal
        second[rows, :] = normal

    by_rows(residual_step)
    seconds = Gather(place, second, group, gather_send.at[1], gather_recv.at[1], own_rows)
    seconds.start()
    start_swap(3)
    advance(1)
    seconds.step(1)
    advance(1)
    wide_copy.wait()
    for stage in range(count - 1):
        lines[0].sent(stage)
        output_line.sent(stage)
    for c in range(8):
        mixed.sent(c)
    for s in range(SLICES):
        for part in range(2):
            if s < SLICES - 1:
                slice_swap(s, part).wait_send()
    seconds.step(2)
    seconds.step(3)
    for part in range(2):
        slice_swap(SLICES - 1, part).wait_send()
    for p in range(4):
        grads.arrived(p)
    advance(1)
    for p in range(4):
        seconds.arrived(p)
    seconds.sent()
    grads.sent()

    sums = []
    sum_items = [(s, 0, packed) for s in range(SLICES)]
    sum_items += [(SLICES, qkv_cols, q_cols), (SLICES, 0, qkv_cols)]
    for index, (item, low, size) in enumerate(sum_items):
        sums.append(
            LineSum(
                place, item, (low, size), index, own_grads, line_got, loads, ring, line_send, line_recv, line_load_sem,
                sums[-1] if sums else None,
            )
        )

    pending = {0: [], 1: []}
    turn_at = [0]

    def next_ready():
        slot = turn_at[0] % 2
        turn_at[0] += 1
        for wait in pending[slot]:
            wait()
        pending[slot] = []
        return slot

    def flush():
        for slot in (0, 1):
            for wait in pending[slot]:
                wait()
            pending[slot] = []

    def finish(index):
        item, low, size = sum_items[index]
        slot = next_ready()
        rows = pl.ds(low, size)
        sums[index].total(ready.at[slot, rows, pl.ds(0, shard2)])

        def copy():
            return pltpu.make_async_copy(
                ready.at[slot, rows, pl.ds(0, shard2)], totals.at[item, rows], ready_sem.at[slot]
            )

        copy().start()
        pending[slot].append(lambda: copy().wait())

    def owner_moves(index):
        item, low, size = sum_items[index]
        rows = pl.ds(low, size)
        if part_width == shard2:
            mine = theirs = totals.at[item, rows]
        else:
            mine, theirs = [
                totals.at[item, rows, pl.ds(pl.multiple_of(side * part_width, part_width), part_width)]
                for side in (place.half, 1 - place.half)
            ]
        target = shares.at[place.half, item, rows]
        keep = pltpu.make_async_copy(mine, target, owner_sem.at[index])
        return keep, place.copy(theirs, target, swap_send.at[index], swap_recv.at[index], "x")

    def to_owner(index):
        flush()
        for copy in owner_moves(index):
            copy.start()

    def stages_of(kind):
        return list(range(2, min(3, count)) if kind == "first" else range(3, count))

    def prepare(item, kind):
        if kind == "total":
            sums[item].prepare_total()
        elif stages_of(kind):
            sums[item].prepare(stages_of(kind)[0])

    def complete(item, kind):
        if kind == "total":
            finish(item)
            return
        for index, stage in enumerate(stages_of(kind)):
            if index:
                sums[item].prepare(stage)
            sums[item].service(stage)

    def weight_grads(item, low, high, right, tasks=()):
        for c in range(4):
            for at, do, task in tasks:
                if at == c:
                    do(*task)
            slot = next_ready()
            columns = pl.ds(c * big, big)
            for first, last, matrix in zip(low, high, right):
                ready[slot, first:last, :] = jnp.dot(
                    turned[first:last, :], matrix[:, columns], preferred_element_type=F32
                ).astype(BF)
            rows = pl.ds(low[0], high[-1] - low[0])
            copy = pltpu.make_async_copy(ready.at[slot, rows], own_grads.at[item, rows, columns], ready_sem.at[slot])
            copy.start()
            pending[slot].append(copy.wait)

    plane = PlaneSum(place, grad, one, got, sum_send.at[1], sum_recv.at[1], chunk)

    def give_credit(index):
        for name in ("core", "first", "second"):
            pl.semaphore_signal(free_sem.at[index], inc=1, device_id=place.partner[name], device_id_type=MESH)

    def second_step(rows):
        residual, grad_second = two[rows, :], one[rows, :]
        factor = lax.rsqrt(jnp.mean(residual * residual, -1, keepdims=True) + EPS)
        normal = residual * factor
        small_own[1:2, :] += jnp.sum(grad_second * normal, 0, keepdims=True)
        scaled = grad_second * gain_ref[1:2, :]
        residual_grad = grad[rows, :].astype(F32) + factor * (
            scaled - normal * jnp.mean(scaled * normal, -1, keepdims=True)
        )
        one[rows, :] = residual_grad
        own_rows[rows, :] = residual_grad.astype(BF)
        both[rows, :] = residual_grad.astype(BF)

    branch = Gather(place, both, group, gather_send.at[3], gather_recv.at[3], own_rows)

    def feed_forward(hidden):
        place.locate()
        for s in range(SLICES):
            advance_through(s)
            lines[1 + s].arrived(count - 2)
            load_wide(w_forward.at[s], s).start()
            load_wide(w_forward.at[s], s).wait()

            def rows_step(b, _, s=s):
                rows = rows_at(b, block)
                gate_up = jnp.dot(second[rows, :], wide[:, :pair], preferred_element_type=F32)
                grad_hidden = jnp.dot(grad[rows, :], wide[:, pair:], preferred_element_type=F32)
                gate, up = gate_up[:, :slice_cols], gate_up[:, slice_cols:]
                sigmoid = 1.0 / (1.0 + jnp.exp(-gate))
                activated = gate * sigmoid
                hidden_rows = (activated * up).astype(BF)
                gate_rows = (grad_hidden * up * (sigmoid + activated * (1.0 - sigmoid))).astype(BF)
                up_rows = (grad_hidden * activated).astype(BF)
                hidden[rows, s * slice_cols : (s + 1) * slice_cols] = hidden_rows
                both[rows, s * pair : s * pair + slice_cols] = gate_rows
                both[rows, s * pair + slice_cols : (s + 1) * pair] = up_rows
                turned[:slice_cols, rows] = gate_rows.T
                turned[slice_cols:pair, rows] = up_rows.T
                turned[pair:, rows] = hidden_rows.T
                return 0

            lax.fori_loop(0, 4, rows_step, 0)
            advance(1)
            weight_grads(
                s, (0, pair), (pair, packed), (second, grad),
                (
                    (),
                    ((2, prepare, (0, "first")), (3, complete, (0, "first"))),
                    ((2, prepare, (0, "later")), (3, complete, (0, "later"))),
                    (
                        (0, prepare, (0, "total")), (1, complete, (0, "total")),
                        (2, prepare, (1, "first")), (3, complete, (1, "first")), (3, to_owner, (0,)),
                    ),
                )[s],
            )
            flush()
            sums[s].start()
            advance(1)

        def chunk_loads(c, low):
            base = (c % 2) * SLICES
            return [
                pltpu.make_async_copy(
                    w_forward.at[s, pl.ds(c * chunk, chunk), pl.ds(low, packed - low)],
                    wide.at[pl.ds((base + s) * chunk, chunk), pl.ds(low, packed - low)],
                    wide_sem.at[SLICES + base + s],
                )
                for s in range(SLICES)
            ]

        def summed(source, rows, step, low, high, base):
            return sum(
                lax.dot_general(
                    source[rows, s * step : (s + 1) * step],
                    wide[(base + s) * chunk : (base + s + 1) * chunk, low:high], NT,
                    preferred_element_type=F32,
                )
                for s in range(SLICES)
            )

        for copy in chunk_loads(0, 0):
            copy.start()
        for c in range(8):
            if c < 7:
                for copy in chunk_loads(c + 1, 0):
                    copy.start()
            for copy in chunk_loads(c, 0):
                copy.wait()
            base = (c % 2) * SLICES
            columns = pl.ds(c * chunk, chunk)

            def grad_rows(b, _, columns=columns, base=base):
                rows = rows_at(b, block)
                grad[rows, columns] = summed(both, rows, pair, 0, pair, base).astype(BF)
                return 0

            first = summed(both, pl.ds(0, block), pair, 0, pair, base)
            one[:, columns] = first[:group]
            grad[pl.ds(group, group), columns] = first[group:].astype(BF)
            lax.fori_loop(1, 4, grad_rows, 0)
            plane.push(c)
            if c >= 1:
                plane.middle(c - 1)
            if c >= 2:
                plane.late(c - 2)
            if c >= 3:
                plane.total(c - 3)
            if c == 3:
                prepare(1, "later")
            if c == 4:
                complete(1, "later")
        for copy in chunk_loads(0, pair):
            copy.start()
        plane.middle(7)
        plane.late(6)
        plane.late(7)
        prepare(1, "total")
        for c in (5, 6, 7):
            plane.total(c)
        give_credit(0)
        complete(1, "total")
        small_own[...] = jnp.zeros_like(small_own)
        by_rows(second_step)
        branch.start()
        prepare(2, "first")
        for c in range(8):
            if c < 7:
                for copy in chunk_loads(c + 1, pair):
                    copy.start()
            for copy in chunk_loads(c, pair):
                copy.wait()

            def branch_rows(b, _, c=c):
                rows = rows_at(b, block)
                second[rows, pl.ds(c * chunk, chunk)] = summed(
                    hidden, rows, slice_cols, pair, packed, (c % 2) * SLICES
                ).astype(BF)
                return 0

            lax.fori_loop(0, 4, branch_rows, 0)
            if c == 0:
                complete(2, "first")
            if c == 5:
                branch.step(1)

    pl.run_scoped(feed_forward, pltpu.VMEM((tokens, SLICES * slice_cols), BF))
    place.locate()
    w_load = load_wide(w_attention, 0)
    w_load.start()

    outer = PlaneSum(place, second, two, got, sum_send.at[2], sum_recv.at[2], width)

    def rows_add(target, first_row, rows, sources):
        def step(b, _):
            at = rows_at(b, group)
            to = pl.ds(pl.multiple_of(first_row + b * group, group), group)
            value = target[to, :].astype(F32)
            for source in sources:
                value = value + source[to, :].astype(F32)
            target[to, :] = value.astype(BF)
            return 0

        lax.fori_loop(0, rows // group, step, 0)

    pl.semaphore_wait(free_sem.at[0], 3)
    outer.push(0)
    for c in range(8):
        plane.sent(c)
    marks = [0, q_cols, q_cols + k_cols, qkv_cols, qkv_cols + q_cols, qkv_cols + 2 * q_cols]
    arrays = [local(heads_out, grad.at[:, pl.ds(0, packed)], load_sem.at[5])]
    for copy in arrays:
        copy.start()
    q_ref, k_ref = grad.at[:, pl.ds(0, q_cols)], grad.at[:, pl.ds(marks[1], k_cols)]
    v_ref, attended = grad.at[:, pl.ds(marks[2], k_cols)], grad.at[:, pl.ds(marks[3], q_cols)]
    attended_grad, qkv_grad = grad.at[:, pl.ds(marks[4], q_cols)], grad.at[:, pl.ds(marks[5], qkv_cols)]
    prepare(2, "later")
    w_load.wait()

    def attended_step(p, _):
        rows = rows_at(p, group)
        attended_grad[rows, :] = jnp.dot(
            both[rows, :], wide[:, qkv_cols:], preferred_element_type=F32
        ).astype(BF)
        return 0

    for copy in arrays:
        copy.wait()
    lax.fori_loop(0, 2, attended_step, 0)
    branch.step(2)
    branch.step(3)
    outer.move(0, 0).wait_recv()
    rows_add(second, 2 * group, 2 * group, (got_core,))
    outer.move(1, 0).start()
    lax.fori_loop(2, 4, attended_step, 0)
    complete(2, "later")
    for p in range(4):
        branch.arrived(p)
    lax.fori_loop(4, 8, attended_step, 0)

    def outer_late():
        outer.move(1, 0).wait_recv()
        rows_add(second, group, group, (got_core, got_first))
        outer.move(2, 0).start()
        prepare(2, "total")

    def attention(table, aux, key_sum, value_sum):
        place.locate()
        table_load = pltpu.make_async_copy(table_out, table, load_sem.at[9])
        aux_load = pltpu.make_async_copy(aux_out, aux, load_sem.at[10])
        table_load.start()
        aux_load.start()
        table_load.wait()
        aux_load.wait()
        attend_back_blocks(
            place, q_ref, k_ref, v_ref, aux, marks_ref, attended_grad, table, qkv_grad, key_sum, value_sum,
            outer_late,
        )

    pl.run_scoped(
        attention,
        pltpu.VMEM((tokens, HEAD_SIZE), F32), pltpu.VMEM((tokens, HEAD_SIZE), F32),
        pltpu.VMEM((tokens, k_cols), F32), pltpu.VMEM((tokens, k_cols), F32),
    )
    place.locate()
    branch.sent()
    complete(2, "total")
    prepare(3, "first")

    def turn_rows(source, first, last):
        def step(b, _):
            rows = rows_at(b, group)
            turned[first:last, rows] = source[rows, :].T
            return 0

        lax.fori_loop(0, 8, step, 0)

    turn_rows(attended, qkv_cols, packed)
    weight_grads(SLICES, (qkv_cols,), (packed,), (both,))
    flush()
    sums[SLICES].start()
    normed_load = pltpu.make_async_copy(normed_out, both, load_sem.at[2])
    normed_load.start()
    complete(3, "first")
    turn_rows(qkv_grad, 0, qkv_cols)
    normed_load.wait()
    weight_grads(SLICES, (0,), (qkv_cols,), (both,))
    flush()
    sums[SLICES + 1].start()
    for index in (1, 2):
        to_owner(index)
    outer.move(2, 0).wait_recv()

    def output_step(rows):
        own_rows[rows, :] = (
            two[rows, :]
            + second[rows, :].astype(F32)
            + got_core[rows, :].astype(F32)
            + got_first[rows, :].astype(F32)
            + got_second[rows, :].astype(F32)
        ).astype(BF)

    by_rows(output_step)
    give_credit(1)
    blocks = HalfGather(place, own_rows, block_output, half_send.at[0], half_recv.at[0], load_sem.at[3])
    blocks.start()
    prepare(3, "later")

    outer.sent(0)
    pl.semaphore_wait(free_sem.at[1], 3)
    inner = PlaneSum(place, second, two, got, sum_send.at[3], sum_recv.at[3], chunk)
    for c in range(8):
        columns = pl.ds(c * chunk, chunk)

        def first_part(rows, c=c):
            return lax.dot_general(
                qkv_grad[rows, :], wide[c * chunk : (c + 1) * chunk, :qkv_cols], NT, preferred_element_type=F32
            )

        def first_rows(b, _, columns=columns, first_part=first_part):
            rows = rows_at(b, block)
            second[rows, columns] = first_part(rows).astype(BF)
            return 0

        first = first_part(pl.ds(0, block))
        two[:, columns] = first[:group]
        second[pl.ds(group, group), columns] = first[group:].astype(BF)
        lax.fori_loop(1, 4, first_rows, 0)
        inner.push(c)
        if c == 0:
            complete(3, "later")
        if c == 1:
            prepare(SLICES, "first")
        if c == 2:
            complete(SLICES, "first")
        if c == 4:
            prepare(SLICES + 1, "first")
        if c == 5:
            complete(SLICES + 1, "first")
        if c == 6:
            prepare(3, "total")
        if c == 7:
            complete(3, "total")
        if c >= 1:
            inner.middle(c - 1)
        if c >= 3:
            inner.late(c - 3)
        if c >= 5:
            inner.total(c - 5)
    inner.middle(7)
    to_owner(3)
    prepare(SLICES, "later")
    blocks.step()
    for c in (5, 6, 7):
        inner.late(c)
        inner.total(c - 2)
    complete(SLICES, "later")
    inner.total(6)
    prepare(SLICES + 1, "later")
    inner.total(7)
    input_load = pltpu.make_async_copy(
        block_input.at[rows_at(place.tensor, group)], second.at[pl.ds(0, group)], load_sem.at[4]
    )
    input_load.start()
    input_load.wait()

    def first_step(rows):
        value, grad_first = second[rows, :].astype(F32), two[rows, :]
        factor = lax.rsqrt(jnp.mean(value * value, -1, keepdims=True) + EPS)
        normal = value * factor
        small_own[0:1, :] += jnp.sum(grad_first * normal, 0, keepdims=True)
        scaled = grad_first * gain_ref[0:1, :]
        input_grad = one[rows, :] + factor * (scaled - normal * jnp.mean(scaled * normal, -1, keepdims=True))
        second[rows, :] = input_grad.astype(BF)

    by_rows(first_step)
    gradients = HalfGather(
        place, second.at[pl.ds(0, group)], input_gradient, half_send.at[1], half_recv.at[1], load_sem.at[4]
    )
    gradients.start()
    complete(SLICES + 1, "later")

    for index, name in enumerate(("core", "y", "x")):
        move = place.copy(
            small_own.at[pl.ds(8 * index, 8)], small_got.at[index], small_send.at[index], small_recv.at[index], name
        )
        move.start()
        move.wait_recv()
        value = small_own[8 * index : 8 * index + 8, :] + small_got[index]
        if index < 2:
            small_own[8 * index + 8 : 8 * index + 16, :] = value
        else:
            small_all[place.sequence] = value
    gain_line = Line(place, lambda k: small_all.at[k], gain_send, gain_recv)
    gain_line.start(0)
    prepare(SLICES, "total")
    gradients.step()
    complete(SLICES, "total")
    to_owner(SLICES)
    for stage in range(count - 1):
        gain_line.arrived(stage)
        if stage < count - 2:
            gain_line.start(stage + 1)
    own_columns = pl.ds(pl.multiple_of(place.sequence * shard2, shard2), shard2)
    gain_out[...] = sum(small_all[k, :, own_columns] for k in range(count))
    prepare(SLICES + 1, "total")
    complete(SLICES + 1, "total")
    to_owner(SLICES + 1)

    flush()
    for line in lines[1:]:
        for stage in range(count - 1):
            line.sent(stage)
    if gains_here:
        for stage in range(count - 1):
            gain_shards.sent(stage)
    for index in (1, 2, 3) if gains_here else (1, 2):
        early(index).wait_send()
    for item, item_sum in enumerate(sums):
        item_sum.sent(item == SLICES + 1)
    for index in range(len(sum_items)):
        keep, swap = owner_moves(index)
        keep.wait()
        swap.wait()
    for c in range(8):
        inner.sent(c)
    for index, name in enumerate(("core", "y", "x")):
        place.copy(
            small_own.at[pl.ds(8 * index, 8)], small_got.at[index], small_send.at[index], small_recv.at[index], name
        ).wait_send()
    for stage in range(count - 1):
        gain_line.sent(stage)
    blocks.end()
    gradients.end()


def rotation(table):
    other = pltpu.roll(table, HEAD_SIZE // 2, 1)
    low = lax.broadcasted_iota(jnp.int32, table.shape, 1) < HEAD_SIZE // 2
    return jnp.where(low, table, other), jnp.where(low, -other, table)


def attend_back_blocks(
    place, q_ref, k_ref, v_ref, aux, columns_ref, grad_ref, table, out_ref, key_sum, value_sum, late
):
    block = q_ref.shape[0] // 8
    scale = 1.0 / math.sqrt(HEAD_SIZE)
    q_cols, k_cols = q_ref.shape[1], k_ref.shape[1]
    key_sum[...] = jnp.zeros_like(key_sum)
    value_sum[...] = jnp.zeros_like(value_sum)
    for at in range(8):
        low, high = key_range(at, block)
        here = slice(at * block, high)
        span = slice(low, high)
        allowed = allowed_pairs(aux, columns_ref, at, block)
        keys, values = k_ref[span, :], v_ref[span, :]
        cosine, sine = rotation(table[here, :])
        to = rows_at(place.of_group(at), block)
        for head in range(q_cols // HEAD_SIZE):
            columns = slice(head * HEAD_SIZE, (head + 1) * HEAD_SIZE)
            rows = q_ref[here, columns]
            grad_rows = grad_ref[to, columns]
            scores = lax.dot_general(rows, keys, NT, preferred_element_type=F32) * scale
            scores = jnp.where(allowed, scores, NEGATIVE)
            probs = jnp.exp(scores - aux[here, 1 + head : 2 + head])
            value_sum[span, :] += lax.dot_general(
                probs.astype(BF), grad_rows, TN, preferred_element_type=F32
            )
            prob_grad = lax.dot_general(grad_rows, values, NT, preferred_element_type=F32)
            inner = jnp.sum(probs * prob_grad, -1, keepdims=True)
            score_grad = (probs * (prob_grad - inner)).astype(BF)
            query_grad = jnp.dot(score_grad, keys, preferred_element_type=F32) * scale
            key_sum[span, :] += lax.dot_general(score_grad, rows, TN, preferred_element_type=F32)
            out_ref[to, columns] = turn(query_grad, cosine, -sine).astype(BF)
        if at == 5:
            late()
    for at in range(8):
        here = slice(at * block, (at + 1) * block)
        cosine, sine = rotation(table[here, :])
        to = rows_at(place.of_group(at), block)
        out_ref[to, q_cols : q_cols + k_cols] = turn(key_sum[here, :] * scale, cosine, -sine).astype(BF)
        out_ref[to, q_cols + k_cols :] = value_sum[here, :].astype(BF)


def layer(block_input, out_grad, gains, table, marks, masters, count):
    half_tokens, width = block_input.shape
    group, tokens = half_tokens // 4, 2 * half_tokens
    shard = masters[0].shape[0]
    q_cols, k_cols = masters[0].shape[1] // 2, masters[1].shape[1] // 2
    slice_cols = masters[4].shape[1] // 2 // SLICES
    packed = 3 * slice_cols
    assert packed == 2 * q_cols + 2 * k_cols and q_cols == group >= shard
    gains_here = shard % 128 == 0
    if not gains_here:
        gains = lax.all_gather(gains, "dp", axis=1, tiled=True)
    part = shard if gains_here else 2 * shard
    vmem, hbm = pl.BlockSpec(memory_space=pltpu.VMEM), pl.BlockSpec(memory_space=pl.ANY)
    struct = jax.ShapeDtypeStruct
    dma = pltpu.SemaphoreType.DMA
    items = 1 + SLICES
    return pl.pallas_call(
        functools.partial(layer_kernel, count, gains_here),
        in_specs=[hbm, hbm, vmem, hbm, vmem] + [hbm] * 7,
        out_specs=[hbm] * 3 + [vmem] + [hbm] * 9,
        out_shape=[
            struct((half_tokens, width), BF),
            struct((half_tokens, width), BF),
            struct((2, items, packed, part), BF),
            struct((8, 2 * shard), F32),
            struct((items, packed, width), BF),
            struct((items, 2, count - 1, packed, 2 * shard), BF),
            struct((items, packed, 2 * shard), BF),
            struct((width, packed), BF),
            struct((SLICES, width, packed), BF),
            struct((tokens, width), BF),
            struct((tokens, packed), BF),
            struct((tokens, HEAD_SIZE), F32),
            struct((tokens, HEAD_SIZE), F32),
        ],
        scratch_shapes=[
            pltpu.VMEM((tokens, width), BF),
            pltpu.VMEM((tokens, width), BF),
            pltpu.VMEM((tokens, width), BF),
            pltpu.VMEM((width, packed), BF),
            pltpu.VMEM((4 * group, width), BF),
            pltpu.VMEM((2 * group, width), BF),
            pltpu.VMEM((group, width), BF),
            pltpu.VMEM((4, packed, 2 * shard), BF),
            pltpu.VMEM((count - 1, packed, 2 * shard), BF),
            pltpu.VMEM((2, packed, width // 4), BF),
            pltpu.VMEM((packed, tokens), BF),
            pltpu.VMEM((group, width), F32),
            pltpu.VMEM((group, width), F32),
            pltpu.VMEM((group, width), BF),
            pltpu.VMEM((24, width), F32),
            pltpu.VMEM((3, 8, width), F32),
            pltpu.VMEM((count, 8, width), F32),
            pltpu.VMEM((8, width), F32),
            pltpu.VMEM((8, tokens), F32),
            dma((12,)),
            dma((3 * SLICES,)),
            dma((2,)),
            dma((1 + items,)),
            dma((1 + items,)),
            dma((1 + items, 2, count - 1)),
            dma((1 + items, 2, count - 1)),
            dma((4, 3, 8)),
            dma((4, 3, 8)),
            dma((4, 7)),
            dma((4, 7)),
            dma((2, 3)),
            dma((2, 3)),
            dma((3,)),
            dma((3,)),
            dma((2, count - 1)),
            dma((2, count - 1)),
            pltpu.SemaphoreType.REGULAR((2,)),
            dma((4,)),
            dma((1 + items,)),
            dma((4,)),
            dma((4,)),
            dma((SLICES, 2)),
            dma((SLICES, 2)),
            dma((2 + items, 2, count - 1)),
            dma((2 + items, 2, count - 1)),
            dma((5,)),
            dma((SLICES, 2)),
            dma((4,)),
        ],
        compiler_params=pltpu.CompilerParams(
            vmem_limit_bytes=VMEM_LIMIT, collective_id=0, has_side_effects=True
        ),
        name="layer",
    )(block_input, out_grad, gains, table, marks, *masters)


def adamw(weight, gradient, first, second, rate, decay):
    first_new = BETA_ONE * first + (1.0 - BETA_ONE) * gradient
    second_new = BETA_TWO * second + (1.0 - BETA_TWO) * gradient * gradient
    bias_first = 1.0 - BETA_ONE**STEP
    bias_second = 1.0 - BETA_TWO**STEP
    moved = first_new * (1.0 / bias_first) / (jnp.sqrt(second_new * (1.0 / bias_second)) + ADAM_EPS)
    return (weight - rate * (moved + decay * weight), first_new, second_new)


def update_kernel(attention_cuts, forward_cuts, *refs):
    a, f = 12, 9
    attention_share, forward_share, block_in, gradient_in = refs[:4]
    states, outs = refs[4 : 4 + a + f], refs[4 + a + f :]
    outs[0][...] = block_in[...]
    outs[1][...] = gradient_in[...].astype(F32)

    def one(gradient, arrays, results, at):
        fresh = adamw(arrays[0][at], gradient, arrays[1][at], arrays[2][at], RATE_MATRIX, DECAY)
        for result, value in zip(results, fresh):
            result[at] = value

    everything = (slice(None), slice(None))
    for i in range(3):
        gradient = forward_share[forward_cuts[i] : forward_cuts[i + 1], :].astype(F32)
        one(gradient if i == 2 else gradient.T, states[a + i :: 3][:3], outs[2 + a + i :: 3][:3], everything)

    @pl.when(pl.program_id(0) == 0)
    def _():
        for i in range(4):
            for side in range(2):
                low, high = attention_cuts[i], attention_cuts[i + 1]
                gradient = attention_share[side, low:high, :].astype(F32)
                span = slice(side * (high - low), (side + 1) * (high - low))
                if i == 3:
                    one(gradient, states[i:a:4], outs[2 + i : 2 + a : 4], (span, slice(None)))
                else:
                    one(gradient.T, states[i:a:4], outs[2 + i : 2 + a : 4], (slice(None), span))


def update(shares, block_output, input_gradient, attention_cuts, attention, forward_cuts, feed):
    packed, part = shares.shape[2:]
    steps = 2 * SLICES

    def rows_block(array):
        return pl.BlockSpec((array.shape[0] // steps, array.shape[1]), lambda g: (g, 0))

    def columns_block(array):
        return pl.BlockSpec((array.shape[0], array.shape[1] // steps), lambda g: (0, g))

    state_specs = [pl.BlockSpec(array.shape, lambda g: (0, 0)) for array in attention]
    state_specs += [rows_block(array) if i % 3 == 2 else columns_block(array) for i, array in enumerate(feed)]
    plain = [rows_block(block_output), rows_block(input_gradient)]
    return pl.pallas_call(
        functools.partial(update_kernel, attention_cuts, forward_cuts),
        grid=(steps,),
        in_specs=[
            pl.BlockSpec((2, None, packed, part), lambda g: (0, SLICES, 0, 0)),
            pl.BlockSpec((None, None, packed, part), lambda g: (g // SLICES, g % SLICES, 0, 0)),
        ]
        + plain
        + state_specs,
        out_specs=plain + state_specs,
        out_shape=[
            jax.ShapeDtypeStruct(block_output.shape, BF),
            jax.ShapeDtypeStruct(input_gradient.shape, F32),
        ]
        + [jax.ShapeDtypeStruct(array.shape, F32) for array in (*attention, *feed)],
        compiler_params=pltpu.CompilerParams(vmem_limit_bytes=VMEM_LIMIT),
        name="update",
    )(shares, shares, block_output, input_gradient, *attention, *feed)


def rotary_tables(positions):
    half = HEAD_SIZE // 2
    frequency = THETA ** (-2.0 * jnp.arange(half, dtype=F32) / HEAD_SIZE)
    angles = positions.astype(F32)[:, None] * frequency[None, :]
    cosine, sine = jnp.cos(angles), jnp.sin(angles)
    return jnp.concatenate([cosine, sine], -1)


def local(
    block_input, out_grad, segments, positions,
    w_query, w_key, w_value, w_output, w_gate, w_up, w_down, gains,
    m_query, m_key, m_value, m_output, m_gate, m_up, m_down, m_gains,
    v_query, v_key, v_value, v_output, v_gate, v_up, v_down, v_gains,
):
    half_tokens = block_input.shape[0]
    rows = w_query.shape[0]
    sequences = lax.axis_size("dp") // 2
    half = lax.axis_index("dp") % 2
    table = rotary_tables(positions)
    marks = jnp.broadcast_to(segments.astype(F32)[None, :], (8, half_tokens))
    gain_rows = jnp.pad(gains.astype(BF).astype(F32), ((0, 6), (0, 0)))
    masters = (w_query, w_key, w_value, w_output, w_gate, w_up, w_down)
    block_output, input_gradient, shares, gain_grads = layer(
        block_input, out_grad, gain_rows, table, marks, masters, sequences
    )[:4]
    if shares.shape[-1] != rows:
        shares = lax.dynamic_slice_in_dim(shares, half * rows, rows, 3)
    q_cols, k_cols, o_cols = w_query.shape[1] // 2, w_key.shape[1] // 2, w_output.shape[0] // 2
    slice_cols = w_gate.shape[1] // 2 // SLICES

    def cuts(*sizes):
        return [sum(sizes[:i]) for i in range(len(sizes) + 1)]

    block_output, input_gradient, *fresh = update(
        shares, block_output, input_gradient,
        cuts(q_cols, k_cols, k_cols, o_cols),
        (w_query, w_key, w_value, w_output, m_query, m_key, m_value, m_output, v_query, v_key, v_value, v_output),
        cuts(slice_cols, slice_cols, slice_cols),
        (w_gate, w_up, w_down, m_gate, m_up, m_down, v_gate, v_up, v_down),
    )
    attention_new, forward_new = fresh[:12], fresh[12:]
    gain_grads = lax.dynamic_slice_in_dim(gain_grads[:2], half * rows, rows, 1)
    gains_new = adamw(gains, gain_grads, m_gains, v_gains, RATE_GAIN, 0.0)
    new = [
        list(attention_new[4 * part : 4 * part + 4]) + list(forward_new[3 * part : 3 * part + 3]) + [gains_new[part]]
        for part in range(3)
    ]
    return tuple([block_output, input_gradient] + new[0] + new[1] + new[2])


def solution(mesh):
    matrices = [P("dp", "tensor")] * 3 + [P("tensor", "dp")] + [P("dp", "tensor")] * 2 + [P("tensor", "dp")]
    state = tuple(matrices + [P(None, "dp")])
    rows = (P("dp", None), P("dp", None))
    return jax.shard_map(
        local,
        mesh=mesh,
        in_specs=rows + (P("dp"), P("dp")) + state * 3,
        out_specs=rows + state * 3,
        check_vma=False,
    )
```

```python
import functools
import math

import jax
import jax.numpy as jnp
from jax import lax
from jax.experimental import pallas as pl
from jax.experimental.pallas import tpu as pltpu
from jax.sharding import PartitionSpec as P

HEAD_SIZE = 128
WINDOW = 1024
STEP = 5
EPS = 1e-06
THETA = 1000000.0
BETA_ONE = 0.5
BETA_TWO = 0.5
RATE_MATRIX = 0.02
RATE_GAIN = 0.3
DECAY = 0.1
ADAM_EPS = 1e-08
NEGATIVE = -1e30
SLICES = 4
BF = jnp.bfloat16
F32 = jnp.float32
VMEM_LIMIT = 63 * 1024 * 1024
MESH = pl.DeviceIdType.MESH


class Place:
    def __init__(self, sequences):
        self.count = sequences
        self.locate()

    def locate(self):
        self.dp, self.tensor = lax.axis_index("dp"), lax.axis_index("tensor")
        self.sequence, self.half = self.dp // 2, self.dp % 2
        self.y, self.core = self.tensor // 2, self.tensor % 2
        across = 1 - 2 * self.half
        beside = 2 - 4 * self.y
        self.partner = {
            "core": (self.dp, self.tensor + 1 - 2 * self.core),
            "x": (self.dp + across, self.tensor),
            "y": (self.dp, self.tensor + beside),
            "first": (self.dp + (1 - self.core) * across, self.tensor + self.core * beside),
            "second": (self.dp + self.core * across, self.tensor + (1 - self.core) * beside),
            "right": (self.dp + 2, self.tensor),
            "left": (self.dp - 2, self.tensor),
        }

    def of_group(self, g):
        dh = (g // 4 + self.half) % 2
        dy = ((g // 2) % 2 + self.y) % 2
        dc = (g % 2 + self.core) % 2
        from_core = (self.core + dc) % 2
        straight = dh * 2 + dy
        return dc * 4 + straight + from_core * (dy * 2 + dh - straight)

    def greet(self):
        barrier = pltpu.get_barrier_semaphore()
        for name in ("core", "x", "y"):
            pl.semaphore_signal(barrier, inc=1, device_id=self.partner[name], device_id_type=MESH)

        @pl.when(self.sequence >= 1)
        def _():
            pl.semaphore_signal(barrier, inc=1, device_id=self.partner["left"], device_id_type=MESH)

        @pl.when(self.sequence <= self.count - 2)
        def _():
            pl.semaphore_signal(barrier, inc=1, device_id=self.partner["right"], device_id_type=MESH)

        ends = (self.sequence + self.count - 1) // self.count + (2 * self.count - 2 - self.sequence) // self.count
        pl.semaphore_wait(barrier, 3 + ends)

    def copy(self, source, target, send, recv, name):
        return pltpu.make_async_remote_copy(
            src_ref=source, dst_ref=target, send_sem=send, recv_sem=recv,
            device_id=self.partner[name], device_id_type=MESH,
        )


class Gather:
    moves = [("second", 0, 1), ("first", 0, 2), ("first", 1, 3)] + [("core", p, p + 4) for p in range(4)]

    def __init__(self, place, buffer, group, send, recv, own=None):
        self.place, self.buffer, self.group = place, buffer, group
        self.send, self.recv, self.own = send, recv, own

    def at(self, index):
        return self.buffer.at[pl.ds(index * self.group, self.group)]

    def copy(self, index):
        name, source, target = self.moves[index]
        source = self.own if self.own is not None and source == 0 else self.at(source)
        return self.place.copy(source, self.at(target), self.send.at[index], self.recv.at[index], name)

    def start(self):
        for index in (0, 1, 3):
            self.copy(index).start()

    def step(self, index):
        if index == 1:
            self.copy(0).wait_recv()
            self.copy(2).start()
            self.copy(4).start()
        else:
            self.copy(index - 1).wait_recv()
            self.copy(index + 3).start()

    def arrived(self, index):
        self.copy(3 + index).wait_recv()

    def sent(self):
        for index in range(7):
            self.copy(index).wait_send()


class Line:
    def __init__(self, place, slot, send, recv):
        self.place, self.slot = place, slot
        self.sends, self.recvs = send, recv

    def move(self, way, stage):
        place = self.place
        shard = place.sequence - stage if way == 0 else place.sequence + stage
        target = self.slot(shard)
        name = "right" if way == 0 else "left"
        return place.copy(target, target, self.sends.at[way, stage], self.recvs.at[way, stage], name)

    def conditions(self, stage):
        place = self.place
        last = place.count - 1
        sends = (
            (place.sequence >= stage) & (place.sequence <= last - 1),
            (place.sequence <= last - stage) & (place.sequence >= 1),
        )
        recvs = (place.sequence >= stage + 1, place.sequence <= last - 1 - stage)
        return sends, recvs

    def start(self, stage):
        for way, condition in enumerate(self.conditions(stage)[0]):
            @pl.when(condition)
            def _(way=way):
                self.move(way, stage).start()

    def arrived(self, stage):
        for way, condition in enumerate(self.conditions(stage)[1]):
            @pl.when(condition)
            def _(way=way):
                place = self.place
                shard = place.sequence - 1 - stage if way == 0 else place.sequence + 1 + stage
                target = self.slot(shard)
                place.copy(
                    target, target, self.sends.at[way, stage], self.recvs.at[way, stage],
                    "right" if way == 0 else "left",
                ).wait_recv()

    def sent(self, stage):
        for way, condition in enumerate(self.conditions(stage)[0]):
            @pl.when(condition)
            def _(way=way):
                self.move(way, stage).wait_send()


def turn(head, cosine, sine):
    return head * cosine + pltpu.roll(head, HEAD_SIZE // 2, 1) * sine


def key_range(block_at, block):
    low = max(0, block_at * block - WINDOW + 1) // block * block
    return low, (block_at + 1) * block


def allowed_pairs(segment_rows, segment_columns, block_at, block):
    low, high = key_range(block_at, block)
    shape = (block, high - low)
    distance = (
        lax.broadcasted_iota(jnp.int32, shape, 0)
        - lax.broadcasted_iota(jnp.int32, shape, 1)
        + (block_at * block - low)
    )
    same = segment_rows[block_at * block : high, 0:1] == segment_columns[0:1, low:high]
    return same & (distance >= 0) & (distance < WINDOW)


NT = (((1,), (1,)), ((), ()))
TN = (((0,), (0,)), ((), ()))


def rows_at(index, size):
    return pl.ds(pl.multiple_of(index * size, size), size)


def group_at(place, p):
    dc = p // 4
    from_core = (place.core + dc) % 2
    one, two = (p // 2) % 2, p % 2
    dh = one + from_core * (two - one)
    dy = two + from_core * (one - two)
    return ((dh + place.half) % 2) * 4 + ((dy + place.y) % 2) * 2 + (dc + place.core) % 2


def attend_blocks(place, heads, q_cols, k_cols, aux, columns_ref, between):
    block = heads.shape[0] // 8
    qkv_cols = q_cols + 2 * k_cols
    scale = 1.0 / math.sqrt(HEAD_SIZE)
    for at in range(8):
        low, high = key_range(at, block)
        allowed = allowed_pairs(aux, columns_ref, at, block)
        keys, values = heads[low:high, q_cols : q_cols + k_cols], heads[low:high, q_cols + k_cols : qkv_cols]
        to = rows_at(place.of_group(at), block)
        for head in range(q_cols // HEAD_SIZE):
            columns = slice(head * HEAD_SIZE, (head + 1) * HEAD_SIZE)
            rows = heads[at * block : high, columns]
            scores = lax.dot_general(rows, keys, NT, preferred_element_type=F32) * scale
            scores = jnp.where(allowed, scores, NEGATIVE)
            top = jnp.max(scores, -1, keepdims=True)
            weights = jnp.exp(scores - top)
            total = jnp.sum(weights, -1, keepdims=True)
            probs = (weights * (1.0 / total)).astype(BF)
            heads[to, qkv_cols + columns.start : qkv_cols + columns.stop] = jnp.dot(
                probs, values, preferred_element_type=F32
            ).astype(BF)
            aux[at * block : high, 1 + head : 2 + head] = top + jnp.log(total)
        between(at)


class LineSum:
    def __init__(self, place, item, rows, index, own, recv, loads, ring, send_sem, recv_sem, load_sem, before):
        self.place, self.item, self.index, self.own, self.recv = place, item, index, own, recv
        self.rows = pl.ds(*rows)
        self.loads, self.ring = loads.at[:, self.rows], ring.at[:, self.rows]
        self.send_sem, self.recv_sem, self.load_sem = send_sem, recv_sem, load_sem
        self.before = before
        self.width = recv.shape[-1]

    def own_part(self, d):
        return self.own.at[self.item, self.rows, pl.ds(pl.multiple_of(d * self.width, self.width), self.width)]

    def dest(self, way, j):
        return self.place.count - 1 - j if way == 0 else j

    def move(self, way, j, source):
        return self.place.copy(
            source, self.recv.at[self.item, way, j, self.rows],
            self.send_sem.at[self.index, way, j], self.recv_sem.at[self.index, way, j],
            "right" if way == 0 else "left",
        )

    def start(self):
        last = self.place.count - 1
        for way, end in ((0, 0), (1, last)):
            @pl.when(self.place.sequence == end)
            def _(way=way):
                for j in range(last):
                    self.move(way, j, self.own_part(self.dest(way, j))).start()

    def turn_of(self, way, stage):
        depth = self.place.sequence if way == 0 else self.place.count - 1 - self.place.sequence
        return (depth >= 1) & (depth <= stage - 1), stage - 1 - depth, depth

    def slot(self, way, j):
        return j if way == 0 else self.place.count - 1 - self.place.sequence + j

    def own_load(self, way, d):
        return pltpu.make_async_copy(self.own_part(d), self.loads.at[2 * way], self.load_sem.at[2 * way])

    def came_load(self, way, j):
        return pltpu.make_async_copy(
            self.recv.at[self.item, way, j, self.rows], self.loads.at[2 * way + 1], self.load_sem.at[2 * way + 1]
        )

    def prepare(self, stage):
        for way in (0, 1):
            condition, j, _ = self.turn_of(way, stage)

            @pl.when(condition)
            def _(way=way, j=j):
                self.own_load(way, self.dest(way, j)).start()
                self.move(way, j, self.ring.at[self.slot(way, j)]).wait_recv()
                self.came_load(way, j).start()

    def service(self, stage):
        for way in (0, 1):
            condition, j, _ = self.turn_of(way, stage)

            @pl.when(condition)
            def _(way=way, j=j):
                slot = self.slot(way, j)
                if self.before is not None:
                    self.before.move(way, j, self.before.ring.at[slot]).wait_send()
                self.own_load(way, self.dest(way, j)).wait()
                self.came_load(way, j).wait()
                self.ring[slot] = (self.loads[2 * way].astype(F32) + self.loads[2 * way + 1].astype(F32)).astype(BF)
                self.move(way, j, self.ring.at[slot]).start()

    def last(self, way):
        place = self.place
        if way == 0:
            return place.sequence >= 1, place.count - 1 - place.sequence
        return place.sequence <= place.count - 2, place.sequence

    def prepare_total(self):
        self.own_load(0, self.place.sequence).start()
        for way in (0, 1):
            condition, j = self.last(way)

            @pl.when(condition)
            def _(way=way, j=j):
                self.move(way, j, self.loads.at[2 * way + 1]).wait_recv()
                self.came_load(way, j).start()

            @pl.when(jnp.logical_not(condition))
            def _(way=way):
                self.loads[2 * way + 1] = jnp.zeros(self.loads.shape[1:], BF)

    def total(self, out):
        self.own_load(0, self.place.sequence).wait()
        for way in (0, 1):
            condition, j = self.last(way)

            @pl.when(condition)
            def _(way=way, j=j):
                self.came_load(way, j).wait()

        out[...] = (
            self.loads[0].astype(F32) + self.loads[1].astype(F32) + self.loads[3].astype(F32)
        ).astype(BF)

    def sent(self, last_item):
        last = self.place.count - 1
        for way, end in ((0, 0), (1, last)):
            @pl.when(self.place.sequence == end)
            def _(way=way):
                for j in range(last):
                    self.move(way, j, self.own_part(self.dest(way, j))).wait_send()

        if last_item:
            for stage in range(2, last + 1):
                for way in (0, 1):
                    condition, j, _ = self.turn_of(way, stage)

                    @pl.when(condition)
                    def _(way=way, j=j):
                        self.move(way, j, self.ring.at[self.slot(way, j)]).wait_send()


class PlaneSum:
    def __init__(self, place, part, own, got, send_sem, recv_sem, chunk):
        self.place, self.part, self.own, self.got = place, part, own, got
        self.send_sem, self.recv_sem, self.chunk = send_sem, recv_sem, chunk
        self.group = own.shape[0]

    def columns(self, c):
        return pl.ds(c * self.chunk, self.chunk)

    def move(self, step, c):
        group, columns = self.group, self.columns(c)
        rows = ((4, 4), (2, 2), (1, 1))[step]
        name = ("core", "first", "second")[step]
        return self.place.copy(
            self.part.at[pl.ds(rows[0] * group, rows[1] * group), columns], self.got[step].at[:, columns],
            self.send_sem.at[step, c], self.recv_sem.at[step, c], name,
        )

    def push(self, c):
        self.move(0, c).start()

    def middle(self, c):
        self.move(0, c).wait_recv()
        rows, columns = pl.ds(2 * self.group, 2 * self.group), self.columns(c)
        self.part[rows, columns] = (
            self.part[rows, columns].astype(F32) + self.got[0][rows, columns].astype(F32)
        ).astype(BF)
        self.move(1, c).start()

    def late(self, c):
        self.move(1, c).wait_recv()
        rows, columns = pl.ds(self.group, self.group), self.columns(c)
        self.part[rows, columns] = (
            self.part[rows, columns].astype(F32)
            + self.got[0][rows, columns].astype(F32)
            + self.got[1][rows, columns].astype(F32)
        ).astype(BF)
        self.move(2, c).start()

    def total(self, c):
        self.move(2, c).wait_recv()
        rows, columns = pl.ds(0, self.group), self.columns(c)
        self.own[:, columns] = (
            self.own[:, columns]
            + self.got[0][rows, columns].astype(F32)
            + self.got[1][rows, columns].astype(F32)
            + self.got[2][:, columns].astype(F32)
        )

    def sent(self, c):
        for step in range(3):
            self.move(step, c).wait_send()


class HalfGather:
    def __init__(self, place, own, buffer, send, recv, local):
        self.place = place
        group = own.shape[0]
        tensor, across = place.tensor, place.tensor + 2 - 4 * place.y

        def at(index):
            return buffer.at[rows_at(index, group)]

        self.keep = pltpu.make_async_copy(own, at(tensor), local)
        self.y = place.copy(own, at(tensor), send.at[0], recv.at[0], "y")
        self.core = place.copy(own, at(tensor), send.at[1], recv.at[1], "core")
        self.far = place.copy(at(across), at(across), send.at[2], recv.at[2], "core")

    def start(self):
        self.keep.start()
        self.y.start()
        self.core.start()

    def step(self):
        self.y.wait_recv()
        self.far.start()

    def end(self):
        self.keep.wait()
        self.y.wait_send()
        self.core.wait()
        self.far.wait()


def layer_kernel(
    count, gains_here,
    block_input, out_grad, gains, table_half, marks_half,
    w_query, w_key, w_value, w_output, w_gate, w_up, w_down,
    block_output, input_gradient, shares, gain_out,
    own_grads, line_got, totals, w_attention, w_forward, normed_out, heads_out, table_out, aux_out,
    second, grad, both, wide, got_core, got_first, got_second, loads, ring, ready, turned,
    one, two, own_rows, small_own, small_got, small_all, gain_ref, marks_ref,
    load_sem, wide_sem, ready_sem, swap_send, swap_recv, line_send, line_recv, sum_send, sum_recv,
    gather_send, gather_recv, half_send, half_recv, small_send, small_recv, gain_send, gain_recv, free_sem,
    line_load_sem, owner_sem, early_send, early_recv, slice_send, slice_recv, shard_send, shard_recv, master_sem, keep_sem, out_sem,
):
    place = Place(count)
    group, width = own_rows.shape
    tokens = 8 * group
    packed = wide.shape[1]
    slice_cols = packed // 3
    pair = 2 * slice_cols
    shard = w_query.shape[0]
    q_cols, k_cols = w_query.shape[1] // 2, w_key.shape[1] // 2
    qkv_cols = q_cols + 2 * k_cols
    shard2 = line_got.shape[-1]
    part_width = shares.shape[-1]
    chunk = width // 4
    block = 2 * group
    got = (got_core, got_first, got_second)

    def load_wide(source, index):
        return pltpu.make_async_copy(source, wide, wide_sem.at[index])

    def shard_rows():
        return pl.ds(pl.multiple_of(place.dp * shard, shard), shard)

    def sequence_rows(k):
        return pl.ds(pl.multiple_of(k * 2 * shard, 2 * shard), 2 * shard)

    local = pltpu.make_async_copy

    masters = [
        local(w_query, one.at[pl.ds(0, shard), pl.ds(0, 2 * q_cols)], master_sem.at[0]),
        local(w_key, one.at[pl.ds(0, shard), pl.ds(2 * q_cols, 2 * k_cols)], master_sem.at[1]),
        local(w_value, one.at[pl.ds(0, shard), pl.ds(2 * q_cols + 2 * k_cols, 2 * k_cols)], master_sem.at[2]),
    ]
    own_loads = [
        local(block_input.at[rows_at(place.tensor, group)], both.at[pl.ds(0, group)], load_sem.at[2]),
        local(out_grad.at[rows_at(place.tensor, group)], grad.at[pl.ds(0, group)], load_sem.at[3]),
    ]
    table_keep = local(table_half, table_out.at[rows_at(place.half, 4 * group)], load_sem.at[4])
    for copy in masters + own_loads + [table_keep]:
        copy.start()
    marks_ref[:, rows_at(place.half, 4 * group)] = marks_half[...]

    def early(index):
        columns = rows_at(place.half, 4 * group)
        source, target = (
            (own_rows.at[pl.ds(0, shard), pl.ds(0, packed)], wide.at[shard_rows()]),
            (marks_half, marks_ref.at[:, columns]),
            (table_half, table_out.at[columns]),
            (gains, gain_ref.at[:, shard_rows()] if gains_here else None),
        )[index]
        return place.copy(source, target, early_send.at[index], early_recv.at[index], "x")

    def unit(s, theirs, part):
        k = 2 * s + theirs
        if part == 0:
            return pl.ds((k // 4) * slice_cols, shard), pl.ds((k % 4) * pair, pair)
        return pl.ds(pair, shard), pl.ds(k * slice_cols, slice_cols)

    def slice_target(s, part):
        return w_forward.at[s, shard_rows(), pl.ds(0, pair) if part == 0 else pl.ds(pair, slice_cols)]

    def slice_swap(s, part):
        return place.copy(
            turned.at[unit(s, 1, part)], slice_target(s, part), slice_send.at[s, part], slice_recv.at[s, part], "x"
        )

    def slice_keep(s, part):
        return local(turned.at[unit(s, 0, part)], slice_target(s, part), keep_sem.at[s, part])

    lines = [
        Line(
            place, lambda k: wide.at[sequence_rows(k), pl.ds(0, qkv_cols)], shard_send.at[0], shard_recv.at[0]
        )
    ] + [
        Line(
            place, lambda k, s=s: w_forward.at[s, sequence_rows(k)], shard_send.at[1 + s], shard_recv.at[1 + s]
        )
        for s in range(SLICES)
    ]
    output_line = Line(
        place, lambda k: wide.at[sequence_rows(k), pl.ds(qkv_cols, q_cols)],
        shard_send.at[2 + SLICES], shard_recv.at[2 + SLICES],
    )

    def output_steps(first, last):
        for stage in range(min(first, count - 1), min(last, count - 1)):
            output_line.arrived(stage)
            if stage < count - 2:
                output_line.start(stage + 1)

    gain_shards = Line(
        place, lambda k: gain_ref.at[:, sequence_rows(k)], shard_send.at[1 + SLICES], shard_recv.at[1 + SLICES]
    )

    begin = (0, 1, 2 * count - 4, 3 * count - 6.5)
    sends = sorted(
        ((s, stage) for s in range(SLICES) for stage in range(count - 1)),
        key=lambda item: (begin[item[0]] + 2 * item[1] + (item[1] > 0) * (item[0] >= 2) * 2, item[0]),
    )

    def advance(number):
        for _ in range(min(number, len(sends))):
            s, stage = sends.pop(0)
            if stage == 0:
                for part in range(2):
                    slice_swap(s, part).wait_recv()
            else:
                lines[1 + s].arrived(stage - 1)
            lines[1 + s].start(stage)

    def advance_through(s):
        while any(item[0] == s for item in sends):
            advance(1)

    place.greet()

    def attention_shard(output, target, rows, side):
        target[rows, :q_cols] = one[:shard, rows_at(side, q_cols)].astype(BF)
        for index in range(2):
            base = 2 * q_cols + 2 * k_cols * index
            target[rows, q_cols + k_cols * index : q_cols + k_cols * (index + 1)] = one[
                :shard, pl.ds(pl.multiple_of(base + side * k_cols, k_cols), k_cols)
            ].astype(BF)
        target[rows, qkv_cols:packed] = output[rows_at(side, q_cols), :].T.astype(BF)

    def fill_attention(output):
        place.locate()
        output_load = local(w_output, output, master_sem.at[3])
        output_load.start()
        for copy in masters + [output_load]:
            copy.wait()
        attention_shard(output, own_rows, slice(0, shard), 1 - place.half)
        early(0).start()
        attention_shard(output, wide, shard_rows(), place.half)

    pl.run_scoped(fill_attention, pltpu.VMEM(w_output.shape, F32))
    place.locate()
    masters = [
        local(w_gate, one.at[pl.ds(0, shard)], master_sem.at[0]),
        local(w_up, two.at[pl.ds(0, shard)], master_sem.at[1]),
    ]
    for copy in masters:
        copy.start()
    early(1).start()
    if gains_here:
        gain_ref[:, shard_rows()] = gains[...]
        early(3).start()
    else:
        gain_ref[...] = gains[...]
    inputs = Gather(place, both, group, gather_send.at[0], gather_recv.at[0])
    own_loads[0].wait()
    inputs.start()
    early(0).wait_recv()
    lines[0].start(0)
    if gains_here:
        early(3).wait_recv()
        gain_shards.start(0)

    def fill_slices(down):
        place.locate()
        down_load = local(w_down, down, master_sem.at[2])
        down_load.start()
        for copy in masters + [down_load]:
            copy.wait()
        for s in range(SLICES):
            for theirs in (1, 0):
                side = place.half + theirs - 2 * theirs * place.half
                columns = rows_at(side * SLICES + s, slice_cols)
                (rows, at), (down_rows, down_at) = unit(s, theirs, 0), unit(s, theirs, 1)
                turned[rows, pl.ds(at.start, slice_cols)] = one[:shard, columns].astype(BF)
                turned[rows, pl.ds(at.start + slice_cols, slice_cols)] = two[:shard, columns].astype(BF)
                turned[down_rows, down_at] = down[columns, :].T.astype(BF)
            for part in range(2):
                slice_keep(s, part).start()
            if s == 0:
                inputs.step(1)

    pl.run_scoped(fill_slices, pltpu.VMEM(w_down.shape, F32))
    place.locate()
    if gains_here:
        for stage in range(count - 1):
            gain_shards.arrived(stage)
            if stage < count - 2:
                gain_shards.start(stage + 1)
    lines[0].arrived(0)
    if count > 2:
        lines[0].start(1)

    def start_swap(s):
        for part in range(2):
            slice_swap(s, part).start()

    inputs.step(2)
    inputs.step(3)
    start_swap(0)
    start_swap(1)
    early(2).start()

    def norm_block(p, _):
        rows = rows_at(p, group)
        x = both[rows, :].astype(F32)
        factor = lax.rsqrt(jnp.mean(x * x, -1, keepdims=True) + EPS)
        second[rows, :] = (x * factor * gain_ref[0:1, :]).astype(BF)
        return 0

    lax.fori_loop(0, 4, norm_block, 0)
    for stage in range(1, count - 1):
        lines[0].arrived(stage)
        if stage < count - 2:
            lines[0].start(stage + 1)
    for p in range(4):
        inputs.arrived(p)
    lax.fori_loop(4, 8, norm_block, 0)
    for s in range(SLICES):
        for part in range(2):
            slice_keep(s, part).wait()
    output_line.start(0)
    grads = Gather(place, grad, group, gather_send.at[2], gather_recv.at[2])
    own_loads[1].wait()
    grads.start()
    start_swap(2)
    normed_copy = local(second, normed_out, out_sem.at[0])
    wide_copy = local(wide, w_attention, out_sem.at[1])
    normed_copy.start()
    mixed = PlaneSum(place, both, two, got, sum_send.at[0], sum_recv.at[0], chunk)

    def attention_forward(heads, table, aux):
        place.locate()
        table_keep.wait()
        early(2).wait_recv()
        table_load = local(table_out, table, load_sem.at[4])
        table_load.start()
        aux[...] = jnp.zeros_like(aux)
        early(1).wait_recv()
        tile = (HEAD_SIZE, HEAD_SIZE)
        diagonal = lax.broadcasted_iota(jnp.int32, tile, 0) == lax.broadcasted_iota(jnp.int32, tile, 1)
        for at in range(0, tokens, HEAD_SIZE):
            aux[at : at + HEAD_SIZE, 0:1] = jnp.sum(
                jnp.where(diagonal, marks_ref[0:1, at : at + HEAD_SIZE], 0.0), -1, keepdims=True
            )
        table_load.wait()

        def project_block(p, _):
            out = jnp.dot(second[rows_at(p, group), :], wide[:, :qkv_cols], preferred_element_type=F32)
            to = rows_at(group_at(place, p), group)
            cosine, sine = rotation(table[to, :])
            for at in range(0, q_cols + k_cols, HEAD_SIZE):
                heads[to, at : at + HEAD_SIZE] = turn(out[:, at : at + HEAD_SIZE], cosine, sine).astype(BF)
            heads[to, q_cols + k_cols : qkv_cols] = out[:, q_cols + k_cols :].astype(BF)
            return 0

        lax.fori_loop(0, 8, project_block, 0)
        output_steps(0, 1)
        advance(1)
        grads.step(1)

        def between(at):
            if at == 2:
                output_steps(1, 2)
            if at == 3:
                advance(1)
            if at == 5:
                output_steps(2, count)
            if at == 6:
                advance(1)

        attend_blocks(place, heads, q_cols, k_cols, aux, marks_ref, between)
        wide_copy.start()
        heads_copy = local(heads, heads_out, out_sem.at[2])
        aux_copy = local(aux, aux_out, out_sem.at[3])
        heads_copy.start()
        aux_copy.start()
        inputs.sent()
        normed_copy.wait()

        for c in range(4):
            columns = pl.ds(c * chunk, chunk)

            def mixed_part(rows, c=c):
                return lax.dot_general(
                    heads[rows, qkv_cols:], wide[c * chunk : (c + 1) * chunk, qkv_cols:], NT,
                    preferred_element_type=F32,
                )

            def mixed_rows(b, _, columns=columns, mixed_part=mixed_part):
                rows = rows_at(b, block)
                both[rows, columns] = mixed_part(rows).astype(BF)
                return 0

            first = mixed_part(pl.ds(0, block))
            two[:, columns] = first[:group]
            both[pl.ds(group, group), columns] = first[group:].astype(BF)
            lax.fori_loop(1, 4, mixed_rows, 0)
            mixed.push(c)
            if c >= 1:
                mixed.middle(c - 1)
            if c >= 2:
                mixed.late(c - 2)
            if c >= 3:
                mixed.total(c - 3)
            if c == 1:
                advance(1)
            if c == 2:
                grads.step(2)
            if c == 3:
                grads.step(3)
        heads_copy.wait()
        aux_copy.wait()

    pl.run_scoped(
        attention_forward,
        pltpu.VMEM((tokens, packed), BF), pltpu.VMEM((tokens, HEAD_SIZE), F32), pltpu.VMEM((tokens, HEAD_SIZE), F32),
    )
    place.locate()
    mixed.middle(3)
    advance(1)
    mixed.late(2)
    mixed.late(3)
    advance(1)
    for c in (1, 2, 3):
        mixed.total(c)
    early(0).wait_send()

    def by_rows(step):
        def some(b, _):
            step(rows_at(b, group // 4))
            return 0

        lax.fori_loop(0, 4, some, 0)

    def residual_step(rows):
        residual = two[rows, :] + both[rows, :].astype(F32)
        two[rows, :] = residual
        factor = lax.rsqrt(jnp.mean(residual * residual, -1, keepdims=True) + EPS)
        normal = (residual * factor * gain_ref[1:2, :]).astype(BF)
        own_rows[rows, :] = normal
        second[rows, :] = normal

    by_rows(residual_step)
    seconds = Gather(place, second, group, gather_send.at[1], gather_recv.at[1], own_rows)
    seconds.start()
    start_swap(3)
    advance(1)
    seconds.step(1)
    advance(1)
    wide_copy.wait()
    for stage in range(count - 1):
        lines[0].sent(stage)
        output_line.sent(stage)
    for c in range(4):
        mixed.sent(c)
    for s in range(SLICES):
        for part in range(2):
            if s < SLICES - 1:
                slice_swap(s, part).wait_send()
    seconds.step(2)
    seconds.step(3)
    for part in range(2):
        slice_swap(SLICES - 1, part).wait_send()
    for p in range(4):
        grads.arrived(p)
    advance(1)
    for p in range(4):
        seconds.arrived(p)
    seconds.sent()
    grads.sent()

    sums = []
    sum_items = [(s, 0, packed) for s in range(SLICES)]
    sum_items += [(SLICES, qkv_cols, q_cols), (SLICES, 0, qkv_cols)]
    for index, (item, low, size) in enumerate(sum_items):
        sums.append(
            LineSum(
                place, item, (low, size), index, own_grads, line_got, loads, ring, line_send, line_recv, line_load_sem,
                sums[-1] if sums else None,
            )
        )

    pending = {0: [], 1: []}
    turn_at = [0]

    def next_ready():
        slot = turn_at[0] % 2
        turn_at[0] += 1
        for wait in pending[slot]:
            wait()
        pending[slot] = []
        return slot

    def flush():
        for slot in (0, 1):
            for wait in pending[slot]:
                wait()
            pending[slot] = []

    def finish(index):
        item, low, size = sum_items[index]
        slot = next_ready()
        rows = pl.ds(low, size)
        sums[index].total(ready.at[slot, rows, pl.ds(0, shard2)])

        def copy():
            return pltpu.make_async_copy(
                ready.at[slot, rows, pl.ds(0, shard2)], totals.at[item, rows], ready_sem.at[slot]
            )

        copy().start()
        pending[slot].append(lambda: copy().wait())

    def owner_moves(index):
        item, low, size = sum_items[index]
        rows = pl.ds(low, size)
        if part_width == shard2:
            mine = theirs = totals.at[item, rows]
        else:
            mine, theirs = [
                totals.at[item, rows, pl.ds(pl.multiple_of(side * part_width, part_width), part_width)]
                for side in (place.half, 1 - place.half)
            ]
        target = shares.at[place.half, item, rows]
        keep = pltpu.make_async_copy(mine, target, owner_sem.at[index])
        return keep, place.copy(theirs, target, swap_send.at[index], swap_recv.at[index], "x")

    def to_owner(index):
        flush()
        for copy in owner_moves(index):
            copy.start()

    def stages_of(kind):
        return list(range(2, min(3, count)) if kind == "first" else range(3, count))

    def prepare(item, kind):
        if kind == "total":
            sums[item].prepare_total()
        elif stages_of(kind):
            sums[item].prepare(stages_of(kind)[0])

    def complete(item, kind):
        if kind == "total":
            finish(item)
            return
        for index, stage in enumerate(stages_of(kind)):
            if index:
                sums[item].prepare(stage)
            sums[item].service(stage)

    def weight_grads_chunk(item, low, high, right, c):
        slot = next_ready()
        columns = pl.ds(c * chunk, chunk)
        for first, last, matrix in zip(low, high, right):
            ready[slot, first:last, :] = jnp.dot(
                turned[first:last, :], matrix[:, columns], preferred_element_type=F32
            ).astype(BF)
        rows = pl.ds(low[0], high[-1] - low[0])

        def copy():
            return pltpu.make_async_copy(
                ready.at[slot, rows], own_grads.at[item, rows, columns], ready_sem.at[slot]
            )

        copy().start()
        pending[slot].append(lambda: copy().wait())

    def weight_grads(item, low, high, right, tasks=()):
        for c in range(4):
            for at, do, task in tasks:
                if at == c:
                    do(*task)
            weight_grads_chunk(item, low, high, right, c)

    plane = PlaneSum(place, grad, one, got, sum_send.at[1], sum_recv.at[1], chunk)

    def give_credit(index):
        for name in ("core", "first", "second"):
            pl.semaphore_signal(free_sem.at[index], inc=1, device_id=place.partner[name], device_id_type=MESH)

    def second_step(rows):
        residual, grad_second = two[rows, :], one[rows, :]
        factor = lax.rsqrt(jnp.mean(residual * residual, -1, keepdims=True) + EPS)
        normal = residual * factor
        small_own[1:2, :] += jnp.sum(grad_second * normal, 0, keepdims=True)
        scaled = grad_second * gain_ref[1:2, :]
        residual_grad = grad[rows, :].astype(F32) + factor * (
            scaled - normal * jnp.mean(scaled * normal, -1, keepdims=True)
        )
        one[rows, :] = residual_grad
        own_rows[rows, :] = residual_grad.astype(BF)
        both[rows, :] = residual_grad.astype(BF)

    branch = Gather(place, both, group, gather_send.at[3], gather_recv.at[3], own_rows)

    def feed_forward(hidden):
        place.locate()
        for s in range(SLICES):
            advance_through(s)
            lines[1 + s].arrived(count - 2)
            load_wide(w_forward.at[s], s).start()
            load_wide(w_forward.at[s], s).wait()

            def rows_step(b, _, s=s):
                rows = rows_at(b, block)
                gate_up = jnp.dot(second[rows, :], wide[:, :pair], preferred_element_type=F32)
                grad_hidden = jnp.dot(grad[rows, :], wide[:, pair:], preferred_element_type=F32)
                gate, up = gate_up[:, :slice_cols], gate_up[:, slice_cols:]
                sigmoid = 1.0 / (1.0 + jnp.exp(-gate))
                activated = gate * sigmoid
                hidden_rows = (activated * up).astype(BF)
                gate_rows = (grad_hidden * up * (sigmoid + activated * (1.0 - sigmoid))).astype(BF)
                up_rows = (grad_hidden * activated).astype(BF)
                hidden[rows, s * slice_cols : (s + 1) * slice_cols] = hidden_rows
                both[rows, s * pair : s * pair + slice_cols] = gate_rows
                both[rows, s * pair + slice_cols : (s + 1) * pair] = up_rows
                turned[:slice_cols, rows] = gate_rows.T
                turned[slice_cols:pair, rows] = up_rows.T
                turned[pair:, rows] = hidden_rows.T
                return 0

            lax.fori_loop(0, 4, rows_step, 0)
            advance(1)
            weight_grads(
                s, (0, pair), (pair, packed), (second, grad),
                (
                    (),
                    ((2, prepare, (0, "first")), (3, complete, (0, "first"))),
                    ((2, prepare, (0, "later")), (3, complete, (0, "later"))),
                    (
                        (0, prepare, (0, "total")), (1, complete, (0, "total")),
                        (2, prepare, (1, "first")), (3, complete, (1, "first")), (3, to_owner, (0,)),
                    ),
                )[s],
            )
            flush()
            sums[s].start()
            advance(1)

        def held(c, s):
            if c % 2 == 0:
                return wide.at[pl.ds(s * chunk, chunk), pl.ds(0, pair)]
            return turned.at[pl.ds(0, chunk), pl.ds(s * pair, pair)]

        def held_branch(c, s):
            return wide.at[pl.ds(s * chunk, chunk), pl.ds(pair if c % 2 == 0 else 0, slice_cols)]

        def chunk_loads(c, where, low, size):
            return [
                pltpu.make_async_copy(
                    w_forward.at[s, pl.ds(c * chunk, chunk), pl.ds(low, size)], where(c, s),
                    wide_sem.at[SLICES + (c % 2) * SLICES + s],
                )
                for s in range(SLICES)
            ]

        def summed(source, rows, step, where, c):
            return sum(
                lax.dot_general(
                    source[rows, s * step : (s + 1) * step], where(c, s)[...], NT, preferred_element_type=F32
                )
                for s in range(SLICES)
            )

        for copy in chunk_loads(0, held, 0, pair):
            copy.start()
        for c in range(4):
            if c < 3:
                for copy in chunk_loads(c + 1, held, 0, pair):
                    copy.start()
            for copy in chunk_loads(c, held, 0, pair):
                copy.wait()
            columns = pl.ds(c * chunk, chunk)

            def grad_rows(b, _, columns=columns, c=c):
                rows = rows_at(b, block)
                grad[rows, columns] = summed(both, rows, pair, held, c).astype(BF)
                return 0

            first = summed(both, pl.ds(0, block), pair, held, c)
            one[:, columns] = first[:group]
            grad[pl.ds(group, group), columns] = first[group:].astype(BF)
            lax.fori_loop(1, 4, grad_rows, 0)
            plane.push(c)
            if c >= 1:
                plane.middle(c - 1)
            if c >= 2:
                plane.late(c - 2)
            if c >= 3:
                plane.total(c - 3)
            if c == 1:
                prepare(1, "later")
            if c == 2:
                complete(1, "later")
        for copy in chunk_loads(0, held_branch, pair, slice_cols):
            copy.start()
        plane.middle(3)
        plane.late(2)
        plane.late(3)
        prepare(1, "total")
        for c in (1, 2, 3):
            plane.total(c)
        give_credit(0)
        complete(1, "total")
        small_own[...] = jnp.zeros_like(small_own)
        by_rows(second_step)
        branch.start()
        prepare(2, "first")
        for c in range(4):
            if c < 3:
                for copy in chunk_loads(c + 1, held_branch, pair, slice_cols):
                    copy.start()
            for copy in chunk_loads(c, held_branch, pair, slice_cols):
                copy.wait()

            def branch_rows(b, _, c=c):
                rows = rows_at(b, block)
                second[rows, pl.ds(c * chunk, chunk)] = summed(
                    hidden, rows, slice_cols, held_branch, c
                ).astype(BF)
                return 0

            lax.fori_loop(0, 4, branch_rows, 0)
            if c == 0:
                complete(2, "first")
            if c == 2:
                branch.step(1)

    pl.run_scoped(feed_forward, pltpu.VMEM((tokens, SLICES * slice_cols), BF))
    place.locate()
    w_load = load_wide(w_attention, 0)
    w_load.start()

    outer = PlaneSum(place, second, two, got, sum_send.at[2], sum_recv.at[2], width)

    def rows_add(target, first_row, rows, sources):
        def step(b, _):
            at = rows_at(b, group)
            to = pl.ds(pl.multiple_of(first_row + b * group, group), group)
            value = target[to, :].astype(F32)
            for source in sources:
                value = value + source[to, :].astype(F32)
            target[to, :] = value.astype(BF)
            return 0

        lax.fori_loop(0, rows // group, step, 0)

    pl.semaphore_wait(free_sem.at[0], 3)
    outer.push(0)
    for c in range(4):
        plane.sent(c)
    marks = [0, q_cols, q_cols + k_cols, qkv_cols, qkv_cols + q_cols, qkv_cols + 2 * q_cols]
    arrays = [local(heads_out, grad.at[:, pl.ds(0, packed)], load_sem.at[5])]
    for copy in arrays:
        copy.start()
    q_ref, k_ref = grad.at[:, pl.ds(0, q_cols)], grad.at[:, pl.ds(marks[1], k_cols)]
    v_ref, attended = grad.at[:, pl.ds(marks[2], k_cols)], grad.at[:, pl.ds(marks[3], q_cols)]
    attended_grad, qkv_grad = grad.at[:, pl.ds(marks[4], q_cols)], grad.at[:, pl.ds(marks[5], qkv_cols)]
    prepare(2, "later")
    w_load.wait()

    def attended_step(p, _):
        rows = rows_at(p, group)
        attended_grad[rows, :] = jnp.dot(
            both[rows, :], wide[:, qkv_cols:], preferred_element_type=F32
        ).astype(BF)
        return 0

    for copy in arrays:
        copy.wait()
    lax.fori_loop(0, 2, attended_step, 0)
    branch.step(2)
    branch.step(3)
    outer.move(0, 0).wait_recv()
    rows_add(second, 2 * group, 2 * group, (got_core,))
    outer.move(1, 0).start()
    lax.fori_loop(2, 4, attended_step, 0)
    complete(2, "later")
    for p in range(4):
        branch.arrived(p)

    def attended_block(b, _):
        rows = rows_at(b, block)
        attended_grad[rows, :] = jnp.dot(
            both[rows, :], wide[:, qkv_cols:], preferred_element_type=F32
        ).astype(BF)
        return 0

    lax.fori_loop(2, 4, attended_block, 0)

    def outer_late():
        outer.move(1, 0).wait_recv()
        rows_add(second, group, group, (got_core, got_first))
        outer.move(2, 0).start()
        prepare(2, "total")

    def attention(table, aux, key_sum, value_sum):
        place.locate()
        table_load = pltpu.make_async_copy(table_out, table, load_sem.at[9])
        aux_load = pltpu.make_async_copy(aux_out, aux, load_sem.at[10])
        table_load.start()
        aux_load.start()
        table_load.wait()
        aux_load.wait()
        attend_back_blocks(
            place, q_ref, k_ref, v_ref, aux, marks_ref, attended_grad, table, qkv_grad, key_sum, value_sum,
            outer_late,
        )

    pl.run_scoped(
        attention,
        pltpu.VMEM((tokens, HEAD_SIZE), F32), pltpu.VMEM((tokens, HEAD_SIZE), F32),
        pltpu.VMEM((tokens, k_cols), F32), pltpu.VMEM((tokens, k_cols), F32),
    )
    place.locate()
    branch.sent()
    to_owner(1)
    complete(2, "total")
    to_owner(2)
    prepare(3, "first")

    def turn_rows(source, first, last):
        def step(b, _):
            rows = rows_at(b, group)
            turned[first:last, rows] = source[rows, :].T
            return 0

        lax.fori_loop(0, 8, step, 0)

    turn_rows(attended, qkv_cols, packed)
    weight_grads(SLICES, (qkv_cols,), (packed,), (both,))
    flush()
    sums[SLICES].start()
    normed_load = pltpu.make_async_copy(normed_out, both, load_sem.at[2])
    normed_load.start()
    complete(3, "first")
    turn_rows(qkv_grad, 0, qkv_cols)
    normed_load.wait()
    outer.move(2, 0).wait_recv()

    def output_step(rows):
        own_rows[rows, :] = (
            two[rows, :]
            + second[rows, :].astype(F32)
            + got_core[rows, :].astype(F32)
            + got_first[rows, :].astype(F32)
            + got_second[rows, :].astype(F32)
        ).astype(BF)

    by_rows(output_step)
    give_credit(1)
    blocks = HalfGather(place, own_rows, block_output, half_send.at[0], half_recv.at[0], load_sem.at[3])
    blocks.start()
    prepare(3, "later")

    outer.sent(0)
    pl.semaphore_wait(free_sem.at[1], 3)
    inner = PlaneSum(place, second, two, got, sum_send.at[3], sum_recv.at[3], chunk)
    for c in range(4):
        columns = pl.ds(c * chunk, chunk)

        def first_part(rows, c=c):
            return lax.dot_general(
                qkv_grad[rows, :], wide[c * chunk : (c + 1) * chunk, :qkv_cols], NT, preferred_element_type=F32
            )

        def first_rows(b, _, columns=columns, first_part=first_part):
            rows = rows_at(b, block)
            second[rows, columns] = first_part(rows).astype(BF)
            return 0

        first = first_part(pl.ds(0, block))
        two[:, columns] = first[:group]
        second[pl.ds(group, group), columns] = first[group:].astype(BF)
        lax.fori_loop(1, 4, first_rows, 0)
        inner.push(c)
        if c == 0:
            complete(3, "later")
        if c == 1:
            prepare(SLICES, "first")
        if c == 2:
            complete(SLICES, "first")
        weight_grads_chunk(SLICES, (0,), (qkv_cols,), (both,), c)
        inner.middle(c)
        if c >= 1:
            inner.late(c - 1)
        if c >= 2:
            inner.total(c - 2)
    flush()
    sums[SLICES + 1].start()
    prepare(3, "total")
    inner.late(3)
    complete(3, "total")
    inner.total(2)
    prepare(SLICES, "later")
    blocks.step()
    complete(SLICES, "later")
    inner.total(3)
    to_owner(3)
    input_load = pltpu.make_async_copy(
        block_input.at[rows_at(place.tensor, group)], second.at[pl.ds(0, group)], load_sem.at[4]
    )
    input_load.start()
    input_load.wait()

    def first_step(rows):
        value, grad_first = second[rows, :].astype(F32), two[rows, :]
        factor = lax.rsqrt(jnp.mean(value * value, -1, keepdims=True) + EPS)
        normal = value * factor
        small_own[0:1, :] += jnp.sum(grad_first * normal, 0, keepdims=True)
        scaled = grad_first * gain_ref[0:1, :]
        input_grad = one[rows, :] + factor * (scaled - normal * jnp.mean(scaled * normal, -1, keepdims=True))
        second[rows, :] = input_grad.astype(BF)

    by_rows(first_step)
    prepare(SLICES + 1, "first")
    gradients = HalfGather(
        place, second.at[pl.ds(0, group)], input_gradient, half_send.at[1], half_recv.at[1], load_sem.at[4]
    )
    gradients.start()
    complete(SLICES + 1, "first")

    for index, name in enumerate(("core", "y", "x")):
        move = place.copy(
            small_own.at[pl.ds(8 * index, 8)], small_got.at[index], small_send.at[index], small_recv.at[index], name
        )
        move.start()
        move.wait_recv()
        value = small_own[8 * index : 8 * index + 8, :] + small_got[index]
        if index < 2:
            small_own[8 * index + 8 : 8 * index + 16, :] = value
        else:
            small_all[place.sequence] = value
    gain_line = Line(place, lambda k: small_all.at[k], gain_send, gain_recv)
    gain_line.start(0)
    prepare(SLICES, "total")
    gradients.step()
    complete(SLICES, "total")
    to_owner(SLICES)
    for stage in range(count - 1):
        gain_line.arrived(stage)
        if stage < count - 2:
            gain_line.start(stage + 1)
    own_columns = pl.ds(pl.multiple_of(place.sequence * shard2, shard2), shard2)
    gain_out[...] = sum(small_all[k, :, own_columns] for k in range(count))
    prepare(SLICES + 1, "later")
    complete(SLICES + 1, "later")
    prepare(SLICES + 1, "total")
    complete(SLICES + 1, "total")
    to_owner(SLICES + 1)

    flush()
    for line in lines[1:]:
        for stage in range(count - 1):
            line.sent(stage)
    if gains_here:
        for stage in range(count - 1):
            gain_shards.sent(stage)
    for index in (1, 2, 3) if gains_here else (1, 2):
        early(index).wait_send()
    for item, item_sum in enumerate(sums):
        item_sum.sent(item == SLICES + 1)
    for index in range(len(sum_items)):
        keep, swap = owner_moves(index)
        keep.wait()
        swap.wait()
    for c in range(4):
        inner.sent(c)
    for index, name in enumerate(("core", "y", "x")):
        place.copy(
            small_own.at[pl.ds(8 * index, 8)], small_got.at[index], small_send.at[index], small_recv.at[index], name
        ).wait_send()
    for stage in range(count - 1):
        gain_line.sent(stage)
    blocks.end()
    gradients.end()


def rotation(table):
    other = pltpu.roll(table, HEAD_SIZE // 2, 1)
    low = lax.broadcasted_iota(jnp.int32, table.shape, 1) < HEAD_SIZE // 2
    return jnp.where(low, table, other), jnp.where(low, -other, table)


def attend_back_blocks(
    place, q_ref, k_ref, v_ref, aux, columns_ref, grad_ref, table, out_ref, key_sum, value_sum, late
):
    block = q_ref.shape[0] // 8
    scale = 1.0 / math.sqrt(HEAD_SIZE)
    q_cols, k_cols = q_ref.shape[1], k_ref.shape[1]
    key_sum[...] = jnp.zeros_like(key_sum)
    value_sum[...] = jnp.zeros_like(value_sum)
    for at in range(8):
        low, high = key_range(at, block)
        here = slice(at * block, high)
        span = slice(low, high)
        allowed = allowed_pairs(aux, columns_ref, at, block)
        keys, values = k_ref[span, :], v_ref[span, :]
        cosine, sine = rotation(table[here, :])
        to = rows_at(place.of_group(at), block)
        for head in range(q_cols // HEAD_SIZE):
            columns = slice(head * HEAD_SIZE, (head + 1) * HEAD_SIZE)
            rows = q_ref[here, columns]
            grad_rows = grad_ref[to, columns]
            scores = lax.dot_general(rows, keys, NT, preferred_element_type=F32) * scale
            scores = jnp.where(allowed, scores, NEGATIVE)
            probs = jnp.exp(scores - aux[here, 1 + head : 2 + head])
            value_sum[span, :] += lax.dot_general(
                probs.astype(BF), grad_rows, TN, preferred_element_type=F32
            )
            prob_grad = lax.dot_general(grad_rows, values, NT, preferred_element_type=F32)
            inner = jnp.sum(probs * prob_grad, -1, keepdims=True)
            score_grad = (probs * (prob_grad - inner)).astype(BF)
            query_grad = jnp.dot(score_grad, keys, preferred_element_type=F32) * scale
            key_sum[span, :] += lax.dot_general(score_grad, rows, TN, preferred_element_type=F32)
            out_ref[to, columns] = turn(query_grad, cosine, -sine).astype(BF)
        if at == 5:
            late()
    for at in range(8):
        here = slice(at * block, (at + 1) * block)
        cosine, sine = rotation(table[here, :])
        to = rows_at(place.of_group(at), block)
        out_ref[to, q_cols : q_cols + k_cols] = turn(key_sum[here, :] * scale, cosine, -sine).astype(BF)
        out_ref[to, q_cols + k_cols :] = value_sum[here, :].astype(BF)


def layer(block_input, out_grad, gains, table, marks, masters, count):
    half_tokens, width = block_input.shape
    group, tokens = half_tokens // 4, 2 * half_tokens
    shard = masters[0].shape[0]
    q_cols, k_cols = masters[0].shape[1] // 2, masters[1].shape[1] // 2
    slice_cols = masters[4].shape[1] // 2 // SLICES
    packed = 3 * slice_cols
    assert packed == 2 * q_cols + 2 * k_cols and q_cols == group >= shard
    gains_here = shard % 128 == 0
    if not gains_here:
        gains = lax.all_gather(gains, "dp", axis=1, tiled=True)
    part = shard if gains_here else 2 * shard
    vmem, hbm = pl.BlockSpec(memory_space=pltpu.VMEM), pl.BlockSpec(memory_space=pl.ANY)
    struct = jax.ShapeDtypeStruct
    dma = pltpu.SemaphoreType.DMA
    items = 1 + SLICES
    return pl.pallas_call(
        functools.partial(layer_kernel, count, gains_here),
        in_specs=[hbm, hbm, vmem, hbm, vmem] + [hbm] * 7,
        out_specs=[hbm] * 3 + [vmem] + [hbm] * 9,
        out_shape=[
            struct((half_tokens, width), BF),
            struct((half_tokens, width), BF),
            struct((2, items, packed, part), BF),
            struct((8, 2 * shard), F32),
            struct((items, packed, width), BF),
            struct((items, 2, count - 1, packed, 2 * shard), BF),
            struct((items, packed, 2 * shard), BF),
            struct((width, packed), BF),
            struct((SLICES, width, packed), BF),
            struct((tokens, width), BF),
            struct((tokens, packed), BF),
            struct((tokens, HEAD_SIZE), F32),
            struct((tokens, HEAD_SIZE), F32),
        ],
        scratch_shapes=[
            pltpu.VMEM((tokens, width), BF),
            pltpu.VMEM((tokens, width), BF),
            pltpu.VMEM((tokens, width), BF),
            pltpu.VMEM((width, packed), BF),
            pltpu.VMEM((4 * group, width), BF),
            pltpu.VMEM((2 * group, width), BF),
            pltpu.VMEM((group, width), BF),
            pltpu.VMEM((4, packed, 2 * shard), BF),
            pltpu.VMEM((count - 1, packed, 2 * shard), BF),
            pltpu.VMEM((2, packed, width // 4), BF),
            pltpu.VMEM((packed, tokens), BF),
            pltpu.VMEM((group, width), F32),
            pltpu.VMEM((group, width), F32),
            pltpu.VMEM((group, width), BF),
            pltpu.VMEM((24, width), F32),
            pltpu.VMEM((3, 8, width), F32),
            pltpu.VMEM((count, 8, width), F32),
            pltpu.VMEM((8, width), F32),
            pltpu.VMEM((8, tokens), F32),
            dma((12,)),
            dma((3 * SLICES,)),
            dma((2,)),
            dma((1 + items,)),
            dma((1 + items,)),
            dma((1 + items, 2, count - 1)),
            dma((1 + items, 2, count - 1)),
            dma((4, 3, 8)),
            dma((4, 3, 8)),
            dma((4, 7)),
            dma((4, 7)),
            dma((2, 3)),
            dma((2, 3)),
            dma((3,)),
            dma((3,)),
            dma((2, count - 1)),
            dma((2, count - 1)),
            pltpu.SemaphoreType.REGULAR((2,)),
            dma((4,)),
            dma((1 + items,)),
            dma((4,)),
            dma((4,)),
            dma((SLICES, 2)),
            dma((SLICES, 2)),
            dma((2 + items, 2, count - 1)),
            dma((2 + items, 2, count - 1)),
            dma((5,)),
            dma((SLICES, 2)),
            dma((4,)),
        ],
        compiler_params=pltpu.CompilerParams(
            vmem_limit_bytes=VMEM_LIMIT, collective_id=0, has_side_effects=True
        ),
        name="layer",
    )(block_input, out_grad, gains, table, marks, *masters)


def adamw(weight, gradient, first, second, rate, decay):
    first_new = BETA_ONE * first + (1.0 - BETA_ONE) * gradient
    second_new = BETA_TWO * second + (1.0 - BETA_TWO) * gradient * gradient
    bias_first = 1.0 - BETA_ONE**STEP
    bias_second = 1.0 - BETA_TWO**STEP
    moved = first_new * (1.0 / bias_first) / (jnp.sqrt(second_new * (1.0 / bias_second)) + ADAM_EPS)
    return (weight - rate * (moved + decay * weight), first_new, second_new)


def update_kernel(attention_cuts, forward_cuts, *refs):
    a, f = 12, 9
    attention_share, forward_share, block_in, gradient_in = refs[:4]
    states, outs = refs[4 : 4 + a + f], refs[4 + a + f :]
    outs[0][...] = block_in[...]
    outs[1][...] = gradient_in[...].astype(F32)

    def one(gradient, arrays, results, at):
        fresh = adamw(arrays[0][at], gradient, arrays[1][at], arrays[2][at], RATE_MATRIX, DECAY)
        for result, value in zip(results, fresh):
            result[at] = value

    everything = (slice(None), slice(None))
    for i in range(3):
        gradient = forward_share[forward_cuts[i] : forward_cuts[i + 1], :].astype(F32)
        one(gradient if i == 2 else gradient.T, states[a + i :: 3][:3], outs[2 + a + i :: 3][:3], everything)

    @pl.when(pl.program_id(0) == 0)
    def _():
        for i in range(4):
            for side in range(2):
                low, high = attention_cuts[i], attention_cuts[i + 1]
                gradient = attention_share[side, low:high, :].astype(F32)
                span = slice(side * (high - low), (side + 1) * (high - low))
                if i == 3:
                    one(gradient, states[i:a:4], outs[2 + i : 2 + a : 4], (span, slice(None)))
                else:
                    one(gradient.T, states[i:a:4], outs[2 + i : 2 + a : 4], (slice(None), span))


def update(shares, block_output, input_gradient, attention_cuts, attention, forward_cuts, feed):
    packed, part = shares.shape[2:]
    steps = 2 * SLICES

    def rows_block(array):
        return pl.BlockSpec((array.shape[0] // steps, array.shape[1]), lambda g: (g, 0))

    def columns_block(array):
        return pl.BlockSpec((array.shape[0], array.shape[1] // steps), lambda g: (0, g))

    state_specs = [pl.BlockSpec(array.shape, lambda g: (0, 0)) for array in attention]
    state_specs += [rows_block(array) if i % 3 == 2 else columns_block(array) for i, array in enumerate(feed)]
    plain = [rows_block(block_output), rows_block(input_gradient)]
    return pl.pallas_call(
        functools.partial(update_kernel, attention_cuts, forward_cuts),
        grid=(steps,),
        in_specs=[
            pl.BlockSpec((2, None, packed, part), lambda g: (0, SLICES, 0, 0)),
            pl.BlockSpec((None, None, packed, part), lambda g: (g // SLICES, g % SLICES, 0, 0)),
        ]
        + plain
        + state_specs,
        out_specs=plain + state_specs,
        out_shape=[
            jax.ShapeDtypeStruct(block_output.shape, BF),
            jax.ShapeDtypeStruct(input_gradient.shape, F32),
        ]
        + [jax.ShapeDtypeStruct(array.shape, F32) for array in (*attention, *feed)],
        compiler_params=pltpu.CompilerParams(vmem_limit_bytes=VMEM_LIMIT),
        name="update",
    )(shares, shares, block_output, input_gradient, *attention, *feed)


def rotary_tables(positions):
    half = HEAD_SIZE // 2
    frequency = THETA ** (-2.0 * jnp.arange(half, dtype=F32) / HEAD_SIZE)
    angles = positions.astype(F32)[:, None] * frequency[None, :]
    cosine, sine = jnp.cos(angles), jnp.sin(angles)
    return jnp.concatenate([cosine, sine], -1)


def local(
    block_input, out_grad, segments, positions,
    w_query, w_key, w_value, w_output, w_gate, w_up, w_down, gains,
    m_query, m_key, m_value, m_output, m_gate, m_up, m_down, m_gains,
    v_query, v_key, v_value, v_output, v_gate, v_up, v_down, v_gains,
):
    half_tokens = block_input.shape[0]
    rows = w_query.shape[0]
    sequences = lax.axis_size("dp") // 2
    half = lax.axis_index("dp") % 2
    table = rotary_tables(positions)
    marks = jnp.broadcast_to(segments.astype(F32)[None, :], (8, half_tokens))
    gain_rows = jnp.pad(gains.astype(BF).astype(F32), ((0, 6), (0, 0)))
    masters = (w_query, w_key, w_value, w_output, w_gate, w_up, w_down)
    block_output, input_gradient, shares, gain_grads = layer(
        block_input, out_grad, gain_rows, table, marks, masters, sequences
    )[:4]
    if shares.shape[-1] != rows:
        shares = lax.dynamic_slice_in_dim(shares, half * rows, rows, 3)
    q_cols, k_cols, o_cols = w_query.shape[1] // 2, w_key.shape[1] // 2, w_output.shape[0] // 2
    slice_cols = w_gate.shape[1] // 2 // SLICES

    def cuts(*sizes):
        return [sum(sizes[:i]) for i in range(len(sizes) + 1)]

    block_output, input_gradient, *fresh = update(
        shares, block_output, input_gradient,
        cuts(q_cols, k_cols, k_cols, o_cols),
        (w_query, w_key, w_value, w_output, m_query, m_key, m_value, m_output, v_query, v_key, v_value, v_output),
        cuts(slice_cols, slice_cols, slice_cols),
        (w_gate, w_up, w_down, m_gate, m_up, m_down, v_gate, v_up, v_down),
    )
    attention_new, forward_new = fresh[:12], fresh[12:]
    gain_grads = lax.dynamic_slice_in_dim(gain_grads[:2], half * rows, rows, 1)
    gains_new = adamw(gains, gain_grads, m_gains, v_gains, RATE_GAIN, 0.0)
    new = [
        list(attention_new[4 * part : 4 * part + 4]) + list(forward_new[3 * part : 3 * part + 3]) + [gains_new[part]]
        for part in range(3)
    ]
    return tuple([block_output, input_gradient] + new[0] + new[1] + new[2])


def solution(mesh):
    matrices = [P("dp", "tensor")] * 3 + [P("tensor", "dp")] + [P("dp", "tensor")] * 2 + [P("tensor", "dp")]
    state = tuple(matrices + [P(None, "dp")])
    rows = (P("dp", None), P("dp", None))
    return jax.shard_map(
        local,
        mesh=mesh,
        in_specs=rows + (P("dp"), P("dp")) + state * 3,
        out_specs=rows + state * 3,
        check_vma=False,
    )
```

```python
import functools
import math

import jax
import jax.numpy as jnp
from jax import lax
from jax.experimental import pallas as pl
from jax.experimental.pallas import tpu as pltpu
from jax.sharding import PartitionSpec as P

HEAD_SIZE = 128
WINDOW = 1024
STEP = 5
EPS = 1e-06
THETA = 1000000.0
BETA_ONE = 0.5
BETA_TWO = 0.5
RATE_MATRIX = 0.02
RATE_GAIN = 0.3
DECAY = 0.1
ADAM_EPS = 1e-08
NEGATIVE = -1e30
SLICES = 4
BF = jnp.bfloat16
F32 = jnp.float32
VMEM_LIMIT = 63 * 1024 * 1024
MESH = pl.DeviceIdType.MESH


class Place:
    def __init__(self, sequences):
        self.count = sequences
        self.locate()

    def locate(self):
        self.dp, self.tensor = lax.axis_index("dp"), lax.axis_index("tensor")
        self.sequence, self.half = self.dp // 2, self.dp % 2
        self.y, self.core = self.tensor // 2, self.tensor % 2
        across = 1 - 2 * self.half
        beside = 2 - 4 * self.y
        self.partner = {
            "core": (self.dp, self.tensor + 1 - 2 * self.core),
            "x": (self.dp + across, self.tensor),
            "y": (self.dp, self.tensor + beside),
            "first": (self.dp + (1 - self.core) * across, self.tensor + self.core * beside),
            "second": (self.dp + self.core * across, self.tensor + (1 - self.core) * beside),
            "right": (self.dp + 2, self.tensor),
            "left": (self.dp - 2, self.tensor),
        }

    def of_group(self, g):
        dh = (g // 4 + self.half) % 2
        dy = ((g // 2) % 2 + self.y) % 2
        dc = (g % 2 + self.core) % 2
        from_core = (self.core + dc) % 2
        straight = dh * 2 + dy
        return dc * 4 + straight + from_core * (dy * 2 + dh - straight)

    def greet(self):
        barrier = pltpu.get_barrier_semaphore()
        for name in ("core", "x", "y"):
            pl.semaphore_signal(barrier, inc=1, device_id=self.partner[name], device_id_type=MESH)

        @pl.when(self.sequence >= 1)
        def _():
            pl.semaphore_signal(barrier, inc=1, device_id=self.partner["left"], device_id_type=MESH)

        @pl.when(self.sequence <= self.count - 2)
        def _():
            pl.semaphore_signal(barrier, inc=1, device_id=self.partner["right"], device_id_type=MESH)

        ends = (self.sequence + self.count - 1) // self.count + (2 * self.count - 2 - self.sequence) // self.count
        pl.semaphore_wait(barrier, 3 + ends)

    def copy(self, source, target, send, recv, name):
        return pltpu.make_async_remote_copy(
            src_ref=source, dst_ref=target, send_sem=send, recv_sem=recv,
            device_id=self.partner[name], device_id_type=MESH,
        )


class Gather:
    moves = [("second", 0, 1), ("first", 0, 2), ("first", 1, 3)] + [("core", p, p + 4) for p in range(4)]

    def __init__(self, place, buffer, group, send, recv, own=None):
        self.place, self.buffer, self.group = place, buffer, group
        self.send, self.recv, self.own = send, recv, own

    def at(self, index):
        return self.buffer.at[pl.ds(index * self.group, self.group)]

    def copy(self, index):
        name, source, target = self.moves[index]
        source = self.own if self.own is not None and source == 0 else self.at(source)
        return self.place.copy(source, self.at(target), self.send.at[index], self.recv.at[index], name)

    def start(self):
        for index in (0, 1, 3):
            self.copy(index).start()

    def step(self, index):
        if index == 1:
            self.copy(0).wait_recv()
            self.copy(2).start()
            self.copy(4).start()
        else:
            self.copy(index - 1).wait_recv()
            self.copy(index + 3).start()

    def arrived(self, index):
        self.copy(3 + index).wait_recv()

    def sent(self):
        for index in range(7):
            self.copy(index).wait_send()


class Line:
    def __init__(self, place, slot, send, recv):
        self.place, self.slot = place, slot
        self.sends, self.recvs = send, recv

    def move(self, way, stage):
        place = self.place
        shard = place.sequence - stage if way == 0 else place.sequence + stage
        target = self.slot(shard)
        name = "right" if way == 0 else "left"
        return place.copy(target, target, self.sends.at[way, stage], self.recvs.at[way, stage], name)

    def conditions(self, stage):
        place = self.place
        last = place.count - 1
        sends = (
            (place.sequence >= stage) & (place.sequence <= last - 1),
            (place.sequence <= last - stage) & (place.sequence >= 1),
        )
        recvs = (place.sequence >= stage + 1, place.sequence <= last - 1 - stage)
        return sends, recvs

    def start(self, stage):
        for way, condition in enumerate(self.conditions(stage)[0]):
            @pl.when(condition)
            def _(way=way):
                self.move(way, stage).start()

    def arrived(self, stage):
        for way, condition in enumerate(self.conditions(stage)[1]):
            @pl.when(condition)
            def _(way=way):
                place = self.place
                shard = place.sequence - 1 - stage if way == 0 else place.sequence + 1 + stage
                target = self.slot(shard)
                place.copy(
                    target, target, self.sends.at[way, stage], self.recvs.at[way, stage],
                    "right" if way == 0 else "left",
                ).wait_recv()

    def sent(self, stage):
        for way, condition in enumerate(self.conditions(stage)[0]):
            @pl.when(condition)
            def _(way=way):
                self.move(way, stage).wait_send()


def turn(head, cosine, sine):
    return head * cosine + pltpu.roll(head, HEAD_SIZE // 2, 1) * sine


def key_range(block_at, block):
    low = max(0, block_at * block - WINDOW + 1) // block * block
    return low, (block_at + 1) * block


def allowed_pairs(segment_rows, segment_columns, block_at, block):
    low, high = key_range(block_at, block)
    shape = (block, high - low)
    distance = (
        lax.broadcasted_iota(jnp.int32, shape, 0)
        - lax.broadcasted_iota(jnp.int32, shape, 1)
        + (block_at * block - low)
    )
    same = segment_rows[block_at * block : high, 0:1] == segment_columns[0:1, low:high]
    return same & (distance >= 0) & (distance < WINDOW)


NT = (((1,), (1,)), ((), ()))
TN = (((0,), (0,)), ((), ()))


def rows_at(index, size):
    return pl.ds(pl.multiple_of(index * size, size), size)


def group_at(place, p):
    dc = p // 4
    from_core = (place.core + dc) % 2
    one, two = (p // 2) % 2, p % 2
    dh = one + from_core * (two - one)
    dy = two + from_core * (one - two)
    return ((dh + place.half) % 2) * 4 + ((dy + place.y) % 2) * 2 + (dc + place.core) % 2


def attend_blocks(place, heads, q_cols, k_cols, aux, columns_ref, between):
    block = heads.shape[0] // 8
    qkv_cols = q_cols + 2 * k_cols
    scale = 1.0 / math.sqrt(HEAD_SIZE)
    for at in range(8):
        low, high = key_range(at, block)
        allowed = allowed_pairs(aux, columns_ref, at, block)
        keys, values = heads[low:high, q_cols : q_cols + k_cols], heads[low:high, q_cols + k_cols : qkv_cols]
        to = rows_at(place.of_group(at), block)
        for head in range(q_cols // HEAD_SIZE):
            columns = slice(head * HEAD_SIZE, (head + 1) * HEAD_SIZE)
            rows = heads[at * block : high, columns]
            scores = lax.dot_general(rows, keys, NT, preferred_element_type=F32) * scale
            scores = jnp.where(allowed, scores, NEGATIVE)
            top = jnp.max(scores, -1, keepdims=True)
            weights = jnp.exp(scores - top)
            total = jnp.sum(weights, -1, keepdims=True)
            probs = (weights * (1.0 / total)).astype(BF)
            heads[to, qkv_cols + columns.start : qkv_cols + columns.stop] = jnp.dot(
                probs, values, preferred_element_type=F32
            ).astype(BF)
            aux[at * block : high, 1 + head : 2 + head] = top + jnp.log(total)
        between(at)


class LineSum:
    def __init__(self, place, item, rows, index, own, recv, loads, ring, send_sem, recv_sem, load_sem, before):
        self.place, self.item, self.index, self.own, self.recv = place, item, index, own, recv
        self.rows = pl.ds(*rows)
        self.loads, self.ring = loads.at[:, self.rows], ring.at[:, self.rows]
        self.send_sem, self.recv_sem, self.load_sem = send_sem, recv_sem, load_sem
        self.before = before
        self.width = recv.shape[-1]

    def own_part(self, d):
        return self.own.at[self.item, self.rows, pl.ds(pl.multiple_of(d * self.width, self.width), self.width)]

    def dest(self, way, j):
        return self.place.count - 1 - j if way == 0 else j

    def move(self, way, j, source):
        return self.place.copy(
            source, self.recv.at[self.item, way, j, self.rows],
            self.send_sem.at[self.index, way, j], self.recv_sem.at[self.index, way, j],
            "right" if way == 0 else "left",
        )

    def start(self):
        last = self.place.count - 1
        for way, end in ((0, 0), (1, last)):
            @pl.when(self.place.sequence == end)
            def _(way=way):
                for j in range(last):
                    self.move(way, j, self.own_part(self.dest(way, j))).start()

    def turn_of(self, way, stage):
        depth = self.place.sequence if way == 0 else self.place.count - 1 - self.place.sequence
        return (depth >= 1) & (depth <= stage - 1), stage - 1 - depth, depth

    def slot(self, way, j):
        return j if way == 0 else self.place.count - 1 - self.place.sequence + j

    def own_load(self, way, d):
        return pltpu.make_async_copy(self.own_part(d), self.loads.at[2 * way], self.load_sem.at[2 * way])

    def came_load(self, way, j):
        return pltpu.make_async_copy(
            self.recv.at[self.item, way, j, self.rows], self.loads.at[2 * way + 1], self.load_sem.at[2 * way + 1]
        )

    def prepare(self, stage):
        for way in (0, 1):
            condition, j, _ = self.turn_of(way, stage)

            @pl.when(condition)
            def _(way=way, j=j):
                self.own_load(way, self.dest(way, j)).start()
                self.move(way, j, self.ring.at[self.slot(way, j)]).wait_recv()
                self.came_load(way, j).start()

    def service(self, stage):
        for way in (0, 1):
            condition, j, _ = self.turn_of(way, stage)

            @pl.when(condition)
            def _(way=way, j=j):
                slot = self.slot(way, j)
                if self.before is not None:
                    self.before.move(way, j, self.before.ring.at[slot]).wait_send()
                self.own_load(way, self.dest(way, j)).wait()
                self.came_load(way, j).wait()
                self.ring[slot] = (self.loads[2 * way].astype(F32) + self.loads[2 * way + 1].astype(F32)).astype(BF)
                self.move(way, j, self.ring.at[slot]).start()

    def last(self, way):
        place = self.place
        if way == 0:
            return place.sequence >= 1, place.count - 1 - place.sequence
        return place.sequence <= place.count - 2, place.sequence

    def prepare_total(self):
        self.own_load(0, self.place.sequence).start()
        for way in (0, 1):
            condition, j = self.last(way)

            @pl.when(condition)
            def _(way=way, j=j):
                self.move(way, j, self.loads.at[2 * way + 1]).wait_recv()
                self.came_load(way, j).start()

            @pl.when(jnp.logical_not(condition))
            def _(way=way):
                self.loads[2 * way + 1] = jnp.zeros(self.loads.shape[1:], BF)

    def total(self, out):
        self.own_load(0, self.place.sequence).wait()
        for way in (0, 1):
            condition, j = self.last(way)

            @pl.when(condition)
            def _(way=way, j=j):
                self.came_load(way, j).wait()

        out[...] = (
            self.loads[0].astype(F32) + self.loads[1].astype(F32) + self.loads[3].astype(F32)
        ).astype(BF)

    def sent(self, last_item):
        last = self.place.count - 1
        for way, end in ((0, 0), (1, last)):
            @pl.when(self.place.sequence == end)
            def _(way=way):
                for j in range(last):
                    self.move(way, j, self.own_part(self.dest(way, j))).wait_send()

        if last_item:
            for stage in range(2, last + 1):
                for way in (0, 1):
                    condition, j, _ = self.turn_of(way, stage)

                    @pl.when(condition)
                    def _(way=way, j=j):
                        self.move(way, j, self.ring.at[self.slot(way, j)]).wait_send()


class PlaneSum:
    def __init__(self, place, part, own, got, send_sem, recv_sem, chunk):
        self.place, self.part, self.own, self.got = place, part, own, got
        self.send_sem, self.recv_sem, self.chunk = send_sem, recv_sem, chunk
        self.group = own.shape[0]

    def columns(self, c):
        return pl.ds(c * self.chunk, self.chunk)

    def move(self, step, c):
        group, columns = self.group, self.columns(c)
        rows = ((4, 4), (2, 2), (1, 1))[step]
        name = ("core", "first", "second")[step]
        return self.place.copy(
            self.part.at[pl.ds(rows[0] * group, rows[1] * group), columns], self.got[step].at[:, columns],
            self.send_sem.at[step, c], self.recv_sem.at[step, c], name,
        )

    def push(self, c):
        self.move(0, c).start()

    def middle(self, c):
        self.move(0, c).wait_recv()
        rows, columns = pl.ds(2 * self.group, 2 * self.group), self.columns(c)
        self.part[rows, columns] = (
            self.part[rows, columns].astype(F32) + self.got[0][rows, columns].astype(F32)
        ).astype(BF)
        self.move(1, c).start()

    def late(self, c):
        self.move(1, c).wait_recv()
        rows, columns = pl.ds(self.group, self.group), self.columns(c)
        self.part[rows, columns] = (
            self.part[rows, columns].astype(F32)
            + self.got[0][rows, columns].astype(F32)
            + self.got[1][rows, columns].astype(F32)
        ).astype(BF)
        self.move(2, c).start()

    def total(self, c):
        self.move(2, c).wait_recv()
        rows, columns = pl.ds(0, self.group), self.columns(c)
        self.own[:, columns] = (
            self.own[:, columns]
            + self.got[0][rows, columns].astype(F32)
            + self.got[1][rows, columns].astype(F32)
            + self.got[2][:, columns].astype(F32)
        )

    def sent(self, c):
        for step in range(3):
            self.move(step, c).wait_send()


class HalfGather:
    def __init__(self, place, own, buffer, send, recv, local):
        self.place = place
        group = own.shape[0]
        tensor, across = place.tensor, place.tensor + 2 - 4 * place.y

        def at(index):
            return buffer.at[rows_at(index, group)]

        self.keep = pltpu.make_async_copy(own, at(tensor), local)
        self.y = place.copy(own, at(tensor), send.at[0], recv.at[0], "y")
        self.core = place.copy(own, at(tensor), send.at[1], recv.at[1], "core")
        self.far = place.copy(at(across), at(across), send.at[2], recv.at[2], "core")

    def start(self):
        self.keep.start()
        self.y.start()
        self.core.start()

    def step(self):
        self.y.wait_recv()
        self.far.start()

    def end(self):
        self.keep.wait()
        self.y.wait_send()
        self.core.wait()
        self.far.wait()


def layer_kernel(
    count, gains_here,
    block_input, out_grad, gains, table_half, marks_half,
    w_query, w_key, w_value, w_output, w_gate, w_up, w_down,
    block_output, input_gradient, shares, gain_out,
    own_grads, line_got, totals, w_attention, w_forward, normed_out, heads_out, table_out, aux_out,
    second, grad, both, wide, got_core, got_first, got_second, loads, ring, ready, turned,
    one, two, own_rows, small_own, small_got, small_all, gain_ref, marks_ref,
    load_sem, wide_sem, ready_sem, swap_send, swap_recv, line_send, line_recv, sum_send, sum_recv,
    gather_send, gather_recv, half_send, half_recv, small_send, small_recv, gain_send, gain_recv, free_sem,
    line_load_sem, owner_sem, early_send, early_recv, slice_send, slice_recv, shard_send, shard_recv, master_sem, keep_sem, out_sem,
):
    place = Place(count)
    group, width = own_rows.shape
    tokens = 8 * group
    packed = wide.shape[1]
    slice_cols = packed // 3
    pair = 2 * slice_cols
    shard = w_query.shape[0]
    q_cols, k_cols = w_query.shape[1] // 2, w_key.shape[1] // 2
    qkv_cols = q_cols + 2 * k_cols
    shard2 = line_got.shape[-1]
    part_width = shares.shape[-1]
    chunk = width // 8
    big = width // 4
    block = 2 * group
    got = (got_core, got_first, got_second)

    def load_wide(source, index):
        return pltpu.make_async_copy(source, wide, wide_sem.at[index])

    def shard_rows():
        return pl.ds(pl.multiple_of(place.dp * shard, shard), shard)

    def sequence_rows(k):
        return pl.ds(pl.multiple_of(k * 2 * shard, 2 * shard), 2 * shard)

    local = pltpu.make_async_copy

    masters = [
        local(w_query, one.at[pl.ds(0, shard), pl.ds(0, 2 * q_cols)], master_sem.at[0]),
        local(w_key, one.at[pl.ds(0, shard), pl.ds(2 * q_cols, 2 * k_cols)], master_sem.at[1]),
        local(w_value, one.at[pl.ds(0, shard), pl.ds(2 * q_cols + 2 * k_cols, 2 * k_cols)], master_sem.at[2]),
    ]
    own_loads = [
        local(block_input.at[rows_at(place.tensor, group)], both.at[pl.ds(0, group)], load_sem.at[2]),
        local(out_grad.at[rows_at(place.tensor, group)], grad.at[pl.ds(0, group)], load_sem.at[3]),
    ]
    table_keep = local(table_half, table_out.at[rows_at(place.half, 4 * group)], load_sem.at[4])
    for copy in masters + own_loads + [table_keep]:
        copy.start()
    marks_ref[:, rows_at(place.half, 4 * group)] = marks_half[...]

    def early(index):
        columns = rows_at(place.half, 4 * group)
        source, target = (
            (own_rows.at[pl.ds(0, shard), pl.ds(0, packed)], wide.at[shard_rows()]),
            (marks_half, marks_ref.at[:, columns]),
            (table_half, table_out.at[columns]),
            (gains, gain_ref.at[:, shard_rows()] if gains_here else None),
        )[index]
        return place.copy(source, target, early_send.at[index], early_recv.at[index], "x")

    def unit(s, theirs, part):
        k = 2 * s + theirs
        if part == 0:
            return pl.ds((k // 4) * slice_cols, shard), pl.ds((k % 4) * pair, pair)
        return pl.ds(pair, shard), pl.ds(k * slice_cols, slice_cols)

    def slice_target(s, part):
        return w_forward.at[s, shard_rows(), pl.ds(0, pair) if part == 0 else pl.ds(pair, slice_cols)]

    def slice_swap(s, part):
        return place.copy(
            turned.at[unit(s, 1, part)], slice_target(s, part), slice_send.at[s, part], slice_recv.at[s, part], "x"
        )

    def slice_keep(s, part):
        return local(turned.at[unit(s, 0, part)], slice_target(s, part), keep_sem.at[s, part])

    lines = [
        Line(
            place, lambda k: wide.at[sequence_rows(k), pl.ds(0, qkv_cols)], shard_send.at[0], shard_recv.at[0]
        )
    ] + [
        Line(
            place, lambda k, s=s: w_forward.at[s, sequence_rows(k)], shard_send.at[1 + s], shard_recv.at[1 + s]
        )
        for s in range(SLICES)
    ]
    output_line = Line(
        place, lambda k: wide.at[sequence_rows(k), pl.ds(qkv_cols, q_cols)],
        shard_send.at[2 + SLICES], shard_recv.at[2 + SLICES],
    )

    def output_steps(first, last):
        for stage in range(min(first, count - 1), min(last, count - 1)):
            output_line.arrived(stage)
            if stage < count - 2:
                output_line.start(stage + 1)

    gain_shards = Line(
        place, lambda k: gain_ref.at[:, sequence_rows(k)], shard_send.at[1 + SLICES], shard_recv.at[1 + SLICES]
    )

    begin = (0, 1, 2 * count - 4, 3 * count - 6.5)
    sends = sorted(
        ((s, stage) for s in range(SLICES) for stage in range(count - 1)),
        key=lambda item: (begin[item[0]] + 2 * item[1] + (item[1] > 0) * (item[0] >= 2) * 2, item[0]),
    )

    def advance(number):
        for _ in range(min(number, len(sends))):
            s, stage = sends.pop(0)
            if stage == 0:
                for part in range(2):
                    slice_swap(s, part).wait_recv()
            else:
                lines[1 + s].arrived(stage - 1)
            lines[1 + s].start(stage)

    def advance_through(s):
        while any(item[0] == s for item in sends):
            advance(1)

    place.greet()

    def attention_shard(output, target, rows, side):
        target[rows, :q_cols] = one[:shard, rows_at(side, q_cols)].astype(BF)
        for index in range(2):
            base = 2 * q_cols + 2 * k_cols * index
            target[rows, q_cols + k_cols * index : q_cols + k_cols * (index + 1)] = one[
                :shard, pl.ds(pl.multiple_of(base + side * k_cols, k_cols), k_cols)
            ].astype(BF)
        target[rows, qkv_cols:packed] = output[rows_at(side, q_cols), :].T.astype(BF)

    def fill_attention(output):
        place.locate()
        output_load = local(w_output, output, master_sem.at[3])
        output_load.start()
        for copy in masters + [output_load]:
            copy.wait()
        attention_shard(output, own_rows, slice(0, shard), 1 - place.half)
        early(0).start()
        attention_shard(output, wide, shard_rows(), place.half)

    pl.run_scoped(fill_attention, pltpu.VMEM(w_output.shape, F32))
    place.locate()
    masters = [
        local(w_gate, one.at[pl.ds(0, shard)], master_sem.at[0]),
        local(w_up, two.at[pl.ds(0, shard)], master_sem.at[1]),
    ]
    for copy in masters:
        copy.start()
    early(1).start()
    if gains_here:
        gain_ref[:, shard_rows()] = gains[...]
        early(3).start()
    else:
        gain_ref[...] = gains[...]
    inputs = Gather(place, both, group, gather_send.at[0], gather_recv.at[0])
    own_loads[0].wait()
    inputs.start()
    early(0).wait_recv()
    lines[0].start(0)
    if gains_here:
        early(3).wait_recv()
        gain_shards.start(0)

    def fill_slices(down):
        place.locate()
        down_load = local(w_down, down, master_sem.at[2])
        down_load.start()
        for copy in masters + [down_load]:
            copy.wait()
        for s in range(SLICES):
            for theirs in (1, 0):
                side = place.half + theirs - 2 * theirs * place.half
                columns = rows_at(side * SLICES + s, slice_cols)
                (rows, at), (down_rows, down_at) = unit(s, theirs, 0), unit(s, theirs, 1)
                turned[rows, pl.ds(at.start, slice_cols)] = one[:shard, columns].astype(BF)
                turned[rows, pl.ds(at.start + slice_cols, slice_cols)] = two[:shard, columns].astype(BF)
                turned[down_rows, down_at] = down[columns, :].T.astype(BF)
            for part in range(2):
                slice_keep(s, part).start()
            if s == 0:
                inputs.step(1)

    pl.run_scoped(fill_slices, pltpu.VMEM(w_down.shape, F32))
    place.locate()
    if gains_here:
        for stage in range(count - 1):
            gain_shards.arrived(stage)
            if stage < count - 2:
                gain_shards.start(stage + 1)
    lines[0].arrived(0)
    if count > 2:
        lines[0].start(1)

    def start_swap(s):
        for part in range(2):
            slice_swap(s, part).start()

    inputs.step(2)
    inputs.step(3)
    start_swap(0)
    start_swap(1)
    early(2).start()

    def norm_block(p, _):
        rows = rows_at(p, group)
        x = both[rows, :].astype(F32)
        factor = lax.rsqrt(jnp.mean(x * x, -1, keepdims=True) + EPS)
        second[rows, :] = (x * factor * gain_ref[0:1, :]).astype(BF)
        return 0

    lax.fori_loop(0, 4, norm_block, 0)
    for stage in range(1, count - 1):
        lines[0].arrived(stage)
        if stage < count - 2:
            lines[0].start(stage + 1)
    for p in range(4):
        inputs.arrived(p)
    lax.fori_loop(4, 8, norm_block, 0)
    for s in range(SLICES):
        for part in range(2):
            slice_keep(s, part).wait()
    output_line.start(0)
    grads = Gather(place, grad, group, gather_send.at[2], gather_recv.at[2])
    own_loads[1].wait()
    grads.start()
    start_swap(2)
    normed_copy = local(second, normed_out, out_sem.at[0])
    wide_copy = local(wide, w_attention, out_sem.at[1])
    normed_copy.start()
    mixed = PlaneSum(place, both, two, got, sum_send.at[0], sum_recv.at[0], chunk)

    def attention_forward(heads, table, aux):
        place.locate()
        table_keep.wait()
        early(2).wait_recv()
        table_load = local(table_out, table, load_sem.at[4])
        table_load.start()
        aux[...] = jnp.zeros_like(aux)
        early(1).wait_recv()
        tile = (HEAD_SIZE, HEAD_SIZE)
        diagonal = lax.broadcasted_iota(jnp.int32, tile, 0) == lax.broadcasted_iota(jnp.int32, tile, 1)
        for at in range(0, tokens, HEAD_SIZE):
            aux[at : at + HEAD_SIZE, 0:1] = jnp.sum(
                jnp.where(diagonal, marks_ref[0:1, at : at + HEAD_SIZE], 0.0), -1, keepdims=True
            )
        table_load.wait()

        def project_block(p, _):
            out = jnp.dot(second[rows_at(p, group), :], wide[:, :qkv_cols], preferred_element_type=F32)
            to = rows_at(group_at(place, p), group)
            cosine, sine = rotation(table[to, :])
            for at in range(0, q_cols + k_cols, HEAD_SIZE):
                heads[to, at : at + HEAD_SIZE] = turn(out[:, at : at + HEAD_SIZE], cosine, sine).astype(BF)
            heads[to, q_cols + k_cols : qkv_cols] = out[:, q_cols + k_cols :].astype(BF)
            return 0

        lax.fori_loop(0, 8, project_block, 0)
        output_steps(0, 1)
        advance(1)
        grads.step(1)

        def between(at):
            if at == 2:
                output_steps(1, 2)
            if at == 3:
                advance(1)
            if at == 5:
                output_steps(2, count)
            if at == 6:
                advance(1)

        attend_blocks(place, heads, q_cols, k_cols, aux, marks_ref, between)
        wide_copy.start()
        heads_copy = local(heads, heads_out, out_sem.at[2])
        aux_copy = local(aux, aux_out, out_sem.at[3])
        heads_copy.start()
        aux_copy.start()
        inputs.sent()
        normed_copy.wait()

        for c in range(8):
            columns = pl.ds(c * chunk, chunk)

            def mixed_part(rows, c=c):
                return lax.dot_general(
                    heads[rows, qkv_cols:], wide[c * chunk : (c + 1) * chunk, qkv_cols:], NT,
                    preferred_element_type=F32,
                )

            def mixed_rows(b, _, columns=columns, mixed_part=mixed_part):
                rows = rows_at(b, block)
                both[rows, columns] = mixed_part(rows).astype(BF)
                return 0

            first = mixed_part(pl.ds(0, block))
            two[:, columns] = first[:group]
            both[pl.ds(group, group), columns] = first[group:].astype(BF)
            lax.fori_loop(1, 4, mixed_rows, 0)
            mixed.push(c)
            if c >= 1:
                mixed.middle(c - 1)
            if c >= 3:
                mixed.late(c - 3)
            if c >= 5:
                mixed.total(c - 5)
            if c == 2:
                advance(1)
            if c == 3:
                grads.step(2)
            if c == 4:
                grads.step(3)
            if c == 5:
                advance(1)
        heads_copy.wait()
        aux_copy.wait()

    pl.run_scoped(
        attention_forward,
        pltpu.VMEM((tokens, packed), BF), pltpu.VMEM((tokens, HEAD_SIZE), F32), pltpu.VMEM((tokens, HEAD_SIZE), F32),
    )
    place.locate()
    mixed.middle(7)
    mixed.late(5)
    advance(1)
    mixed.total(3)
    for c in (6, 7):
        mixed.late(c)
        mixed.total(c - 2)
    mixed.total(6)
    mixed.total(7)
    early(0).wait_send()

    def by_rows(step):
        def some(b, _):
            step(rows_at(b, group // 4))
            return 0

        lax.fori_loop(0, 4, some, 0)

    def residual_step(rows):
        residual = two[rows, :] + both[rows, :].astype(F32)
        two[rows, :] = residual
        factor = lax.rsqrt(jnp.mean(residual * residual, -1, keepdims=True) + EPS)
        normal = (residual * factor * gain_ref[1:2, :]).astype(BF)
        own_rows[rows, :] = normal
        second[rows, :] = normal

    by_rows(residual_step)
    seconds = Gather(place, second, group, gather_send.at[1], gather_recv.at[1], own_rows)
    seconds.start()
    start_swap(3)
    advance(1)
    seconds.step(1)
    advance(1)
    wide_copy.wait()
    for stage in range(count - 1):
        lines[0].sent(stage)
        output_line.sent(stage)
    for c in range(8):
        mixed.sent(c)
    for s in range(SLICES):
        for part in range(2):
            if s < SLICES - 1:
                slice_swap(s, part).wait_send()
    seconds.step(2)
    seconds.step(3)
    for part in range(2):
        slice_swap(SLICES - 1, part).wait_send()
    for p in range(4):
        grads.arrived(p)
    advance(1)
    for p in range(4):
        seconds.arrived(p)
    seconds.sent()
    grads.sent()

    sums = []
    sum_items = [(s, 0, packed) for s in range(SLICES)]
    sum_items += [(SLICES, qkv_cols, q_cols), (SLICES, 0, qkv_cols)]
    for index, (item, low, size) in enumerate(sum_items):
        sums.append(
            LineSum(
                place, item, (low, size), index, own_grads, line_got, loads, ring, line_send, line_recv, line_load_sem,
                sums[-1] if sums else None,
            )
        )

    pending = {0: [], 1: []}
    turn_at = [0]

    def next_ready():
        slot = turn_at[0] % 2
        turn_at[0] += 1
        for wait in pending[slot]:
            wait()
        pending[slot] = []
        return slot

    def flush():
        for slot in (0, 1):
            for wait in pending[slot]:
                wait()
            pending[slot] = []

    def finish(index):
        item, low, size = sum_items[index]
        slot = next_ready()
        rows = pl.ds(low, size)
        sums[index].total(ready.at[slot, rows, pl.ds(0, shard2)])

        def copy():
            return pltpu.make_async_copy(
                ready.at[slot, rows, pl.ds(0, shard2)], totals.at[item, rows], ready_sem.at[slot]
            )

        copy().start()
        pending[slot].append(lambda: copy().wait())

    def owner_moves(index):
        item, low, size = sum_items[index]
        rows = pl.ds(low, size)
        if part_width == shard2:
            mine = theirs = totals.at[item, rows]
        else:
            mine, theirs = [
                totals.at[item, rows, pl.ds(pl.multiple_of(side * part_width, part_width), part_width)]
                for side in (place.half, 1 - place.half)
            ]
        target = shares.at[place.half, item, rows]
        keep = pltpu.make_async_copy(mine, target, owner_sem.at[index])
        return keep, place.copy(theirs, target, swap_send.at[index], swap_recv.at[index], "x")

    def to_owner(index):
        flush()
        for copy in owner_moves(index):
            copy.start()

    def stages_of(kind):
        return list(range(2, min(3, count)) if kind == "first" else range(3, count))

    def prepare(item, kind):
        if kind == "total":
            sums[item].prepare_total()
        elif stages_of(kind):
            sums[item].prepare(stages_of(kind)[0])

    def complete(item, kind):
        if kind == "total":
            finish(item)
            return
        for index, stage in enumerate(stages_of(kind)):
            if index:
                sums[item].prepare(stage)
            sums[item].service(stage)

    def weight_grads(item, low, high, right, tasks=()):
        for c in range(4):
            for at, do, task in tasks:
                if at == c:
                    do(*task)
            slot = next_ready()
            columns = pl.ds(c * big, big)
            for first, last, matrix in zip(low, high, right):
                ready[slot, first:last, :] = jnp.dot(
                    turned[first:last, :], matrix[:, columns], preferred_element_type=F32
                ).astype(BF)
            rows = pl.ds(low[0], high[-1] - low[0])
            copy = pltpu.make_async_copy(ready.at[slot, rows], own_grads.at[item, rows, columns], ready_sem.at[slot])
            copy.start()
            pending[slot].append(copy.wait)

    plane = PlaneSum(place, grad, one, got, sum_send.at[1], sum_recv.at[1], chunk)

    def give_credit(index):
        for name in ("core", "first", "second"):
            pl.semaphore_signal(free_sem.at[index], inc=1, device_id=place.partner[name], device_id_type=MESH)

    def second_step(rows):
        residual, grad_second = two[rows, :], one[rows, :]
        factor = lax.rsqrt(jnp.mean(residual * residual, -1, keepdims=True) + EPS)
        normal = residual * factor
        small_own[1:2, :] += jnp.sum(grad_second * normal, 0, keepdims=True)
        scaled = grad_second * gain_ref[1:2, :]
        residual_grad = grad[rows, :].astype(F32) + factor * (
            scaled - normal * jnp.mean(scaled * normal, -1, keepdims=True)
        )
        one[rows, :] = residual_grad
        own_rows[rows, :] = residual_grad.astype(BF)
        both[rows, :] = residual_grad.astype(BF)

    branch = Gather(place, both, group, gather_send.at[3], gather_recv.at[3], own_rows)

    def feed_forward(hidden):
        place.locate()
        for s in range(SLICES):
            advance_through(s)
            lines[1 + s].arrived(count - 2)
            load_wide(w_forward.at[s], s).start()
            load_wide(w_forward.at[s], s).wait()

            def rows_step(b, _, s=s):
                rows = rows_at(b, block)
                gate_up = jnp.dot(second[rows, :], wide[:, :pair], preferred_element_type=F32)
                grad_hidden = jnp.dot(grad[rows, :], wide[:, pair:], preferred_element_type=F32)
                gate, up = gate_up[:, :slice_cols], gate_up[:, slice_cols:]
                sigmoid = 1.0 / (1.0 + jnp.exp(-gate))
                activated = gate * sigmoid
                hidden_rows = (activated * up).astype(BF)
                gate_rows = (grad_hidden * up * (sigmoid + activated * (1.0 - sigmoid))).astype(BF)
                up_rows = (grad_hidden * activated).astype(BF)
                hidden[rows, s * slice_cols : (s + 1) * slice_cols] = hidden_rows
                both[rows, s * pair : s * pair + slice_cols] = gate_rows
                both[rows, s * pair + slice_cols : (s + 1) * pair] = up_rows
                turned[:slice_cols, rows] = gate_rows.T
                turned[slice_cols:pair, rows] = up_rows.T
                turned[pair:, rows] = hidden_rows.T
                return 0

            lax.fori_loop(0, 4, rows_step, 0)
            advance(1)
            weight_grads(
                s, (0, pair), (pair, packed), (second, grad),
                (
                    (),
                    ((2, prepare, (0, "first")), (3, complete, (0, "first"))),
                    ((2, prepare, (0, "later")), (3, complete, (0, "later"))),
                    (
                        (0, prepare, (0, "total")), (1, complete, (0, "total")),
                        (2, prepare, (1, "first")), (3, complete, (1, "first")), (3, to_owner, (0,)),
                    ),
                )[s],
            )
            flush()
            sums[s].start()
            advance(1)

        def chunk_loads(c, low):
            base = (c % 2) * SLICES
            return [
                pltpu.make_async_copy(
                    w_forward.at[s, pl.ds(c * chunk, chunk), pl.ds(low, packed - low)],
                    wide.at[pl.ds((base + s) * chunk, chunk), pl.ds(low, packed - low)],
                    wide_sem.at[SLICES + base + s],
                )
                for s in range(SLICES)
            ]

        def summed(source, rows, step, low, high, base):
            return sum(
                lax.dot_general(
                    source[rows, s * step : (s + 1) * step],
                    wide[(base + s) * chunk : (base + s + 1) * chunk, low:high], NT,
                    preferred_element_type=F32,
                )
                for s in range(SLICES)
            )

        for copy in chunk_loads(0, 0):
            copy.start()
        for c in range(8):
            if c < 7:
                for copy in chunk_loads(c + 1, 0):
                    copy.start()
            for copy in chunk_loads(c, 0):
                copy.wait()
            base = (c % 2) * SLICES
            columns = pl.ds(c * chunk, chunk)

            def grad_rows(b, _, columns=columns, base=base):
                rows = rows_at(b, block)
                grad[rows, columns] = summed(both, rows, pair, 0, pair, base).astype(BF)
                return 0

            first = summed(both, pl.ds(0, block), pair, 0, pair, base)
            one[:, columns] = first[:group]
            grad[pl.ds(group, group), columns] = first[group:].astype(BF)
            lax.fori_loop(1, 4, grad_rows, 0)
            plane.push(c)
            if c >= 1:
                plane.middle(c - 1)
            if c >= 2:
                plane.late(c - 2)
            if c >= 3:
                plane.total(c - 3)
            if c == 3:
                prepare(1, "later")
            if c == 4:
                complete(1, "later")
        for copy in chunk_loads(0, pair):
            copy.start()
        plane.middle(7)
        plane.late(6)
        plane.late(7)
        prepare(1, "total")
        for c in (5, 6, 7):
            plane.total(c)
        give_credit(0)
        complete(1, "total")
        small_own[...] = jnp.zeros_like(small_own)
        by_rows(second_step)
        branch.start()
        prepare(2, "first")
        for c in range(8):
            if c < 7:
                for copy in chunk_loads(c + 1, pair):
                    copy.start()
            for copy in chunk_loads(c, pair):
                copy.wait()

            def branch_rows(b, _, c=c):
                rows = rows_at(b, block)
                second[rows, pl.ds(c * chunk, chunk)] = summed(
                    hidden, rows, slice_cols, pair, packed, (c % 2) * SLICES
                ).astype(BF)
                return 0

            lax.fori_loop(0, 4, branch_rows, 0)
            if c == 0:
                complete(2, "first")
            if c == 5:
                branch.step(1)

    pl.run_scoped(feed_forward, pltpu.VMEM((tokens, SLICES * slice_cols), BF))
    place.locate()
    w_load = load_wide(w_attention, 0)
    w_load.start()

    outer = PlaneSum(place, second, two, got, sum_send.at[2], sum_recv.at[2], width)

    def rows_add(target, first_row, rows, sources):
        def step(b, _):
            at = rows_at(b, group)
            to = pl.ds(pl.multiple_of(first_row + b * group, group), group)
            value = target[to, :].astype(F32)
            for source in sources:
                value = value + source[to, :].astype(F32)
            target[to, :] = value.astype(BF)
            return 0

        lax.fori_loop(0, rows // group, step, 0)

    pl.semaphore_wait(free_sem.at[0], 3)
    outer.push(0)
    for c in range(8):
        plane.sent(c)
    marks = [0, q_cols, q_cols + k_cols, qkv_cols, qkv_cols + q_cols, qkv_cols + 2 * q_cols]
    arrays = [local(heads_out, grad.at[:, pl.ds(0, packed)], load_sem.at[5])]
    for copy in arrays:
        copy.start()
    q_ref, k_ref = grad.at[:, pl.ds(0, q_cols)], grad.at[:, pl.ds(marks[1], k_cols)]
    v_ref, attended = grad.at[:, pl.ds(marks[2], k_cols)], grad.at[:, pl.ds(marks[3], q_cols)]
    attended_grad, qkv_grad = grad.at[:, pl.ds(marks[4], q_cols)], grad.at[:, pl.ds(marks[5], qkv_cols)]
    prepare(2, "later")
    w_load.wait()

    def attended_step(p, _):
        rows = rows_at(p, group)
        attended_grad[rows, :] = jnp.dot(
            both[rows, :], wide[:, qkv_cols:], preferred_element_type=F32
        ).astype(BF)
        return 0

    for copy in arrays:
        copy.wait()
    lax.fori_loop(0, 2, attended_step, 0)
    branch.step(2)
    branch.step(3)
    outer.move(0, 0).wait_recv()
    rows_add(second, 2 * group, 2 * group, (got_core,))
    outer.move(1, 0).start()
    lax.fori_loop(2, 4, attended_step, 0)
    complete(2, "later")
    for p in range(4):
        branch.arrived(p)
    lax.fori_loop(4, 8, attended_step, 0)

    def outer_late():
        outer.move(1, 0).wait_recv()
        rows_add(second, group, group, (got_core, got_first))
        outer.move(2, 0).start()
        prepare(2, "total")

    def attention(table, aux, key_sum, value_sum):
        place.locate()
        table_load = pltpu.make_async_copy(table_out, table, load_sem.at[9])
        aux_load = pltpu.make_async_copy(aux_out, aux, load_sem.at[10])
        table_load.start()
        aux_load.start()
        table_load.wait()
        aux_load.wait()
        attend_back_blocks(
            place, q_ref, k_ref, v_ref, aux, marks_ref, attended_grad, table, qkv_grad, key_sum, value_sum,
            outer_late,
        )

    pl.run_scoped(
        attention,
        pltpu.VMEM((tokens, HEAD_SIZE), F32), pltpu.VMEM((tokens, HEAD_SIZE), F32),
        pltpu.VMEM((tokens, k_cols), F32), pltpu.VMEM((tokens, k_cols), F32),
    )
    place.locate()
    branch.sent()
    to_owner(1)
    complete(2, "total")
    to_owner(2)
    prepare(3, "first")

    def turn_rows(source, first, last):
        def step(b, _):
            rows = rows_at(b, group)
            turned[first:last, rows] = source[rows, :].T
            return 0

        lax.fori_loop(0, 8, step, 0)

    turn_rows(attended, qkv_cols, packed)
    weight_grads(SLICES, (qkv_cols,), (packed,), (both,))
    flush()
    sums[SLICES].start()
    normed_load = pltpu.make_async_copy(normed_out, both, load_sem.at[2])
    normed_load.start()
    complete(3, "first")
    turn_rows(qkv_grad, 0, qkv_cols)
    normed_load.wait()
    weight_grads(SLICES, (0,), (qkv_cols,), (both,))
    flush()
    sums[SLICES + 1].start()
    outer.move(2, 0).wait_recv()

    def output_step(rows):
        own_rows[rows, :] = (
            two[rows, :]
            + second[rows, :].astype(F32)
            + got_core[rows, :].astype(F32)
            + got_first[rows, :].astype(F32)
            + got_second[rows, :].astype(F32)
        ).astype(BF)

    by_rows(output_step)
    give_credit(1)
    blocks = HalfGather(place, own_rows, block_output, half_send.at[0], half_recv.at[0], load_sem.at[3])
    blocks.start()
    prepare(3, "later")

    outer.sent(0)
    pl.semaphore_wait(free_sem.at[1], 3)
    inner = PlaneSum(place, second, two, got, sum_send.at[3], sum_recv.at[3], chunk)
    for c in range(8):
        columns = pl.ds(c * chunk, chunk)

        def first_part(rows, c=c):
            return lax.dot_general(
                qkv_grad[rows, :], wide[c * chunk : (c + 1) * chunk, :qkv_cols], NT, preferred_element_type=F32
            )

        def first_rows(b, _, columns=columns, first_part=first_part):
            rows = rows_at(b, block)
            second[rows, columns] = first_part(rows).astype(BF)
            return 0

        first = first_part(pl.ds(0, block))
        two[:, columns] = first[:group]
        second[pl.ds(group, group), columns] = first[group:].astype(BF)
        lax.fori_loop(1, 4, first_rows, 0)
        inner.push(c)
        if c == 0:
            complete(3, "later")
        if c == 1:
            prepare(SLICES, "first")
        if c == 2:
            complete(SLICES, "first")
        if c == 4:
            prepare(SLICES + 1, "first")
        if c == 5:
            complete(SLICES + 1, "first")
        if c == 6:
            prepare(SLICES, "later")
        if c == 7:
            complete(SLICES, "later")
        if c >= 1:
            inner.middle(c - 1)
        if c >= 3:
            inner.late(c - 3)
        if c >= 5:
            inner.total(c - 5)
    inner.middle(7)
    prepare(SLICES + 1, "later")
    blocks.step()
    inner.late(5)
    complete(SLICES + 1, "later")
    inner.total(3)
    for c in (6, 7):
        inner.late(c)
        inner.total(c - 2)
    prepare(3, "total")
    inner.total(6)
    inner.total(7)
    complete(3, "total")
    to_owner(3)
    input_load = pltpu.make_async_copy(
        block_input.at[rows_at(place.tensor, group)], second.at[pl.ds(0, group)], load_sem.at[4]
    )
    input_load.start()
    input_load.wait()

    def first_step(rows):
        value, grad_first = second[rows, :].astype(F32), two[rows, :]
        factor = lax.rsqrt(jnp.mean(value * value, -1, keepdims=True) + EPS)
        normal = value * factor
        small_own[0:1, :] += jnp.sum(grad_first * normal, 0, keepdims=True)
        scaled = grad_first * gain_ref[0:1, :]
        input_grad = one[rows, :] + factor * (scaled - normal * jnp.mean(scaled * normal, -1, keepdims=True))
        second[rows, :] = input_grad.astype(BF)

    by_rows(first_step)
    gradients = HalfGather(
        place, second.at[pl.ds(0, group)], input_gradient, half_send.at[1], half_recv.at[1], load_sem.at[4]
    )
    gradients.start()

    def small_move(index):
        return place.copy(
            small_own.at[pl.ds(8 * index, 8)], small_got.at[index], small_send.at[index], small_recv.at[index],
            ("core", "y", "x")[index],
        )

    def small_sum(index):
        small_move(index).wait_recv()
        value = small_own[8 * index : 8 * index + 8, :] + small_got[index]
        if index < 2:
            small_own[8 * index + 8 : 8 * index + 16, :] = value
            small_move(index + 1).start()
        else:
            small_all[place.sequence] = value

    small_move(0).start()
    prepare(SLICES, "total")
    small_sum(0)
    complete(SLICES, "total")
    to_owner(SLICES)
    small_sum(1)
    prepare(SLICES + 1, "total")
    small_sum(2)
    gain_line = Line(place, lambda k: small_all.at[k], gain_send, gain_recv)
    gain_line.start(0)
    complete(SLICES + 1, "total")
    to_owner(SLICES + 1)
    gradients.step()
    for stage in range(count - 1):
        gain_line.arrived(stage)
        if stage < count - 2:
            gain_line.start(stage + 1)
    own_columns = pl.ds(pl.multiple_of(place.sequence * shard2, shard2), shard2)
    gain_out[...] = sum(small_all[k, :, own_columns] for k in range(count))

    flush()
    for line in lines[1:]:
        for stage in range(count - 1):
            line.sent(stage)
    if gains_here:
        for stage in range(count - 1):
            gain_shards.sent(stage)
    for index in (1, 2, 3) if gains_here else (1, 2):
        early(index).wait_send()
    for item, item_sum in enumerate(sums):
        item_sum.sent(item == SLICES + 1)
    for index in range(len(sum_items)):
        keep, swap = owner_moves(index)
        keep.wait()
        swap.wait()
    for c in range(8):
        inner.sent(c)
    for index in range(3):
        small_move(index).wait_send()
    for stage in range(count - 1):
        gain_line.sent(stage)
    blocks.end()
    gradients.end()


def rotation(table):
    other = pltpu.roll(table, HEAD_SIZE // 2, 1)
    low = lax.broadcasted_iota(jnp.int32, table.shape, 1) < HEAD_SIZE // 2
    return jnp.where(low, table, other), jnp.where(low, -other, table)


def attend_back_blocks(
    place, q_ref, k_ref, v_ref, aux, columns_ref, grad_ref, table, out_ref, key_sum, value_sum, late
):
    block = q_ref.shape[0] // 8
    scale = 1.0 / math.sqrt(HEAD_SIZE)
    q_cols, k_cols = q_ref.shape[1], k_ref.shape[1]
    key_sum[...] = jnp.zeros_like(key_sum)
    value_sum[...] = jnp.zeros_like(value_sum)
    for at in range(8):
        low, high = key_range(at, block)
        here = slice(at * block, high)
        span = slice(low, high)
        allowed = allowed_pairs(aux, columns_ref, at, block)
        keys, values = k_ref[span, :], v_ref[span, :]
        cosine, sine = rotation(table[here, :])
        to = rows_at(place.of_group(at), block)
        for head in range(q_cols // HEAD_SIZE):
            columns = slice(head * HEAD_SIZE, (head + 1) * HEAD_SIZE)
            rows = q_ref[here, columns]
            grad_rows = grad_ref[to, columns]
            scores = lax.dot_general(rows, keys, NT, preferred_element_type=F32) * scale
            scores = jnp.where(allowed, scores, NEGATIVE)
            probs = jnp.exp(scores - aux[here, 1 + head : 2 + head])
            value_sum[span, :] += lax.dot_general(
                probs.astype(BF), grad_rows, TN, preferred_element_type=F32
            )
            prob_grad = lax.dot_general(grad_rows, values, NT, preferred_element_type=F32)
            inner = jnp.sum(probs * prob_grad, -1, keepdims=True)
            score_grad = (probs * (prob_grad - inner)).astype(BF)
            query_grad = jnp.dot(score_grad, keys, preferred_element_type=F32) * scale
            key_sum[span, :] += lax.dot_general(score_grad, rows, TN, preferred_element_type=F32)
            out_ref[to, columns] = turn(query_grad, cosine, -sine).astype(BF)
        if at == 5:
            late()
    for at in range(8):
        here = slice(at * block, (at + 1) * block)
        cosine, sine = rotation(table[here, :])
        to = rows_at(place.of_group(at), block)
        out_ref[to, q_cols : q_cols + k_cols] = turn(key_sum[here, :] * scale, cosine, -sine).astype(BF)
        out_ref[to, q_cols + k_cols :] = value_sum[here, :].astype(BF)


def layer(block_input, out_grad, gains, table, marks, masters, count):
    half_tokens, width = block_input.shape
    group, tokens = half_tokens // 4, 2 * half_tokens
    shard = masters[0].shape[0]
    q_cols, k_cols = masters[0].shape[1] // 2, masters[1].shape[1] // 2
    slice_cols = masters[4].shape[1] // 2 // SLICES
    packed = 3 * slice_cols
    assert packed == 2 * q_cols + 2 * k_cols and q_cols == group >= shard
    gains_here = shard % 128 == 0
    if not gains_here:
        gains = lax.all_gather(gains, "dp", axis=1, tiled=True)
    part = shard if gains_here else 2 * shard
    vmem, hbm = pl.BlockSpec(memory_space=pltpu.VMEM), pl.BlockSpec(memory_space=pl.ANY)
    struct = jax.ShapeDtypeStruct
    dma = pltpu.SemaphoreType.DMA
    items = 1 + SLICES
    return pl.pallas_call(
        functools.partial(layer_kernel, count, gains_here),
        in_specs=[hbm, hbm, vmem, hbm, vmem] + [hbm] * 7,
        out_specs=[hbm] * 3 + [vmem] + [hbm] * 9,
        out_shape=[
            struct((half_tokens, width), BF),
            struct((half_tokens, width), BF),
            struct((2, items, packed, part), BF),
            struct((8, 2 * shard), F32),
            struct((items, packed, width), BF),
            struct((items, 2, count - 1, packed, 2 * shard), BF),
            struct((items, packed, 2 * shard), BF),
            struct((width, packed), BF),
            struct((SLICES, width, packed), BF),
            struct((tokens, width), BF),
            struct((tokens, packed), BF),
            struct((tokens, HEAD_SIZE), F32),
            struct((tokens, HEAD_SIZE), F32),
        ],
        scratch_shapes=[
            pltpu.VMEM((tokens, width), BF),
            pltpu.VMEM((tokens, width), BF),
            pltpu.VMEM((tokens, width), BF),
            pltpu.VMEM((width, packed), BF),
            pltpu.VMEM((4 * group, width), BF),
            pltpu.VMEM((2 * group, width), BF),
            pltpu.VMEM((group, width), BF),
            pltpu.VMEM((4, packed, 2 * shard), BF),
            pltpu.VMEM((count - 1, packed, 2 * shard), BF),
            pltpu.VMEM((2, packed, width // 4), BF),
            pltpu.VMEM((packed, tokens), BF),
            pltpu.VMEM((group, width), F32),
            pltpu.VMEM((group, width), F32),
            pltpu.VMEM((group, width), BF),
            pltpu.VMEM((24, width), F32),
            pltpu.VMEM((3, 8, width), F32),
            pltpu.VMEM((count, 8, width), F32),
            pltpu.VMEM((8, width), F32),
            pltpu.VMEM((8, tokens), F32),
            dma((12,)),
            dma((3 * SLICES,)),
            dma((2,)),
            dma((1 + items,)),
            dma((1 + items,)),
            dma((1 + items, 2, count - 1)),
            dma((1 + items, 2, count - 1)),
            dma((4, 3, 8)),
            dma((4, 3, 8)),
            dma((4, 7)),
            dma((4, 7)),
            dma((2, 3)),
            dma((2, 3)),
            dma((3,)),
            dma((3,)),
            dma((2, count - 1)),
            dma((2, count - 1)),
            pltpu.SemaphoreType.REGULAR((2,)),
            dma((4,)),
            dma((1 + items,)),
            dma((4,)),
            dma((4,)),
            dma((SLICES, 2)),
            dma((SLICES, 2)),
            dma((2 + items, 2, count - 1)),
            dma((2 + items, 2, count - 1)),
            dma((5,)),
            dma((SLICES, 2)),
            dma((4,)),
        ],
        compiler_params=pltpu.CompilerParams(
            vmem_limit_bytes=VMEM_LIMIT, collective_id=0, has_side_effects=True
        ),
        name="layer",
    )(block_input, out_grad, gains, table, marks, *masters)


def adamw(weight, gradient, first, second, rate, decay):
    first_new = BETA_ONE * first + (1.0 - BETA_ONE) * gradient
    second_new = BETA_TWO * second + (1.0 - BETA_TWO) * gradient * gradient
    bias_first = 1.0 - BETA_ONE**STEP
    bias_second = 1.0 - BETA_TWO**STEP
    moved = first_new * (1.0 / bias_first) / (jnp.sqrt(second_new * (1.0 / bias_second)) + ADAM_EPS)
    return (weight - rate * (moved + decay * weight), first_new, second_new)


def update_kernel(attention_cuts, forward_cuts, *refs):
    a, f = 12, 9
    attention_share, forward_share, block_in, gradient_in = refs[:4]
    states, outs = refs[4 : 4 + a + f], refs[4 + a + f :]
    outs[0][...] = block_in[...]
    outs[1][...] = gradient_in[...].astype(F32)

    def one(gradient, arrays, results, at):
        fresh = adamw(arrays[0][at], gradient, arrays[1][at], arrays[2][at], RATE_MATRIX, DECAY)
        for result, value in zip(results, fresh):
            result[at] = value

    everything = (slice(None), slice(None))
    for i in range(3):
        gradient = forward_share[forward_cuts[i] : forward_cuts[i + 1], :].astype(F32)
        one(gradient if i == 2 else gradient.T, states[a + i :: 3][:3], outs[2 + a + i :: 3][:3], everything)

    @pl.when(pl.program_id(0) == 0)
    def _():
        for i in range(4):
            for side in range(2):
                low, high = attention_cuts[i], attention_cuts[i + 1]
                gradient = attention_share[side, low:high, :].astype(F32)
                span = slice(side * (high - low), (side + 1) * (high - low))
                if i == 3:
                    one(gradient, states[i:a:4], outs[2 + i : 2 + a : 4], (span, slice(None)))
                else:
                    one(gradient.T, states[i:a:4], outs[2 + i : 2 + a : 4], (slice(None), span))


def update(shares, block_output, input_gradient, attention_cuts, attention, forward_cuts, feed):
    packed, part = shares.shape[2:]
    steps = 2 * SLICES

    def rows_block(array):
        return pl.BlockSpec((array.shape[0] // steps, array.shape[1]), lambda g: (g, 0))

    def columns_block(array):
        return pl.BlockSpec((array.shape[0], array.shape[1] // steps), lambda g: (0, g))

    state_specs = [pl.BlockSpec(array.shape, lambda g: (0, 0)) for array in attention]
    state_specs += [rows_block(array) if i % 3 == 2 else columns_block(array) for i, array in enumerate(feed)]
    plain = [rows_block(block_output), rows_block(input_gradient)]
    return pl.pallas_call(
        functools.partial(update_kernel, attention_cuts, forward_cuts),
        grid=(steps,),
        in_specs=[
            pl.BlockSpec((2, None, packed, part), lambda g: (0, SLICES, 0, 0)),
            pl.BlockSpec((None, None, packed, part), lambda g: (g // SLICES, g % SLICES, 0, 0)),
        ]
        + plain
        + state_specs,
        out_specs=plain + state_specs,
        out_shape=[
            jax.ShapeDtypeStruct(block_output.shape, BF),
            jax.ShapeDtypeStruct(input_gradient.shape, F32),
        ]
        + [jax.ShapeDtypeStruct(array.shape, F32) for array in (*attention, *feed)],
        compiler_params=pltpu.CompilerParams(vmem_limit_bytes=VMEM_LIMIT),
        name="update",
    )(shares, shares, block_output, input_gradient, *attention, *feed)


def rotary_tables(positions):
    half = HEAD_SIZE // 2
    frequency = THETA ** (-2.0 * jnp.arange(half, dtype=F32) / HEAD_SIZE)
    angles = positions.astype(F32)[:, None] * frequency[None, :]
    cosine, sine = jnp.cos(angles), jnp.sin(angles)
    return jnp.concatenate([cosine, sine], -1)


def local(
    block_input, out_grad, segments, positions,
    w_query, w_key, w_value, w_output, w_gate, w_up, w_down, gains,
    m_query, m_key, m_value, m_output, m_gate, m_up, m_down, m_gains,
    v_query, v_key, v_value, v_output, v_gate, v_up, v_down, v_gains,
):
    half_tokens = block_input.shape[0]
    rows = w_query.shape[0]
    sequences = lax.axis_size("dp") // 2
    half = lax.axis_index("dp") % 2
    table = rotary_tables(positions)
    marks = jnp.broadcast_to(segments.astype(F32)[None, :], (8, half_tokens))
    gain_rows = jnp.pad(gains.astype(BF).astype(F32), ((0, 6), (0, 0)))
    masters = (w_query, w_key, w_value, w_output, w_gate, w_up, w_down)
    block_output, input_gradient, shares, gain_grads = layer(
        block_input, out_grad, gain_rows, table, marks, masters, sequences
    )[:4]
    if shares.shape[-1] != rows:
        shares = lax.dynamic_slice_in_dim(shares, half * rows, rows, 3)
    q_cols, k_cols, o_cols = w_query.shape[1] // 2, w_key.shape[1] // 2, w_output.shape[0] // 2
    slice_cols = w_gate.shape[1] // 2 // SLICES

    def cuts(*sizes):
        return [sum(sizes[:i]) for i in range(len(sizes) + 1)]

    block_output, input_gradient, *fresh = update(
        shares, block_output, input_gradient,
        cuts(q_cols, k_cols, k_cols, o_cols),
        (w_query, w_key, w_value, w_output, m_query, m_key, m_value, m_output, v_query, v_key, v_value, v_output),
        cuts(slice_cols, slice_cols, slice_cols),
        (w_gate, w_up, w_down, m_gate, m_up, m_down, v_gate, v_up, v_down),
    )
    attention_new, forward_new = fresh[:12], fresh[12:]
    gain_grads = lax.dynamic_slice_in_dim(gain_grads[:2], half * rows, rows, 1)
    gains_new = adamw(gains, gain_grads, m_gains, v_gains, RATE_GAIN, 0.0)
    new = [
        list(attention_new[4 * part : 4 * part + 4]) + list(forward_new[3 * part : 3 * part + 3]) + [gains_new[part]]
        for part in range(3)
    ]
    return tuple([block_output, input_gradient] + new[0] + new[1] + new[2])


def solution(mesh):
    matrices = [P("dp", "tensor")] * 3 + [P("tensor", "dp")] + [P("dp", "tensor")] * 2 + [P("tensor", "dp")]
    state = tuple(matrices + [P(None, "dp")])
    rows = (P("dp", None), P("dp", None))
    return jax.shard_map(
        local,
        mesh=mesh,
        in_specs=rows + (P("dp"), P("dp")) + state * 3,
        out_specs=rows + state * 3,
        check_vma=False,
    )
```
